512 devices in a mesh: radial: 64 (over z_hi, x, y), axial: 8 (over z_lo, core).
Axes of the slice: x: 4, y: 8, z: 8 (z_hi: 2, z_lo: 4; z = z_hi * 4 + z_lo), core: 2. Of those that a mesh axis runs over, the one named last changes fastest.
Arguments:
- velocity: float32 [3, 32, 512, 512], P(None, 'axial', 'radial'), may hold values from -6 to 6
- previous_rhs: float32 [3, 32, 512, 512], P(None, 'axial', 'radial'), may hold values from -6 to 6
- radial_deriv: float32 [512, 512], replicated, may hold values from -0.25 to 0.25
- inv_radius: float32 [512], P('radial'), may hold values from 0.5 to 2
Outputs:
- velocity_new: float32 [3, 32, 512, 512], P(None, 'axial', 'radial')
- rhs_new: float32 [3, 32, 512, 512], P(None, 'axial', 'radial')
The draws below stay inside these ranges and needn't reach their ends.
All inputs are finite; a program needn't handle non-finite values.
Results may differ from the reference program's by a relative error of at most 0.00005.
Values sent between devices are 32-bit elements; how exact they have to be, the bound alone decides.
No kernel may reach another device: no remote copies, remote signals or barrier semaphores. Data moves between devices by JAX's collectives and lax.ppermute only.
A program may use at most 64 MiB of HBM per device.

```python
import math
import jax
import jax.numpy as jnp
from jax import lax

NR = 512
NT = 512
KEEP = 192
NZ = 32


def shard_levels(stream_key, extent, pieces, least, high):
    level = 1.0
    for dim, parts in pieces:
        heights = jax.random.uniform(jax.random.fold_in(jax.random.fold_in(stream_key, 6), dim), (parts,), jnp.float32, least / len(pieces), high / len(pieces))
        level = level * jnp.repeat(jnp.exp(heights), extent[dim] // parts).reshape((-1,) + (1,) * (len(extent) - 1 - dim))
    return level


def scatter_about(stream_key, shape, deviation, bound, cuts=(), held_as=jnp.bfloat16):
    result = jax.random.normal(stream_key, shape, jnp.float32) * deviation
    if len(cuts) > 0:
        result = shard_levels(stream_key, shape, cuts, -0.22, 0.18) * result
    return jnp.clip(result, min=-bound, max=bound).astype(held_as)


def setup_inputs(seed: int = 0) -> dict:
    key_list = jax.random.split(jax.random.key(seed), 5)
    velocity = scatter_about(key_list[0], (3, NZ, NR, NT), 1.0, 6.0, ((1, 8), (2, 64)), jnp.float32)
    previous_rhs = scatter_about(key_list[1], (3, NZ, NR, NT), 1.0, 6.0, ((1, 8), (2, 64)), jnp.float32)
    radial_deriv = scatter_about(key_list[2], (NR, NR), NR ** -0.5, 0.25, (), jnp.float32)
    inv_radius = jnp.clip(jnp.exp(math.log(2.0) - 1.3862944 * jax.random.uniform(key_list[3], (NR,), jnp.float32) ** shard_levels(key_list[3], (NR,), ((0, 64),), -0.2, 0.2)), 0.5, 2.0)
    return {"velocity": velocity, "previous_rhs": previous_rhs, "radial_deriv": radial_deriv, "inv_radius": inv_radius}


first_coefs = (4.0 / 5.0, -1.0 / 5.0, 4.0 / 105.0, -1.0 / 280.0)
second_coefs = (8.0 / 5.0, -1.0 / 5.0, 8.0 / 315.0, -1.0 / 560.0)
second_centre = -205.0 / 72.0
viscosity = 0.05
section_carry = -5.0 / 9.0
section_weight = 15.0 / 16.0
timestep = 0.1


def to_modes(field):
    spectrum = jnp.fft.rfft(field, axis=-1)[..., :KEEP]
    return jnp.concatenate([jnp.real(spectrum), jnp.imag(spectrum)], axis=-1)


def to_points(spectra):
    widths = [(0, 0)] * (spectra.ndim - 1) + [(0, NT // 2 + 1 - KEEP)]
    real_part = jnp.pad(spectra[..., :KEEP], widths)
    imag_part = jnp.pad(spectra[..., KEEP:], widths)
    return jnp.fft.irfft(real_part + 1j * imag_part, n=NT, axis=-1)


def reference(velocity, previous_rhs, radial_deriv, inv_radius):
    spectra = to_modes(velocity)
    padded = jnp.concatenate([spectra[:, -4:], spectra, spectra[:, :4]], axis=1)
    wavenumber = jnp.arange(KEEP).astype(velocity.dtype) * (2.0 * math.pi / NT)
    ratio_col = inv_radius[None, :, None]

    def plane(plane_index):
        plane_block = lax.dynamic_slice_in_dim(padded, plane_index, 9, 1)
        centre = plane_block[:, 4]
        axial_first = sum(first_coefs[offset] * (plane_block[:, 5 + offset] - plane_block[:, 3 - offset]) for offset in range(4))
        second = second_centre * centre + sum(second_coefs[offset] * (plane_block[:, 5 + offset] + plane_block[:, 3 - offset]) for offset in range(4))
        real_part = centre[..., :KEEP]
        imag_part = centre[..., KEEP:]
        theta_spec = jnp.concatenate([-wavenumber * imag_part, wavenumber * real_part], axis=-1)
        wave_square = jnp.concatenate([wavenumber * wavenumber, wavenumber * wavenumber])
        smooth = to_points(centre)
        theta_deriv = to_points(theta_spec) * ratio_col
        axial_deriv = to_points(axial_first)
        radial_first = jnp.einsum("ij,cjt->cit", radial_deriv, smooth, precision=lax.Precision.HIGHEST)
        radial_second = jnp.einsum("ij,cjt->cit", radial_deriv, radial_first, precision=lax.Precision.HIGHEST)
        laplace = radial_second + to_points(second) + ratio_col * ratio_col * to_points(-wave_square * centre)
        advection = smooth[0:1] * radial_first + smooth[1:2] * theta_deriv + smooth[2:3] * axial_deriv
        return viscosity * laplace - advection

    tendency = lax.map(plane, jnp.arange(velocity.shape[1], dtype=jnp.int32))
    tendency = jnp.transpose(tendency, (1, 0, 2, 3))
    rhs_new = section_carry * previous_rhs + tendency
    velocity_new = velocity + (section_weight * timestep) * rhs_new
    return velocity_new, rhs_new
```

```python
import functools
import math

import jax
import jax.numpy as jnp
import ml_dtypes
import numpy as np
from jax import lax
from jax.experimental import pallas as pl
from jax.experimental.pallas import tpu as pltpu
from jax.sharding import PartitionSpec as P

KEEP = 192
LANES = 128
GROUP = 32
GROUPS = LANES // GROUP

first_coefs = (4.0 / 5.0, -1.0 / 5.0, 4.0 / 105.0, -1.0 / 280.0)
second_coefs = (8.0 / 5.0, -1.0 / 5.0, 8.0 / 315.0, -1.0 / 560.0)
second_centre = -205.0 / 72.0
viscosity = 0.05
section_carry = -5.0 / 9.0
section_weight = 15.0 / 16.0
timestep = 0.1


def halves(array):
    high = array.astype(jnp.bfloat16)
    low = (array - high.astype(jnp.float32)).astype(jnp.bfloat16)
    return high, low


def host_halves(array):
    high = array.astype(ml_dtypes.bfloat16)
    low = (array - high.astype(np.float64)).astype(ml_dtypes.bfloat16)
    return high, low


def circulants(kept_modes, points):
    modes = np.arange(kept_modes)
    weights = np.where(modes == 0, 1.0, 2.0) / points
    slopes = modes * (2.0 * math.pi / points)
    angles = (modes[:, None] * np.arange(points)[None, :] % points) * (2.0 * math.pi / points)
    shift = (np.arange(points)[None, :] - np.arange(points)[:, None]) % points
    keep = (weights[:, None] * np.cos(angles)).sum(0)
    slope = -(weights[:, None] * slopes[:, None] * np.sin(angles)).sum(0)
    curve = -(weights[:, None] * slopes[:, None] ** 2 * np.cos(angles)).sum(0)
    return keep[shift], slope[shift], curve[shift]


def product(left, right):
    dot = functools.partial(jnp.dot, preferred_element_type=jnp.float32)
    return dot(left[0], right[0]) + (dot(left[0], right[1]) + dot(left[1], right[0]))


def lane_groups(shape):
    return lax.broadcasted_iota(jnp.int32, shape, len(shape) - 1) // GROUP


def filter_kernel(velocity_ref, high_ref, low_ref, smooth_ref, message_ref):
    components, planes, rows, points = velocity_ref.shape
    velocity = velocity_ref[...].reshape(components * planes * rows, points)
    smooth = product(halves(velocity), (high_ref[...], low_ref[...]))
    smooth = smooth.reshape(components, planes, rows, points)
    smooth_ref[...] = smooth
    blocks = points // LANES
    groups = lane_groups((planes, rows, LANES))
    for block in range(blocks):
        tile = smooth[:, :, :, block * LANES : (block + 1) * LANES]
        turned = [tile[0]] + [pltpu.roll(tile[c], c * GROUP, 2) for c in range(1, components)]
        for part in range(GROUPS):
            chosen = jnp.zeros_like(turned[0])
            for c in range(components):
                chosen = jnp.where(groups == (part + c) % GROUPS, turned[c], chosen)
            for plane in range(planes):
                message_ref[(plane * blocks + block) * GROUPS + part] = chosen[plane]


def theta_kernel(velocity_ref, high_ref, low_ref, slope_ref, curve_ref):
    components, planes, rows, points = velocity_ref.shape
    velocity = velocity_ref[...].reshape(components * planes * rows, points)
    both = product(halves(velocity), (high_ref[...], low_ref[...]))
    slope_ref[...] = both[:, :points].reshape(velocity_ref.shape)
    curve_ref[...] = both[:, points:].reshape(velocity_ref.shape)


def radial_kernel(part_ref, pencil_ref, matrix_ref, result_ref):
    part = part_ref[0]
    pencil = pencil_ref[...]
    matrix = halves(matrix_ref[...])
    once = product(matrix, halves(pencil))
    twice = product(matrix, halves(once))
    groups = lane_groups(pencil.shape)
    place = lax.rem(groups - part + GROUPS, GROUPS)
    speed = jnp.where(place == 0, pencil, jnp.zeros_like(pencil))
    speed = jnp.where(place == 1, pltpu.roll(pencil, GROUP, 1), speed)
    speed = jnp.where(place == 2, pltpu.roll(pencil, 2 * GROUP, 1), speed)
    result_ref[...] = viscosity * twice - speed * once


def local_kernel(
    smooth_ref, before_ref, after_ref, slope_ref, curve_ref, previous_ref, ratio_ref, result_ref
):
    components, planes, rows, points = smooth_ref.shape
    ratio = ratio_ref[...]
    square = ratio * ratio
    for plane in range(planes):
        speed_theta = smooth_ref[1, plane] * ratio
        speed_axial = smooth_ref[2, plane]
        for c in range(components):
            def at(index):
                if index < 0:
                    return before_ref[c, index + planes]
                if index >= planes:
                    return after_ref[c, index - planes]
                return smooth_ref[c, index]

            first = jnp.zeros_like(speed_axial)
            second = second_centre * smooth_ref[c, plane]
            for k in range(4):
                up, down = at(plane + k + 1), at(plane - k - 1)
                first = first + first_coefs[k] * (up - down)
                second = second + second_coefs[k] * (up + down)
            second = second + square * curve_ref[c, plane]
            result_ref[c, plane] = (
                section_carry * previous_ref[c, plane]
                + viscosity * second
                - speed_theta * slope_ref[c, plane]
                - speed_axial * first
            )


def final_kernel(radial_ref, local_ref, velocity_ref, velocity_out_ref, rhs_out_ref):
    components, planes, rows, points = velocity_ref.shape
    blocks = points // LANES
    groups = lane_groups((rows, LANES))
    for plane in range(planes):
        for block in range(blocks):
            tiles = [
                radial_ref[(plane * blocks + block) * GROUPS + part] for part in range(GROUPS)
            ]
            for c in range(components):
                chosen = tiles[0]
                for part in range(1, GROUPS):
                    chosen = jnp.where(groups == (part + c) % GROUPS, tiles[part], chosen)
                if c > 0:
                    chosen = pltpu.roll(chosen, LANES - c * GROUP, 1)
                lanes = slice(block * LANES, (block + 1) * LANES)
                rhs = local_ref[c, plane, :, lanes] + chosen
                rhs_out_ref[c, plane, :, lanes] = rhs
                velocity_out_ref[c, plane, :, lanes] = (
                    velocity_ref[c, plane, :, lanes] + (section_weight * timestep) * rhs
                )


VMEM = pl.BlockSpec(memory_space=pltpu.VMEM)
SMEM = pl.BlockSpec(memory_space=pltpu.SMEM)


def call(kernel, in_specs, shapes, name, flops, moved):
    out_shape = [jax.ShapeDtypeStruct(shape, jnp.float32) for shape in shapes]
    single = len(out_shape) == 1
    return pl.pallas_call(
        kernel,
        out_shape=out_shape[0] if single else out_shape,
        in_specs=in_specs,
        out_specs=VMEM if single else [VMEM] * len(out_shape),
        compiler_params=pltpu.CompilerParams(vmem_limit_bytes=24 * 1024 * 1024),
        cost_estimate=pl.CostEstimate(flops=flops, bytes_accessed=moved, transcendentals=0),
        name=name,
    )


def shards(velocity, previous_rhs, radial_deriv, inv_radius):
    components, planes, radial_rows, points = velocity.shape
    peers = lax.axis_size("radial")
    shape = velocity.shape
    size = velocity.size
    keep, slope, curve = circulants(KEEP, points)
    keep_high, keep_low = host_halves(keep)
    theta_high, theta_low = host_halves(np.concatenate([slope, curve], axis=1))

    smooth, message = call(
        filter_kernel,
        [VMEM] * 3,
        [shape, (peers, radial_rows, LANES)],
        "filter",
        6 * size * points,
        20 * size,
    )(velocity, jnp.asarray(keep_high), jnp.asarray(keep_low))
    pencil = lax.all_to_all(message, "radial", split_axis=0, concat_axis=0, tiled=True)

    ring = lax.axis_size("axial")
    up = [(i, (i + 1) % ring) for i in range(ring)]
    down = [(j, i) for i, j in up]
    before = lax.ppermute(smooth, "axial", up)
    after = lax.ppermute(smooth, "axial", down)
    theta_slope, theta_curve = call(
        theta_kernel, [VMEM] * 3, [shape, shape], "theta", 12 * size * points, 24 * size
    )(velocity, jnp.asarray(theta_high), jnp.asarray(theta_low))

    part = (lax.axis_index("radial") % GROUPS).astype(jnp.int32).reshape(1)
    full = peers * radial_rows
    result = call(
        radial_kernel,
        [SMEM, VMEM, VMEM],
        [(full, LANES)],
        "radial",
        12 * full * full * LANES,
        4 * full * (full + 2 * LANES),
    )(part, pencil.reshape(full, LANES), radial_deriv)
    radial = lax.all_to_all(
        result.reshape(peers, radial_rows, LANES), "radial", split_axis=0, concat_axis=0, tiled=True
    )
    ratio = jnp.broadcast_to(inv_radius[:, None], (radial_rows, points))
    local = call(local_kernel, [VMEM] * 7, [shape], "local", 40 * size, 32 * size)(
        smooth, before, after, theta_slope, theta_curve, previous_rhs, ratio
    )
    return call(final_kernel, [VMEM] * 3, [shape, shape], "final", 10 * size, 20 * size)(
        radial, local, velocity
    )


def solution(mesh):
    in_specs = (
        P(None, "axial", "radial", None),
        P(None, "axial", "radial", None),
        P(),
        P("radial"),
    )
    out_specs = (P(None, "axial", "radial", None), P(None, "axial", "radial", None))

    def whole(*args):
        return tuple(shards(*args))

    return jax.shard_map(whole, mesh=mesh, in_specs=in_specs, out_specs=out_specs, check_vma=False)
```

```python
import functools
import math

import jax
import jax.numpy as jnp
import ml_dtypes
import numpy as np
from jax import lax
from jax.experimental import pallas as pl
from jax.experimental.pallas import tpu as pltpu
from jax.sharding import PartitionSpec as P

KEEP = 192
LANES = 128
GROUP = 32
GROUPS = LANES // GROUP

first_coefs = (4.0 / 5.0, -1.0 / 5.0, 4.0 / 105.0, -1.0 / 280.0)
second_coefs = (8.0 / 5.0, -1.0 / 5.0, 8.0 / 315.0, -1.0 / 560.0)
second_centre = -205.0 / 72.0
viscosity = 0.05
section_carry = -5.0 / 9.0
section_weight = 15.0 / 16.0
timestep = 0.1


def halves(array):
    high = array.astype(jnp.bfloat16)
    low = (array - high.astype(jnp.float32)).astype(jnp.bfloat16)
    return high, low


def host_halves(array):
    high = array.astype(ml_dtypes.bfloat16)
    low = (array - high.astype(np.float64)).astype(ml_dtypes.bfloat16)
    return high, low


def circulants(kept_modes, points):
    modes = np.arange(kept_modes)
    weights = np.where(modes == 0, 1.0, 2.0) / points
    slopes = modes * (2.0 * math.pi / points)
    angles = (modes[:, None] * np.arange(points)[None, :] % points) * (2.0 * math.pi / points)
    shift = (np.arange(points)[None, :] - np.arange(points)[:, None]) % points
    keep = (weights[:, None] * np.cos(angles)).sum(0)
    slope = -(weights[:, None] * slopes[:, None] * np.sin(angles)).sum(0)
    curve = -(weights[:, None] * slopes[:, None] ** 2 * np.cos(angles)).sum(0)
    return keep[shift], slope[shift], curve[shift]


def product(left, right):
    dot = functools.partial(jnp.dot, preferred_element_type=jnp.float32)
    return dot(left[0], right[0]) + (dot(left[0], right[1]) + dot(left[1], right[0]))


def lane_groups(shape):
    return lax.broadcasted_iota(jnp.int32, shape, len(shape) - 1) // GROUP


def filter_kernel(
    velocity_hbm,
    high_hbm,
    low_hbm,
    smooth_hbm,
    message_hbm,
    velocity_ref,
    high_ref,
    low_ref,
    smooth_ref,
    message_ref,
    in_sems,
    out_sems,
):
    sections, points, width = high_ref.shape
    components, planes, rows, _ = velocity_ref.shape
    incoming = [pltpu.make_async_copy(velocity_hbm, velocity_ref, in_sems.at[0])]
    for section in range(sections):
        for source, target in ((high_hbm, high_ref), (low_hbm, low_ref)):
            incoming.append(
                pltpu.make_async_copy(
                    source.at[section], target.at[section], in_sems.at[len(incoming)]
                )
            )
    for copy in incoming:
        copy.start()
    incoming[0].wait()
    lines = components * planes * rows
    high, low = halves(velocity_ref[...].reshape(lines, points))
    both = jnp.concatenate([high, low], axis=0)
    groups = lane_groups((planes, rows, LANES))
    outgoing = []
    for section in range(sections):
        incoming[1 + 2 * section].wait()
        large = jnp.dot(both, high_ref[section], preferred_element_type=jnp.float32)
        incoming[2 + 2 * section].wait()
        small = jnp.dot(high, low_ref[section], preferred_element_type=jnp.float32)
        smooth = large[:lines] + (large[lines:] + small)
        smooth = smooth.reshape(components, planes, rows, width)
        for local in range(width // LANES):
            block = section * (width // LANES) + local
            tile = smooth[:, :, :, local * LANES : (local + 1) * LANES]
            smooth_ref[block] = tile
            turned = [tile[0]] + [pltpu.roll(tile[c], c * GROUP, 2) for c in range(1, components)]
            for part in range(GROUPS):
                chosen = jnp.zeros_like(turned[0])
                for c in range(components):
                    chosen = jnp.where(groups == (part + c) % GROUPS, turned[c], chosen)
                message_ref[block, part] = chosen
        here = pl.ds(section * (width // LANES), width // LANES)
        for source, target in ((message_ref, message_hbm), (smooth_ref, smooth_hbm)):
            copy = pltpu.make_async_copy(
                source.at[here], target.at[here], out_sems.at[len(outgoing)]
            )
            copy.start()
            outgoing.append(copy)
    for copy in outgoing:
        copy.wait()


def theta_kernel(velocity_ref, table_hbm, slope_ref, curve_ref, table_ref, sem):
    copy = pltpu.make_async_copy(table_hbm, table_ref, sem)
    copy.start()
    components, planes, rows, points = velocity_ref.shape
    velocity = halves(velocity_ref[...].reshape(components * planes * rows, points))
    copy.wait()
    both = product(velocity, (table_ref[0], table_ref[1]))
    slope_ref[...] = both[:, :points].reshape(velocity_ref.shape)
    curve_ref[...] = both[:, points:].reshape(velocity_ref.shape)


def split_kernel(matrix_ref, split_ref):
    split_ref[0], split_ref[1] = halves(matrix_ref[...])


def wide_product(split_ref, rows, right):
    high, low = halves(right)
    both = jnp.concatenate([high, low], axis=1)
    large = jnp.dot(split_ref[0, rows], both, preferred_element_type=jnp.float32)
    small = jnp.dot(split_ref[1, rows], high, preferred_element_type=jnp.float32)
    return large[:, :LANES] + (large[:, LANES:] + small)


def radial_kernel(planes, pencil_ref, split_ref, result_hbm, result_ref, sems):
    part = lax.rem(lax.div(lax.axis_index("radial"), planes), GROUPS)
    pencil = pencil_ref[...]
    full = pencil.shape[0]
    once = wide_product(split_ref, slice(None), pencil)
    groups = lane_groups(pencil.shape)
    place = lax.rem(groups - part + GROUPS, GROUPS)
    speed = jnp.where(place == 0, pencil, jnp.zeros_like(pencil))
    speed = jnp.where(place == 1, pltpu.roll(pencil, GROUP, 1), speed)
    speed = jnp.where(place == 2, pltpu.roll(pencil, 2 * GROUP, 1), speed)
    pieces = sems.shape[0]
    copies = []
    for piece in range(pieces):
        rows = slice(piece * full // pieces, (piece + 1) * full // pieces)
        twice = wide_product(split_ref, rows, once)
        result_ref[rows] = viscosity * twice - speed[rows] * once[rows]
        here = pl.ds(piece * full // pieces, full // pieces)
        copy = pltpu.make_async_copy(result_ref.at[here], result_hbm.at[here], sems.at[piece])
        copy.start()
        copies.append(copy)
    for copy in copies:
        copy.wait()


def local_kernel(
    smooth_ref, before_ref, after_ref, slope_ref, curve_ref, previous_ref, ratio_ref, result_ref
):
    blocks, components, planes, rows, _ = smooth_ref.shape
    ratio = ratio_ref[...]
    square = ratio * ratio
    for block in range(blocks):
        lanes = slice(block * LANES, (block + 1) * LANES)
        for c in range(components):
            line = [before_ref[block, c, plane] for plane in range(planes)]
            line += [smooth_ref[block, c, plane] for plane in range(planes)]
            line += [after_ref[block, c, plane] for plane in range(planes)]
            for plane in range(planes):
                here = planes + plane
                first = jnp.zeros_like(line[here])
                second = second_centre * line[here]
                for k in range(4):
                    up, down = line[here + k + 1], line[here - k - 1]
                    first = first + first_coefs[k] * (up - down)
                    second = second + second_coefs[k] * (up + down)
                second = second + square * curve_ref[c, plane, :, lanes]
                speed_theta = smooth_ref[block, 1, plane] * ratio
                result_ref[c, plane, :, lanes] = (
                    section_carry * previous_ref[c, plane, :, lanes]
                    + viscosity * second
                    - speed_theta * slope_ref[c, plane, :, lanes]
                    - smooth_ref[block, 2, plane] * first
                )


def final_kernel(radial_ref, local_ref, velocity_ref, velocity_out_ref, rhs_out_ref):
    components, planes, rows, points = velocity_ref.shape
    blocks = points // LANES
    groups = lane_groups((rows, LANES))
    for plane in range(planes):
        for block in range(blocks):
            tiles = [
                radial_ref[(block * GROUPS + part) * planes + plane] for part in range(GROUPS)
            ]
            for c in range(components):
                chosen = tiles[0]
                for part in range(1, GROUPS):
                    chosen = jnp.where(groups == (part + c) % GROUPS, tiles[part], chosen)
                if c > 0:
                    chosen = pltpu.roll(chosen, LANES - c * GROUP, 1)
                lanes = slice(block * LANES, (block + 1) * LANES)
                rhs = local_ref[c, plane, :, lanes] + chosen
                rhs_out_ref[c, plane, :, lanes] = rhs
                velocity_out_ref[c, plane, :, lanes] = (
                    velocity_ref[c, plane, :, lanes] + (section_weight * timestep) * rhs
                )


VMEM = pl.BlockSpec(memory_space=pltpu.VMEM)
HBM = pl.BlockSpec(memory_space=pltpu.HBM)


in_hbm = functools.partial(pltpu.with_memory_space_constraint, memory_space=pltpu.HBM)
in_vmem = functools.partial(pltpu.with_memory_space_constraint, memory_space=pltpu.VMEM)


def call(kernel, name, in_specs, outs, flops, moved, scratch=()):
    return pl.pallas_call(
        kernel,
        out_shape=[
            pltpu.HBM(shape, dtype) if spec is HBM else jax.ShapeDtypeStruct(shape, dtype)
            for shape, dtype, spec in outs
        ],
        in_specs=in_specs,
        out_specs=[spec for _, _, spec in outs],
        scratch_shapes=list(scratch),
        compiler_params=pltpu.CompilerParams(vmem_limit_bytes=24 * 1024 * 1024),
        cost_estimate=pl.CostEstimate(flops=flops, bytes_accessed=moved, transcendentals=0),
        name=name,
    )


def sections_of(matrix, sections):
    points, width = matrix.shape
    return np.ascontiguousarray(
        np.transpose(matrix.reshape(points, sections, width // sections), (1, 0, 2))
    )


def shards(velocity, previous_rhs, radial_deriv, inv_radius):
    components, planes, radial_rows, points = velocity.shape
    peers = lax.axis_size("radial")
    shape = velocity.shape
    size = velocity.size
    blocks = points // LANES
    sections = 2
    f32, bf16, dma = jnp.float32, jnp.bfloat16, pltpu.SemaphoreType.DMA
    keep, slope, curve = circulants(KEEP, points)
    keep_high, keep_low = (sections_of(half, sections) for half in host_halves(keep))
    theta = np.stack(host_halves(np.concatenate([slope, curve], axis=1)))

    smooth_shape = (blocks, components, planes, radial_rows, LANES)
    message_shape = (blocks, GROUPS, planes, radial_rows, LANES)
    smooth, message = call(
        filter_kernel,
        "filter",
        [HBM] * 3,
        [(smooth_shape, f32, HBM), (message_shape, f32, HBM)],
        6 * size * points,
        20 * size,
        [
            pltpu.VMEM(shape, f32),
            pltpu.VMEM(keep_high.shape, bf16),
            pltpu.VMEM(keep_low.shape, bf16),
            pltpu.VMEM(smooth_shape, f32),
            pltpu.VMEM(message_shape, f32),
            dma((1 + 2 * sections,)),
            dma((2 * sections,)),
        ],
    )(*(in_hbm(part) for part in (velocity, jnp.asarray(keep_high), jnp.asarray(keep_low))))
    pencil = lax.all_to_all(
        message.reshape(peers, radial_rows, LANES), "radial", split_axis=0, concat_axis=0, tiled=True
    )

    ring = lax.axis_size("axial")
    up = [(i, (i + 1) % ring) for i in range(ring)]
    down = [(j, i) for i, j in up]
    before = lax.ppermute(smooth, "axial", up)
    after = lax.ppermute(smooth, "axial", down)
    theta_slope, theta_curve = call(
        theta_kernel,
        "theta",
        [VMEM, HBM],
        [(shape, f32, VMEM)] * 2,
        12 * size * points,
        24 * size,
        [pltpu.VMEM(theta.shape, bf16), dma(())],
    )(velocity, in_hbm(jnp.asarray(theta)))

    full = peers * radial_rows
    (split,) = call(
        split_kernel,
        "split",
        [VMEM],
        [((2, full, full), bf16, VMEM)],
        4 * full * full,
        8 * full * full,
    )(radial_deriv)
    pieces = 4
    (result,) = call(
        functools.partial(radial_kernel, planes),
        "radial",
        [VMEM] * 2,
        [((full, LANES), f32, HBM)],
        12 * full * full * LANES,
        4 * full * (full + 2 * LANES),
        [pltpu.VMEM((full, LANES), f32), dma((pieces,))],
    )(in_vmem(pencil.reshape(full, LANES)), split)
    radial = lax.all_to_all(
        result.reshape(peers, radial_rows, LANES), "radial", split_axis=0, concat_axis=0, tiled=True
    )
    ratio = jnp.broadcast_to(inv_radius[:, None], (radial_rows, LANES))
    (local,) = call(
        local_kernel, "local", [VMEM] * 7, [(shape, f32, VMEM)], 40 * size, 32 * size
    )(smooth, before, after, theta_slope, theta_curve, previous_rhs, ratio)
    return call(
        final_kernel, "final", [VMEM] * 3, [(shape, f32, VMEM)] * 2, 10 * size, 20 * size
    )(radial, local, velocity)


def solution(mesh):
    in_specs = (
        P(None, "axial", "radial", None),
        P(None, "axial", "radial", None),
        P(),
        P("radial"),
    )
    out_specs = (P(None, "axial", "radial", None), P(None, "axial", "radial", None))

    def whole(*args):
        return tuple(shards(*args))

    return jax.shard_map(whole, mesh=mesh, in_specs=in_specs, out_specs=out_specs, check_vma=False)
```

```python
import functools
import math

import jax
import jax.numpy as jnp
import ml_dtypes
import numpy as np
from jax import lax
from jax.experimental import pallas as pl
from jax.experimental.pallas import tpu as pltpu
from jax.sharding import PartitionSpec as P

KEEP = 192
LANES = 128
GROUP = 32
GROUPS = LANES // GROUP

first_coefs = (4.0 / 5.0, -1.0 / 5.0, 4.0 / 105.0, -1.0 / 280.0)
second_coefs = (8.0 / 5.0, -1.0 / 5.0, 8.0 / 315.0, -1.0 / 560.0)
second_centre = -205.0 / 72.0
viscosity = 0.05
section_carry = -5.0 / 9.0
section_weight = 15.0 / 16.0
timestep = 0.1


def halves(array):
    high = array.astype(jnp.bfloat16)
    low = (array - high.astype(jnp.float32)).astype(jnp.bfloat16)
    return high, low


def host_halves(array):
    high = array.astype(ml_dtypes.bfloat16)
    low = (array - high.astype(np.float64)).astype(ml_dtypes.bfloat16)
    return high, low


def circulants(kept_modes, points):
    modes = np.arange(kept_modes)
    weights = np.where(modes == 0, 1.0, 2.0) / points
    slopes = modes * (2.0 * math.pi / points)
    angles = (modes[:, None] * np.arange(points)[None, :] % points) * (2.0 * math.pi / points)
    shift = (np.arange(points)[None, :] - np.arange(points)[:, None]) % points
    keep = (weights[:, None] * np.cos(angles)).sum(0)
    slope = -(weights[:, None] * slopes[:, None] * np.sin(angles)).sum(0)
    curve = -(weights[:, None] * slopes[:, None] ** 2 * np.cos(angles)).sum(0)
    return keep[shift], slope[shift], curve[shift]


def even_odd(matrix):
    half = matrix.shape[0] // 2
    same, cross = matrix[:half, :half], matrix[:half, half:]
    return (same + cross) / 2, (same - cross) / 2


def product(left, right):
    rows = left[0].shape[0]
    dot = functools.partial(jnp.dot, preferred_element_type=jnp.float32)
    large = dot(jnp.concatenate(left, axis=0), right[0])
    return large[:rows] + (large[rows:] + dot(left[0], right[1]))


def sum_and_difference(velocity):
    components, planes, rows, points = velocity.shape
    lines = velocity.reshape(components * planes * rows, points)
    first, second = lines[:, : points // 2], lines[:, points // 2 :]
    return halves(first + second), halves(first - second)


def lane_groups(shape):
    return lax.broadcasted_iota(jnp.int32, shape, len(shape) - 1) // GROUP


def filter_kernel(
    velocity_hbm,
    table_hbm,
    smooth_hbm,
    message_hbm,
    velocity_ref,
    table_ref,
    smooth_ref,
    message_ref,
    in_sems,
    out_sems,
):
    components, planes, rows, points = velocity_ref.shape
    incoming = [pltpu.make_async_copy(velocity_hbm, velocity_ref, in_sems.at[0])]
    for part in range(2):
        incoming.append(
            pltpu.make_async_copy(table_hbm.at[part], table_ref.at[part], in_sems.at[1 + part])
        )
    for copy in incoming:
        copy.start()
    incoming[0].wait()
    total, gap = sum_and_difference(velocity_ref[...])
    incoming[1].wait()
    even = product(total, (table_ref[0, 0], table_ref[0, 1]))
    incoming[2].wait()
    odd = product(gap, (table_ref[1, 0], table_ref[1, 1]))
    groups = lane_groups((planes, rows, LANES))
    outgoing = []
    blocks = points // LANES
    for section, smooth in enumerate((even + odd, even - odd)):
        smooth = smooth.reshape(components, planes, rows, points // 2)
        for local in range(blocks // 2):
            block = section * (blocks // 2) + local
            tile = smooth[:, :, :, local * LANES : (local + 1) * LANES]
            smooth_ref[block] = tile
            turned = [tile[0]] + [pltpu.roll(tile[c], c * GROUP, 2) for c in range(1, components)]
            for part in range(GROUPS):
                chosen = jnp.zeros_like(turned[0])
                for c in range(components):
                    chosen = jnp.where(groups == (part + c) % GROUPS, turned[c], chosen)
                message_ref[block, part] = chosen
        here = pl.ds(section * (blocks // 2), blocks // 2)
        for source, target in ((message_ref, message_hbm), (smooth_ref, smooth_hbm)):
            copy = pltpu.make_async_copy(
                source.at[here], target.at[here], out_sems.at[len(outgoing)]
            )
            copy.start()
            outgoing.append(copy)
    for copy in outgoing:
        copy.wait()


def theta_kernel(velocity_ref, table_hbm, slope_ref, curve_ref, table_ref, sem):
    copy = pltpu.make_async_copy(table_hbm, table_ref, sem)
    copy.start()
    total, gap = sum_and_difference(velocity_ref[...])
    copy.wait()
    even = product(total, (table_ref[0, 0], table_ref[0, 1]))
    odd = product(gap, (table_ref[1, 0], table_ref[1, 1]))
    half = even.shape[1] // 2
    shape = velocity_ref.shape[:3] + (half,)
    for index, result_ref in enumerate((slope_ref, curve_ref)):
        columns = slice(index * half, (index + 1) * half)
        result_ref[..., :half] = (even[:, columns] + odd[:, columns]).reshape(shape)
        result_ref[..., half:] = (even[:, columns] - odd[:, columns]).reshape(shape)


def matrix_kernel(matrix_ref, split_ref):
    matrix = matrix_ref[...]
    once = halves(matrix)
    twice = halves(product(once, once))
    _, pieces, rows, _ = split_ref.shape
    rows //= 2
    for piece in range(pieces):
        here = slice(piece * rows, (piece + 1) * rows)
        for half in range(2):
            split_ref[half, piece, :rows] = once[half][here]
            split_ref[half, piece, rows:] = twice[half][here]


def radial_kernel(planes, pencil_ref, split_ref, result_hbm, result_ref, sems):
    part = lax.rem(lax.div(lax.axis_index("radial"), planes), GROUPS)
    pencil = pencil_ref[...]
    high, low = halves(pencil)
    both = jnp.concatenate([high, low], axis=1)
    groups = lane_groups(pencil.shape)
    place = lax.rem(groups - part + GROUPS, GROUPS)
    speed = jnp.where(place == 0, pencil, jnp.zeros_like(pencil))
    speed = jnp.where(place == 1, pltpu.roll(pencil, GROUP, 1), speed)
    speed = jnp.where(place == 2, pltpu.roll(pencil, 2 * GROUP, 1), speed)
    _, pieces, rows, _ = split_ref.shape
    rows //= 2
    copies = []
    for piece in range(pieces):
        large = jnp.dot(split_ref[0, piece], both, preferred_element_type=jnp.float32)
        small = jnp.dot(split_ref[1, piece], high, preferred_element_type=jnp.float32)
        derivs = large[:, :LANES] + (large[:, LANES:] + small)
        here = slice(piece * rows, (piece + 1) * rows)
        result_ref[here] = viscosity * derivs[rows:] - speed[here] * derivs[:rows]
        here = pl.ds(piece * rows, rows)
        copy = pltpu.make_async_copy(result_ref.at[here], result_hbm.at[here], sems.at[piece])
        copy.start()
        copies.append(copy)
    for copy in copies:
        copy.wait()


def local_kernel(
    smooth_ref, before_ref, after_ref, slope_ref, curve_ref, previous_ref, ratio_ref, result_ref
):
    blocks, components, planes, rows, _ = smooth_ref.shape
    ratio = ratio_ref[...]
    square = ratio * ratio
    for block in range(blocks):
        lanes = slice(block * LANES, (block + 1) * LANES)
        for c in range(components):
            line = [before_ref[block, c, plane] for plane in range(planes)]
            line += [smooth_ref[block, c, plane] for plane in range(planes)]
            line += [after_ref[block, c, plane] for plane in range(planes)]
            for plane in range(planes):
                here = planes + plane
                first = jnp.zeros_like(line[here])
                second = second_centre * line[here]
                for k in range(4):
                    up, down = line[here + k + 1], line[here - k - 1]
                    first = first + first_coefs[k] * (up - down)
                    second = second + second_coefs[k] * (up + down)
                second = second + square * curve_ref[c, plane, :, lanes]
                speed_theta = smooth_ref[block, 1, plane] * ratio
                result_ref[c, plane, :, lanes] = (
                    section_carry * previous_ref[c, plane, :, lanes]
                    + viscosity * second
                    - speed_theta * slope_ref[c, plane, :, lanes]
                    - smooth_ref[block, 2, plane] * first
                )


def final_kernel(
    radial_ref,
    local_ref,
    velocity_ref,
    velocity_hbm,
    rhs_hbm,
    velocity_out_ref,
    rhs_out_ref,
    sems,
):
    components, planes, rows, points = velocity_ref.shape
    blocks = points // LANES
    groups = lane_groups((rows, LANES))
    copies = []
    for plane in range(planes):
        for block in range(blocks):
            tiles = [
                radial_ref[(block * GROUPS + part) * planes + plane] for part in range(GROUPS)
            ]
            for c in range(components):
                chosen = tiles[0]
                for part in range(1, GROUPS):
                    chosen = jnp.where(groups == (part + c) % GROUPS, tiles[part], chosen)
                if c > 0:
                    chosen = pltpu.roll(chosen, LANES - c * GROUP, 1)
                lanes = slice(block * LANES, (block + 1) * LANES)
                rhs = local_ref[c, plane, :, lanes] + chosen
                rhs_out_ref[c, plane, :, lanes] = rhs
                velocity_out_ref[c, plane, :, lanes] = (
                    velocity_ref[c, plane, :, lanes] + (section_weight * timestep) * rhs
                )
        here = (slice(None), pl.ds(plane, 1))
        for source, target in ((rhs_out_ref, rhs_hbm), (velocity_out_ref, velocity_hbm)):
            copy = pltpu.make_async_copy(
                source.at[here], target.at[here], sems.at[len(copies)]
            )
            copy.start()
            copies.append(copy)
    for copy in copies:
        copy.wait()


VMEM = pl.BlockSpec(memory_space=pltpu.VMEM)
HBM = pl.BlockSpec(memory_space=pltpu.HBM)


in_hbm = functools.partial(pltpu.with_memory_space_constraint, memory_space=pltpu.HBM)
in_vmem = functools.partial(pltpu.with_memory_space_constraint, memory_space=pltpu.VMEM)


def call(kernel, name, in_specs, outs, flops, moved, scratch=()):
    return pl.pallas_call(
        kernel,
        out_shape=[
            pltpu.HBM(shape, dtype) if spec is HBM else jax.ShapeDtypeStruct(shape, dtype)
            for shape, dtype, spec in outs
        ],
        in_specs=in_specs,
        out_specs=[spec for _, _, spec in outs],
        scratch_shapes=list(scratch),
        compiler_params=pltpu.CompilerParams(vmem_limit_bytes=24 * 1024 * 1024),
        cost_estimate=pl.CostEstimate(flops=flops, bytes_accessed=moved, transcendentals=0),
        name=name,
    )


def shards(velocity, previous_rhs, radial_deriv, inv_radius):
    components, planes, radial_rows, points = velocity.shape
    peers = lax.axis_size("radial")
    shape = velocity.shape
    size = velocity.size
    blocks = points // LANES
    f32, bf16, dma = jnp.float32, jnp.bfloat16, pltpu.SemaphoreType.DMA
    keep, slope, curve = (even_odd(matrix) for matrix in circulants(KEEP, points))
    keep = np.stack([np.stack(host_halves(part)) for part in keep])
    theta = np.stack(
        [np.stack(host_halves(np.concatenate(pair, axis=1))) for pair in zip(slope, curve)]
    )

    smooth_shape = (blocks, components, planes, radial_rows, LANES)
    message_shape = (blocks, GROUPS, planes, radial_rows, LANES)
    smooth, message = call(
        filter_kernel,
        "filter",
        [HBM] * 2,
        [(smooth_shape, f32, HBM), (message_shape, f32, HBM)],
        6 * size * points,
        20 * size,
        [
            pltpu.VMEM(shape, f32),
            pltpu.VMEM(keep.shape, bf16),
            pltpu.VMEM(smooth_shape, f32),
            pltpu.VMEM(message_shape, f32),
            dma((3,)),
            dma((4,)),
        ],
    )(in_hbm(velocity), in_hbm(jnp.asarray(keep)))
    pencil = lax.all_to_all(
        message.reshape(peers, radial_rows, LANES), "radial", split_axis=0, concat_axis=0, tiled=True
    )

    ring = lax.axis_size("axial")
    up = [(i, (i + 1) % ring) for i in range(ring)]
    down = [(j, i) for i, j in up]
    before = lax.ppermute(smooth, "axial", up)
    after = lax.ppermute(smooth, "axial", down)
    theta_slope, theta_curve = call(
        theta_kernel,
        "theta",
        [VMEM, HBM],
        [(shape, f32, VMEM)] * 2,
        12 * size * points,
        24 * size,
        [pltpu.VMEM(theta.shape, bf16), dma(())],
    )(velocity, in_hbm(jnp.asarray(theta)))

    full = peers * radial_rows
    pieces = 4
    (split,) = call(
        matrix_kernel,
        "matrix",
        [VMEM],
        [((2, pieces, 2 * full // pieces, full), bf16, VMEM)],
        6 * full * full * full,
        12 * full * full,
    )(radial_deriv)
    (result,) = call(
        functools.partial(radial_kernel, planes),
        "radial",
        [VMEM] * 2,
        [((full, LANES), f32, HBM)],
        12 * full * full * LANES,
        4 * full * (full + 2 * LANES),
        [pltpu.VMEM((full, LANES), f32), dma((pieces,))],
    )(in_vmem(pencil.reshape(full, LANES)), split)
    radial = lax.all_to_all(
        result.reshape(peers, radial_rows, LANES), "radial", split_axis=0, concat_axis=0, tiled=True
    )
    ratio = jnp.broadcast_to(inv_radius[:, None], (radial_rows, LANES))
    (local,) = call(
        local_kernel, "local", [VMEM] * 7, [(shape, f32, VMEM)], 40 * size, 32 * size
    )(smooth, before, after, theta_slope, theta_curve, previous_rhs, ratio)
    return call(
        final_kernel,
        "final",
        [VMEM] * 3,
        [(shape, f32, HBM)] * 2,
        10 * size,
        20 * size,
        [pltpu.VMEM(shape, f32), pltpu.VMEM(shape, f32), dma((2 * planes,))],
    )(radial, local, velocity)


def solution(mesh):
    in_specs = (
        P(None, "axial", "radial", None),
        P(None, "axial", "radial", None),
        P(),
        P("radial"),
    )
    out_specs = (P(None, "axial", "radial", None), P(None, "axial", "radial", None))

    def whole(*args):
        return tuple(shards(*args))

    return jax.shard_map(whole, mesh=mesh, in_specs=in_specs, out_specs=out_specs, check_vma=False)
```

```python
import functools
import math

import jax
import jax.numpy as jnp
import ml_dtypes
import numpy as np
from jax import lax
from jax.experimental import pallas as pl
from jax.experimental.pallas import tpu as pltpu
from jax.sharding import PartitionSpec as P

KEEP = 192
LANES = 128
GROUP = 32
GROUPS = LANES // GROUP
FIRST = 52

first_coefs = (4.0 / 5.0, -1.0 / 5.0, 4.0 / 105.0, -1.0 / 280.0)
second_coefs = (8.0 / 5.0, -1.0 / 5.0, 8.0 / 315.0, -1.0 / 560.0)
second_centre = -205.0 / 72.0
viscosity = 0.05
section_carry = -5.0 / 9.0
section_weight = 15.0 / 16.0
timestep = 0.1


def halves(array):
    high = array.astype(jnp.bfloat16)
    low = (array - high.astype(jnp.float32)).astype(jnp.bfloat16)
    return high, low


def host_halves(array):
    high = array.astype(ml_dtypes.bfloat16)
    low = (array - high.astype(np.float64)).astype(ml_dtypes.bfloat16)
    return high, low


def circulants(kept_modes, points):
    modes = np.arange(kept_modes)
    weights = np.where(modes == 0, 1.0, 2.0) / points
    slopes = modes * (2.0 * math.pi / points)
    angles = (modes[:, None] * np.arange(points)[None, :] % points) * (2.0 * math.pi / points)
    shift = (np.arange(points)[None, :] - np.arange(points)[:, None]) % points
    keep = (weights[:, None] * np.cos(angles)).sum(0)
    slope = -(weights[:, None] * slopes[:, None] * np.sin(angles)).sum(0)
    curve = -(weights[:, None] * slopes[:, None] ** 2 * np.cos(angles)).sum(0)
    return keep[shift], slope[shift], curve[shift]


def even_odd(matrix):
    half = matrix.shape[0] // 2
    same, cross = matrix[:half, :half], matrix[:half, half:]
    return (same + cross) / 2, (same - cross) / 2


def product(left, right):
    rows = left[0].shape[0]
    dot = functools.partial(jnp.dot, preferred_element_type=jnp.float32)
    large = dot(jnp.concatenate(left, axis=0), right[0])
    return large[:rows] + (large[rows:] + dot(left[0], right[1]))


def sum_and_difference(velocity):
    components, planes, rows, points = velocity.shape
    lines = velocity.reshape(components * planes * rows, points)
    first, second = lines[:, : points // 2], lines[:, points // 2 :]
    return halves(first + second), halves(first - second)


def lane_groups(shape):
    return lax.broadcasted_iota(jnp.int32, shape, len(shape) - 1) // GROUP


def filter_kernel(
    velocity_hbm,
    table_hbm,
    smooth_hbm,
    message_hbm,
    velocity_ref,
    table_ref,
    smooth_ref,
    message_ref,
    in_sems,
    out_sems,
):
    components, planes, rows, points = velocity_ref.shape
    incoming = [pltpu.make_async_copy(velocity_hbm, velocity_ref, in_sems.at[0])]
    for part in range(2):
        incoming.append(
            pltpu.make_async_copy(table_hbm.at[part], table_ref.at[part], in_sems.at[1 + part])
        )
    for copy in incoming:
        copy.start()
    incoming[0].wait()
    total, gap = sum_and_difference(velocity_ref[...])
    incoming[1].wait()
    even = product(total, (table_ref[0, 0], table_ref[0, 1]))
    incoming[2].wait()
    odd = product(gap, (table_ref[1, 0], table_ref[1, 1]))
    groups = lane_groups((planes, rows, LANES))
    outgoing = []
    blocks = points // LANES
    for section, smooth in enumerate((even + odd, even - odd)):
        smooth = smooth.reshape(components, planes, rows, points // 2)
        for local in range(blocks // 2):
            block = section * (blocks // 2) + local
            tile = smooth[:, :, :, local * LANES : (local + 1) * LANES]
            smooth_ref[block] = tile
            turned = [tile[0]] + [pltpu.roll(tile[c], c * GROUP, 2) for c in range(1, components)]
            for part in range(GROUPS):
                chosen = jnp.zeros_like(turned[0])
                for c in range(components):
                    chosen = jnp.where(groups == (part + c) % GROUPS, turned[c], chosen)
                message_ref[block, part] = chosen
        here = pl.ds(section * (blocks // 2), blocks // 2)
        for source, target in ((message_ref, message_hbm), (smooth_ref, smooth_hbm)):
            copy = pltpu.make_async_copy(
                source.at[here], target.at[here], out_sems.at[len(outgoing)]
            )
            copy.start()
            outgoing.append(copy)
    for copy in outgoing:
        copy.wait()


def theta_kernel(velocity_ref, table_hbm, slope_ref, curve_ref, table_ref, sem):
    copy = pltpu.make_async_copy(table_hbm, table_ref, sem)
    copy.start()
    total, gap = sum_and_difference(velocity_ref[...])
    copy.wait()
    even = product(total, (table_ref[0, 0], table_ref[0, 1]))
    odd = product(gap, (table_ref[1, 0], table_ref[1, 1]))
    half = even.shape[1] // 2
    shape = velocity_ref.shape[:3] + (half,)
    for index, result_ref in enumerate((slope_ref, curve_ref)):
        columns = slice(index * half, (index + 1) * half)
        result_ref[..., :half] = (even[:, columns] + odd[:, columns]).reshape(shape)
        result_ref[..., half:] = (even[:, columns] - odd[:, columns]).reshape(shape)


def matrix_kernel(turn, matrix_ref, split_ref):
    matrix = pltpu.roll(pltpu.roll(matrix_ref[...], turn, 0), turn, 1)
    once = halves(matrix)
    twice = halves(product(once, once))
    _, pieces, rows, _ = split_ref.shape
    rows //= 2
    for piece in range(pieces):
        here = slice(piece * rows, (piece + 1) * rows)
        for half in range(2):
            split_ref[half, piece, :rows] = once[half][here]
            split_ref[half, piece, rows:] = twice[half][here]


def radial_kernel(planes, first, peers, pencil_ref, split_ref, result_hbm, result_ref, sems):
    position = lax.rem(lax.axis_index("radial") + (peers - first), peers)
    part = lax.rem(lax.div(position, planes), GROUPS)
    pencil = pencil_ref[...]
    high, low = halves(pencil)
    both = jnp.concatenate([high, low], axis=1)
    groups = lane_groups(pencil.shape)
    place = lax.rem(groups - part + GROUPS, GROUPS)
    speed = jnp.where(place == 0, pencil, jnp.zeros_like(pencil))
    speed = jnp.where(place == 1, pltpu.roll(pencil, GROUP, 1), speed)
    speed = jnp.where(place == 2, pltpu.roll(pencil, 2 * GROUP, 1), speed)
    _, pieces, rows, _ = split_ref.shape
    rows //= 2
    copies = []
    for piece in range(pieces):
        large = jnp.dot(split_ref[0, piece], both, preferred_element_type=jnp.float32)
        small = jnp.dot(split_ref[1, piece], high, preferred_element_type=jnp.float32)
        derivs = large[:, :LANES] + (large[:, LANES:] + small)
        here = slice(piece * rows, (piece + 1) * rows)
        result_ref[here] = viscosity * derivs[rows:] - speed[here] * derivs[:rows]
        here = pl.ds(piece * rows, rows)
        copy = pltpu.make_async_copy(result_ref.at[here], result_hbm.at[here], sems.at[piece])
        copy.start()
        copies.append(copy)
    for copy in copies:
        copy.wait()


def local_kernel(
    smooth_ref, before_ref, after_ref, slope_ref, curve_ref, previous_ref, ratio_ref, result_ref
):
    blocks, components, planes, rows, _ = smooth_ref.shape
    ratio = ratio_ref[...]
    square = ratio * ratio
    for block in range(blocks):
        lanes = slice(block * LANES, (block + 1) * LANES)
        for c in range(components):
            line = [before_ref[block, c, plane] for plane in range(planes)]
            line += [smooth_ref[block, c, plane] for plane in range(planes)]
            line += [after_ref[block, c, plane] for plane in range(planes)]
            for plane in range(planes):
                here = planes + plane
                first = jnp.zeros_like(line[here])
                second = second_centre * line[here]
                for k in range(4):
                    up, down = line[here + k + 1], line[here - k - 1]
                    first = first + first_coefs[k] * (up - down)
                    second = second + second_coefs[k] * (up + down)
                second = second + square * curve_ref[c, plane, :, lanes]
                speed_theta = smooth_ref[block, 1, plane] * ratio
                result_ref[c, plane, :, lanes] = (
                    section_carry * previous_ref[c, plane, :, lanes]
                    + viscosity * second
                    - speed_theta * slope_ref[c, plane, :, lanes]
                    - smooth_ref[block, 2, plane] * first
                )


def final_kernel(
    radial_ref,
    local_ref,
    velocity_ref,
    velocity_hbm,
    rhs_hbm,
    velocity_out_ref,
    rhs_out_ref,
    sems,
):
    components, planes, rows, points = velocity_ref.shape
    blocks = points // LANES
    groups = lane_groups((rows, LANES))
    copies = []
    for plane in range(planes):
        for block in range(blocks):
            tiles = [
                radial_ref[(block * GROUPS + part) * planes + plane] for part in range(GROUPS)
            ]
            for c in range(components):
                chosen = tiles[0]
                for part in range(1, GROUPS):
                    chosen = jnp.where(groups == (part + c) % GROUPS, tiles[part], chosen)
                if c > 0:
                    chosen = pltpu.roll(chosen, LANES - c * GROUP, 1)
                lanes = slice(block * LANES, (block + 1) * LANES)
                rhs = local_ref[c, plane, :, lanes] + chosen
                rhs_out_ref[c, plane, :, lanes] = rhs
                velocity_out_ref[c, plane, :, lanes] = (
                    velocity_ref[c, plane, :, lanes] + (section_weight * timestep) * rhs
                )
        here = (slice(None), pl.ds(plane, 1))
        for source, target in ((rhs_out_ref, rhs_hbm), (velocity_out_ref, velocity_hbm)):
            copy = pltpu.make_async_copy(
                source.at[here], target.at[here], sems.at[len(copies)]
            )
            copy.start()
            copies.append(copy)
    for copy in copies:
        copy.wait()


VMEM = pl.BlockSpec(memory_space=pltpu.VMEM)
HBM = pl.BlockSpec(memory_space=pltpu.HBM)


in_hbm = functools.partial(pltpu.with_memory_space_constraint, memory_space=pltpu.HBM)
in_vmem = functools.partial(pltpu.with_memory_space_constraint, memory_space=pltpu.VMEM)


def call(kernel, name, in_specs, outs, flops, moved, scratch=()):
    return pl.pallas_call(
        kernel,
        out_shape=[
            pltpu.HBM(shape, dtype) if spec is HBM else jax.ShapeDtypeStruct(shape, dtype)
            for shape, dtype, spec in outs
        ],
        in_specs=in_specs,
        out_specs=[spec for _, _, spec in outs],
        scratch_shapes=list(scratch),
        compiler_params=pltpu.CompilerParams(vmem_limit_bytes=24 * 1024 * 1024),
        cost_estimate=pl.CostEstimate(flops=flops, bytes_accessed=moved, transcendentals=0),
        name=name,
    )


def shards(velocity, previous_rhs, radial_deriv, inv_radius):
    components, planes, radial_rows, points = velocity.shape
    peers = lax.axis_size("radial")
    shape = velocity.shape
    size = velocity.size
    blocks = points // LANES
    f32, bf16, dma = jnp.float32, jnp.bfloat16, pltpu.SemaphoreType.DMA
    keep, slope, curve = (even_odd(matrix) for matrix in circulants(KEEP, points))
    keep = np.stack([np.stack(host_halves(part)) for part in keep])
    theta = np.stack(
        [np.stack(host_halves(np.concatenate(pair, axis=1))) for pair in zip(slope, curve)]
    )

    smooth_shape = (blocks, components, planes, radial_rows, LANES)
    message_shape = (blocks, GROUPS, planes, radial_rows, LANES)
    smooth, message = call(
        filter_kernel,
        "filter",
        [HBM] * 2,
        [(smooth_shape, f32, HBM), (message_shape, f32, HBM)],
        6 * size * points,
        20 * size,
        [
            pltpu.VMEM(shape, f32),
            pltpu.VMEM(keep.shape, bf16),
            pltpu.VMEM(smooth_shape, f32),
            pltpu.VMEM(message_shape, f32),
            dma((3,)),
            dma((4,)),
        ],
    )(in_hbm(velocity), in_hbm(jnp.asarray(keep)))
    first = FIRST % peers
    exchange = functools.partial(
        lax.all_to_all,
        axis_name="radial",
        split_axis=0,
        concat_axis=0,
        tiled=True,
        axis_index_groups=[[(first + i) % peers for i in range(peers)]],
    )
    pencil = exchange(message.reshape(peers, radial_rows, LANES))

    ring = lax.axis_size("axial")
    up = [(i, (i + 1) % ring) for i in range(ring)]
    down = [(j, i) for i, j in up]
    before = lax.ppermute(smooth, "axial", up)
    after = lax.ppermute(smooth, "axial", down)
    theta_slope, theta_curve = call(
        theta_kernel,
        "theta",
        [VMEM, HBM],
        [(shape, f32, VMEM)] * 2,
        12 * size * points,
        24 * size,
        [pltpu.VMEM(theta.shape, bf16), dma(())],
    )(velocity, in_hbm(jnp.asarray(theta)))

    full = peers * radial_rows
    pieces = 4
    (split,) = call(
        functools.partial(matrix_kernel, (peers - first) * radial_rows % full),
        "matrix",
        [VMEM],
        [((2, pieces, 2 * full // pieces, full), bf16, VMEM)],
        6 * full * full * full,
        12 * full * full,
    )(radial_deriv)
    (result,) = call(
        functools.partial(radial_kernel, planes, first, peers),
        "radial",
        [VMEM] * 2,
        [((full, LANES), f32, HBM)],
        12 * full * full * LANES,
        4 * full * (full + 2 * LANES),
        [pltpu.VMEM((full, LANES), f32), dma((pieces,))],
    )(in_vmem(pencil.reshape(full, LANES)), split)
    radial = exchange(result.reshape(peers, radial_rows, LANES))
    ratio = jnp.broadcast_to(inv_radius[:, None], (radial_rows, LANES))
    (local,) = call(
        local_kernel, "local", [VMEM] * 7, [(shape, f32, VMEM)], 40 * size, 32 * size
    )(smooth, before, after, theta_slope, theta_curve, previous_rhs, ratio)
    return call(
        final_kernel,
        "final",
        [VMEM] * 3,
        [(shape, f32, HBM)] * 2,
        10 * size,
        20 * size,
        [pltpu.VMEM(shape, f32), pltpu.VMEM(shape, f32), dma((2 * planes,))],
    )(radial, local, velocity)


def solution(mesh):
    in_specs = (
        P(None, "axial", "radial", None),
        P(None, "axial", "radial", None),
        P(),
        P("radial"),
    )
    out_specs = (P(None, "axial", "radial", None), P(None, "axial", "radial", None))

    def whole(*args):
        return tuple(shards(*args))

    return jax.shard_map(whole, mesh=mesh, in_specs=in_specs, out_specs=out_specs, check_vma=False)
```

```python
import functools
import math

import jax
import jax.numpy as jnp
import ml_dtypes
import numpy as np
from jax import lax
from jax.experimental import pallas as pl
from jax.experimental.pallas import tpu as pltpu
from jax.sharding import PartitionSpec as P

KEEP = 192
LANES = 128
GROUP = 32
GROUPS = LANES // GROUP
FIRST = 52

first_coefs = (4.0 / 5.0, -1.0 / 5.0, 4.0 / 105.0, -1.0 / 280.0)
second_coefs = (8.0 / 5.0, -1.0 / 5.0, 8.0 / 315.0, -1.0 / 560.0)
second_centre = -205.0 / 72.0
viscosity = 0.05
section_carry = -5.0 / 9.0
section_weight = 15.0 / 16.0
timestep = 0.1


def halves(array):
    high = array.astype(jnp.bfloat16)
    low = (array - high.astype(jnp.float32)).astype(jnp.bfloat16)
    return high, low


def host_halves(array):
    high = array.astype(ml_dtypes.bfloat16)
    low = (array - high.astype(np.float64)).astype(ml_dtypes.bfloat16)
    return high, low


def circulants(kept_modes, points):
    modes = np.arange(kept_modes)
    weights = np.where(modes == 0, 1.0, 2.0) / points
    slopes = modes * (2.0 * math.pi / points)
    angles = (modes[:, None] * np.arange(points)[None, :] % points) * (2.0 * math.pi / points)
    shift = (np.arange(points)[None, :] - np.arange(points)[:, None]) % points
    keep = (weights[:, None] * np.cos(angles)).sum(0)
    slope = -(weights[:, None] * slopes[:, None] * np.sin(angles)).sum(0)
    curve = -(weights[:, None] * slopes[:, None] ** 2 * np.cos(angles)).sum(0)
    return keep[shift], slope[shift], curve[shift]


def even_odd(matrix):
    half = matrix.shape[0] // 2
    same, cross = matrix[:half, :half], matrix[:half, half:]
    return (same + cross) / 2, (same - cross) / 2


def product(left, right):
    rows = left[0].shape[0]
    dot = functools.partial(jnp.dot, preferred_element_type=jnp.float32)
    large = dot(jnp.concatenate(left, axis=0), right[0])
    return large[:rows] + (large[rows:] + dot(left[0], right[1]))


def sum_and_difference(velocity):
    components, planes, rows, points = velocity.shape
    lines = velocity.reshape(components * planes * rows, points)
    first, second = lines[:, : points // 2], lines[:, points // 2 :]
    return halves(first + second), halves(first - second)


def lane_groups(shape):
    return lax.broadcasted_iota(jnp.int32, shape, len(shape) - 1) // GROUP


def filter_kernel(
    velocity_hbm,
    table_hbm,
    smooth_hbm,
    message_hbm,
    velocity_ref,
    table_ref,
    smooth_ref,
    message_ref,
    in_sems,
    out_sems,
):
    components, planes, rows, points = velocity_ref.shape
    incoming = [pltpu.make_async_copy(velocity_hbm, velocity_ref, in_sems.at[0])]
    for part in range(2):
        incoming.append(
            pltpu.make_async_copy(table_hbm.at[part], table_ref.at[part], in_sems.at[1 + part])
        )
    for copy in incoming:
        copy.start()
    incoming[0].wait()
    total, gap = sum_and_difference(velocity_ref[...])
    incoming[1].wait()
    even = product(total, (table_ref[0, 0], table_ref[0, 1]))
    incoming[2].wait()
    odd = product(gap, (table_ref[1, 0], table_ref[1, 1]))
    groups = lane_groups((planes, rows, LANES))
    outgoing = []
    blocks = points // LANES
    for section, smooth in enumerate((even + odd, even - odd)):
        smooth = smooth.reshape(components, planes, rows, points // 2)
        for local in range(blocks // 2):
            block = section * (blocks // 2) + local
            tile = smooth[:, :, :, local * LANES : (local + 1) * LANES]
            smooth_ref[block] = tile
            turned = [tile[0]] + [pltpu.roll(tile[c], c * GROUP, 2) for c in range(1, components)]
            for part in range(GROUPS):
                chosen = jnp.zeros_like(turned[0])
                for c in range(components):
                    chosen = jnp.where(groups == (part + c) % GROUPS, turned[c], chosen)
                message_ref[block, part] = chosen
        here = pl.ds(section * (blocks // 2), blocks // 2)
        for source, target in ((message_ref, message_hbm), (smooth_ref, smooth_hbm)):
            copy = pltpu.make_async_copy(
                source.at[here], target.at[here], out_sems.at[len(outgoing)]
            )
            copy.start()
            outgoing.append(copy)
    for copy in outgoing:
        copy.wait()


def theta_kernel(velocity_ref, table_hbm, slope_ref, curve_ref, table_ref, sem):
    copy = pltpu.make_async_copy(table_hbm, table_ref, sem)
    copy.start()
    total, gap = sum_and_difference(velocity_ref[...])
    copy.wait()
    even = product(total, (table_ref[0, 0], table_ref[0, 1]))
    odd = product(gap, (table_ref[1, 0], table_ref[1, 1]))
    half = even.shape[1] // 2
    shape = velocity_ref.shape[:3] + (half,)
    for index, result_ref in enumerate((slope_ref, curve_ref)):
        columns = slice(index * half, (index + 1) * half)
        result_ref[..., :half] = (even[:, columns] + odd[:, columns]).reshape(shape)
        result_ref[..., half:] = (even[:, columns] - odd[:, columns]).reshape(shape)


def matrix_kernel(turn, matrix_ref, split_ref):
    matrix = pltpu.roll(pltpu.roll(matrix_ref[...], turn, 0), turn, 1)
    once = halves(matrix)
    twice = halves(product(once, once))
    _, pieces, rows, _ = split_ref.shape
    rows //= 2
    for piece in range(pieces):
        here = slice(piece * rows, (piece + 1) * rows)
        for half in range(2):
            split_ref[half, piece, :rows] = once[half][here]
            split_ref[half, piece, rows:] = twice[half][here]


def radial_kernel(planes, first, peers, pencil_ref, split_ref, result_hbm, result_ref, sems):
    position = lax.rem(lax.axis_index("radial") + (peers - first), peers)
    part = lax.rem(lax.div(position, planes), GROUPS)
    pencil = pencil_ref[...]
    high, low = halves(pencil)
    both = jnp.concatenate([high, low], axis=1)
    groups = lane_groups(pencil.shape)
    place = lax.rem(groups - part + GROUPS, GROUPS)
    speed = jnp.where(place == 0, pencil, jnp.zeros_like(pencil))
    speed = jnp.where(place == 1, pltpu.roll(pencil, GROUP, 1), speed)
    speed = jnp.where(place == 2, pltpu.roll(pencil, 2 * GROUP, 1), speed)
    _, pieces, rows, _ = split_ref.shape
    rows //= 2
    copies = []
    for piece in range(pieces):
        large = jnp.dot(split_ref[0, piece], both, preferred_element_type=jnp.float32)
        small = jnp.dot(split_ref[1, piece], high, preferred_element_type=jnp.float32)
        derivs = large[:, :LANES] + (large[:, LANES:] + small)
        here = slice(piece * rows, (piece + 1) * rows)
        result_ref[here] = viscosity * derivs[rows:] - speed[here] * derivs[:rows]
        here = pl.ds(piece * rows, rows)
        copy = pltpu.make_async_copy(result_ref.at[here], result_hbm.at[here], sems.at[piece])
        copy.start()
        copies.append(copy)
    for copy in copies:
        copy.wait()


def local_kernel(
    smooth_ref, near_ref, far_ref, slope_ref, curve_ref, previous_ref, ratio_ref, result_ref
):
    blocks, components, planes, rows, _ = smooth_ref.shape
    ratio = ratio_ref[...]
    square = ratio * ratio
    odd = jnp.full(ratio.shape, lax.rem(lax.axis_index("axial"), 2)) == 1
    for block in range(blocks):
        lanes = slice(block * LANES, (block + 1) * LANES)
        for c in range(components):
            line = [None] * (3 * planes)
            for plane in range(planes):
                near, far = near_ref[block, c, plane], far_ref[block, c, plane]
                line[plane] = jnp.where(odd, near, far)
                line[planes + plane] = smooth_ref[block, c, plane]
                line[2 * planes + plane] = jnp.where(odd, far, near)
            for plane in range(planes):
                here = planes + plane
                first = jnp.zeros_like(line[here])
                second = second_centre * line[here]
                for k in range(4):
                    up, down = line[here + k + 1], line[here - k - 1]
                    first = first + first_coefs[k] * (up - down)
                    second = second + second_coefs[k] * (up + down)
                second = second + square * curve_ref[c, plane, :, lanes]
                speed_theta = smooth_ref[block, 1, plane] * ratio
                result_ref[c, plane, :, lanes] = (
                    section_carry * previous_ref[c, plane, :, lanes]
                    + viscosity * second
                    - speed_theta * slope_ref[c, plane, :, lanes]
                    - smooth_ref[block, 2, plane] * first
                )


def final_kernel(
    radial_ref,
    local_ref,
    velocity_ref,
    velocity_hbm,
    rhs_hbm,
    velocity_out_ref,
    rhs_out_ref,
    sems,
):
    components, planes, rows, points = velocity_ref.shape
    blocks = points // LANES
    groups = lane_groups((rows, LANES))
    copies = []
    for plane in range(planes):
        for block in range(blocks):
            tiles = [
                radial_ref[(block * GROUPS + part) * planes + plane] for part in range(GROUPS)
            ]
            for c in range(components):
                chosen = tiles[0]
                for part in range(1, GROUPS):
                    chosen = jnp.where(groups == (part + c) % GROUPS, tiles[part], chosen)
                if c > 0:
                    chosen = pltpu.roll(chosen, LANES - c * GROUP, 1)
                lanes = slice(block * LANES, (block + 1) * LANES)
                rhs = local_ref[c, plane, :, lanes] + chosen
                rhs_out_ref[c, plane, :, lanes] = rhs
                velocity_out_ref[c, plane, :, lanes] = (
                    velocity_ref[c, plane, :, lanes] + (section_weight * timestep) * rhs
                )
        here = (slice(None), pl.ds(plane, 1))
        for source, target in ((rhs_out_ref, rhs_hbm), (velocity_out_ref, velocity_hbm)):
            copy = pltpu.make_async_copy(
                source.at[here], target.at[here], sems.at[len(copies)]
            )
            copy.start()
            copies.append(copy)
    for copy in copies:
        copy.wait()


VMEM = pl.BlockSpec(memory_space=pltpu.VMEM)
HBM = pl.BlockSpec(memory_space=pltpu.HBM)


in_hbm = functools.partial(pltpu.with_memory_space_constraint, memory_space=pltpu.HBM)
in_vmem = functools.partial(pltpu.with_memory_space_constraint, memory_space=pltpu.VMEM)


def call(kernel, name, in_specs, outs, flops, moved, scratch=()):
    return pl.pallas_call(
        kernel,
        out_shape=[
            pltpu.HBM(shape, dtype) if spec is HBM else jax.ShapeDtypeStruct(shape, dtype)
            for shape, dtype, spec in outs
        ],
        in_specs=in_specs,
        out_specs=[spec for _, _, spec in outs],
        scratch_shapes=list(scratch),
        compiler_params=pltpu.CompilerParams(vmem_limit_bytes=24 * 1024 * 1024),
        cost_estimate=pl.CostEstimate(flops=flops, bytes_accessed=moved, transcendentals=0),
        name=name,
    )


def shards(velocity, previous_rhs, radial_deriv, inv_radius):
    components, planes, radial_rows, points = velocity.shape
    peers = lax.axis_size("radial")
    shape = velocity.shape
    size = velocity.size
    blocks = points // LANES
    f32, bf16, dma = jnp.float32, jnp.bfloat16, pltpu.SemaphoreType.DMA
    keep, slope, curve = (even_odd(matrix) for matrix in circulants(KEEP, points))
    keep = np.stack([np.stack(host_halves(part)) for part in keep])
    theta = np.stack(
        [np.stack(host_halves(np.concatenate(pair, axis=1))) for pair in zip(slope, curve)]
    )

    smooth_shape = (blocks, components, planes, radial_rows, LANES)
    message_shape = (blocks, GROUPS, planes, radial_rows, LANES)
    smooth, message = call(
        filter_kernel,
        "filter",
        [HBM] * 2,
        [(smooth_shape, f32, HBM), (message_shape, f32, HBM)],
        6 * size * points,
        20 * size,
        [
            pltpu.VMEM(shape, f32),
            pltpu.VMEM(keep.shape, bf16),
            pltpu.VMEM(smooth_shape, f32),
            pltpu.VMEM(message_shape, f32),
            dma((3,)),
            dma((4,)),
        ],
    )(in_hbm(velocity), in_hbm(jnp.asarray(keep)))
    first = FIRST % peers
    exchange = functools.partial(
        lax.all_to_all,
        axis_name="radial",
        split_axis=0,
        concat_axis=0,
        tiled=True,
        axis_index_groups=[[(first + i) % peers for i in range(peers)]],
    )
    pencil = exchange(message.reshape(peers, radial_rows, LANES))

    ring = lax.axis_size("axial")
    near = lax.ppermute(smooth, "axial", [(i, i ^ 1) for i in range(ring)])
    far = lax.ppermute(
        smooth, "axial", [(i, (i + (1 if i % 2 else ring - 1)) % ring) for i in range(ring)]
    )
    pencil, far = lax.optimization_barrier((pencil, far))
    theta_slope, theta_curve = call(
        theta_kernel,
        "theta",
        [VMEM, HBM],
        [(shape, f32, VMEM)] * 2,
        12 * size * points,
        24 * size,
        [pltpu.VMEM(theta.shape, bf16), dma(())],
    )(velocity, in_hbm(jnp.asarray(theta)))

    full = peers * radial_rows
    pieces = 4
    (split,) = call(
        functools.partial(matrix_kernel, (peers - first) * radial_rows % full),
        "matrix",
        [VMEM],
        [((2, pieces, 2 * full // pieces, full), bf16, VMEM)],
        6 * full * full * full,
        12 * full * full,
    )(radial_deriv)
    (result,) = call(
        functools.partial(radial_kernel, planes, first, peers),
        "radial",
        [VMEM] * 2,
        [((full, LANES), f32, HBM)],
        12 * full * full * LANES,
        4 * full * (full + 2 * LANES),
        [pltpu.VMEM((full, LANES), f32), dma((pieces,))],
    )(in_vmem(pencil.reshape(full, LANES)), split)
    radial = exchange(result.reshape(peers, radial_rows, LANES))
    ratio = jnp.broadcast_to(inv_radius[:, None], (radial_rows, LANES))
    (local,) = call(
        local_kernel, "local", [VMEM] * 7, [(shape, f32, VMEM)], 40 * size, 32 * size
    )(smooth, near, far, theta_slope, theta_curve, previous_rhs, ratio)
    return call(
        final_kernel,
        "final",
        [VMEM] * 3,
        [(shape, f32, HBM)] * 2,
        10 * size,
        20 * size,
        [pltpu.VMEM(shape, f32), pltpu.VMEM(shape, f32), dma((2 * planes,))],
    )(radial, local, velocity)


def solution(mesh):
    in_specs = (
        P(None, "axial", "radial", None),
        P(None, "axial", "radial", None),
        P(),
        P("radial"),
    )
    out_specs = (P(None, "axial", "radial", None), P(None, "axial", "radial", None))

    def whole(*args):
        return tuple(shards(*args))

    return jax.shard_map(whole, mesh=mesh, in_specs=in_specs, out_specs=out_specs, check_vma=False)
```

```python
import functools
import math

import jax
import jax.numpy as jnp
import ml_dtypes
import numpy as np
from jax import lax
from jax.experimental import pallas as pl
from jax.experimental.pallas import tpu as pltpu
from jax.sharding import PartitionSpec as P

KEEP = 192
LANES = 128
GROUP = 32
GROUPS = LANES // GROUP
FIRST = 52

first_coefs = (4.0 / 5.0, -1.0 / 5.0, 4.0 / 105.0, -1.0 / 280.0)
second_coefs = (8.0 / 5.0, -1.0 / 5.0, 8.0 / 315.0, -1.0 / 560.0)
second_centre = -205.0 / 72.0
viscosity = 0.05
section_carry = -5.0 / 9.0
section_weight = 15.0 / 16.0
timestep = 0.1


def halves(array):
    high = array.astype(jnp.bfloat16)
    low = (array - high.astype(jnp.float32)).astype(jnp.bfloat16)
    return high, low


def host_halves(array):
    high = array.astype(ml_dtypes.bfloat16)
    low = (array - high.astype(np.float64)).astype(ml_dtypes.bfloat16)
    return high, low


def circulants(kept_modes, points):
    modes = np.arange(kept_modes)
    weights = np.where(modes == 0, 1.0, 2.0) / points
    slopes = modes * (2.0 * math.pi / points)
    angles = (modes[:, None] * np.arange(points)[None, :] % points) * (2.0 * math.pi / points)
    shift = (np.arange(points)[None, :] - np.arange(points)[:, None]) % points
    keep = (weights[:, None] * np.cos(angles)).sum(0)
    slope = -(weights[:, None] * slopes[:, None] * np.sin(angles)).sum(0)
    curve = -(weights[:, None] * slopes[:, None] ** 2 * np.cos(angles)).sum(0)
    return keep[shift], slope[shift], curve[shift]


def even_odd(matrix):
    half = matrix.shape[0] // 2
    same, cross = matrix[:half, :half], matrix[:half, half:]
    return (same + cross) / 2, (same - cross) / 2


def product(left, right):
    rows = left[0].shape[0]
    dot = functools.partial(jnp.dot, preferred_element_type=jnp.float32)
    large = dot(jnp.concatenate(left, axis=0), right[0])
    return large[:rows] + (large[rows:] + dot(left[0], right[1]))


def sum_and_difference(velocity):
    components, planes, rows, points = velocity.shape
    lines = velocity.reshape(components * planes * rows, points)
    first, second = lines[:, : points // 2], lines[:, points // 2 :]
    return halves(first + second), halves(first - second)


def lane_groups(shape):
    return lax.broadcasted_iota(jnp.int32, shape, len(shape) - 1) // GROUP


def filter_kernel(
    velocity_hbm,
    table_hbm,
    smooth_hbm,
    message_hbm,
    velocity_ref,
    table_ref,
    smooth_ref,
    message_ref,
    in_sems,
    out_sems,
):
    components, planes, rows, points = velocity_ref.shape
    incoming = [pltpu.make_async_copy(velocity_hbm, velocity_ref, in_sems.at[0])]
    for part in range(2):
        incoming.append(
            pltpu.make_async_copy(table_hbm.at[part], table_ref.at[part], in_sems.at[1 + part])
        )
    for copy in incoming:
        copy.start()
    incoming[0].wait()
    total, gap = sum_and_difference(velocity_ref[...])
    incoming[1].wait()
    even = product(total, (table_ref[0, 0], table_ref[0, 1]))
    incoming[2].wait()
    odd = product(gap, (table_ref[1, 0], table_ref[1, 1]))
    groups = lane_groups((planes, rows, LANES))
    outgoing = []
    blocks = points // LANES
    for section, smooth in enumerate((even + odd, even - odd)):
        smooth = smooth.reshape(components, planes, rows, points // 2)
        for local in range(blocks // 2):
            block = section * (blocks // 2) + local
            tile = smooth[:, :, :, local * LANES : (local + 1) * LANES]
            smooth_ref[block] = tile
            turned = [tile[0]] + [pltpu.roll(tile[c], c * GROUP, 2) for c in range(1, components)]
            for part in range(GROUPS):
                chosen = jnp.zeros_like(turned[0])
                for c in range(components):
                    chosen = jnp.where(groups == (part + c) % GROUPS, turned[c], chosen)
                message_ref[block, part] = chosen
        here = pl.ds(section * (blocks // 2), blocks // 2)
        for source, target in ((message_ref, message_hbm), (smooth_ref, smooth_hbm)):
            copy = pltpu.make_async_copy(
                source.at[here], target.at[here], out_sems.at[len(outgoing)]
            )
            copy.start()
            outgoing.append(copy)
    for copy in outgoing:
        copy.wait()


def theta_kernel(velocity_ref, table_hbm, slope_ref, curve_ref, table_ref, sem):
    copy = pltpu.make_async_copy(table_hbm, table_ref, sem)
    copy.start()
    total, gap = sum_and_difference(velocity_ref[...])
    copy.wait()
    even = product(total, (table_ref[0, 0], table_ref[0, 1]))
    odd = product(gap, (table_ref[1, 0], table_ref[1, 1]))
    half = even.shape[1] // 2
    shape = velocity_ref.shape[:3] + (half,)
    for index, result_ref in enumerate((slope_ref, curve_ref)):
        columns = slice(index * half, (index + 1) * half)
        result_ref[..., :half] = (even[:, columns] + odd[:, columns]).reshape(shape)
        result_ref[..., half:] = (even[:, columns] - odd[:, columns]).reshape(shape)


def matrix_kernel(turn, matrix_ref, split_ref):
    matrix = pltpu.roll(pltpu.roll(matrix_ref[...], turn, 0), turn, 1)
    once = halves(matrix)
    twice = halves(product(once, once))
    _, pieces, rows, _ = split_ref.shape
    rows //= 2
    for piece in range(pieces):
        here = slice(piece * rows, (piece + 1) * rows)
        for half in range(2):
            split_ref[half, piece, :rows] = once[half][here]
            split_ref[half, piece, rows:] = twice[half][here]


def radial_kernel(planes, first, peers, pencil_ref, split_ref, result_hbm, result_ref, sems):
    position = lax.rem(lax.axis_index("radial") + (peers - first), peers)
    part = lax.rem(lax.div(position, planes), GROUPS)
    pencil = pencil_ref[...]
    high, low = halves(pencil)
    both = jnp.concatenate([high, low], axis=1)
    groups = lane_groups(pencil.shape)
    place = lax.rem(groups - part + GROUPS, GROUPS)
    speed = jnp.where(place == 0, pencil, jnp.zeros_like(pencil))
    speed = jnp.where(place == 1, pltpu.roll(pencil, GROUP, 1), speed)
    speed = jnp.where(place == 2, pltpu.roll(pencil, 2 * GROUP, 1), speed)
    _, pieces, rows, _ = split_ref.shape
    rows //= 2
    copies = []
    for piece in range(pieces):
        large = jnp.dot(split_ref[0, piece], both, preferred_element_type=jnp.float32)
        small = jnp.dot(split_ref[1, piece], high, preferred_element_type=jnp.float32)
        derivs = large[:, :LANES] + (large[:, LANES:] + small)
        here = slice(piece * rows, (piece + 1) * rows)
        result_ref[here] = viscosity * derivs[rows:] - speed[here] * derivs[:rows]
        here = pl.ds(piece * rows, rows)
        copy = pltpu.make_async_copy(result_ref.at[here], result_hbm.at[here], sems.at[piece])
        copy.start()
        copies.append(copy)
    for copy in copies:
        copy.wait()


def local_kernel(
    smooth_ref, near_ref, far_ref, slope_ref, curve_ref, previous_ref, ratio_ref, result_ref
):
    blocks, components, planes, rows, _ = smooth_ref.shape
    ratio = ratio_ref[...]
    square = ratio * ratio
    odd = jnp.full(ratio.shape, lax.rem(lax.axis_index("axial"), 2)) == 1
    for block in range(blocks):
        lanes = slice(block * LANES, (block + 1) * LANES)
        for c in range(components):
            line = [None] * (3 * planes)
            for plane in range(planes):
                near, far = near_ref[block, c, plane], far_ref[block, c, plane]
                line[plane] = jnp.where(odd, near, far)
                line[planes + plane] = smooth_ref[block, c, plane]
                line[2 * planes + plane] = jnp.where(odd, far, near)
            for plane in range(planes):
                here = planes + plane
                first = jnp.zeros_like(line[here])
                second = second_centre * line[here]
                for k in range(4):
                    up, down = line[here + k + 1], line[here - k - 1]
                    first = first + first_coefs[k] * (up - down)
                    second = second + second_coefs[k] * (up + down)
                second = second + square * curve_ref[c, plane, :, lanes]
                speed_theta = smooth_ref[block, 1, plane] * ratio
                result_ref[c, plane, :, lanes] = (
                    section_carry * previous_ref[c, plane, :, lanes]
                    + viscosity * second
                    - speed_theta * slope_ref[c, plane, :, lanes]
                    - smooth_ref[block, 2, plane] * first
                )


def final_kernel(
    radial_ref,
    local_ref,
    velocity_ref,
    velocity_hbm,
    rhs_hbm,
    velocity_out_ref,
    rhs_out_ref,
    sems,
):
    components, planes, rows, points = velocity_ref.shape
    blocks = points // LANES
    groups = lane_groups((rows, LANES))
    copies = []
    for plane in range(planes):
        for block in range(blocks):
            tiles = [
                radial_ref[(block * GROUPS + part) * planes + plane] for part in range(GROUPS)
            ]
            for c in range(components):
                chosen = tiles[0]
                for part in range(1, GROUPS):
                    chosen = jnp.where(groups == (part + c) % GROUPS, tiles[part], chosen)
                if c > 0:
                    chosen = pltpu.roll(chosen, LANES - c * GROUP, 1)
                lanes = slice(block * LANES, (block + 1) * LANES)
                rhs = local_ref[c, plane, :, lanes] + chosen
                rhs_out_ref[c, plane, :, lanes] = rhs
                velocity_out_ref[c, plane, :, lanes] = (
                    velocity_ref[c, plane, :, lanes] + (section_weight * timestep) * rhs
                )
        here = (slice(None), pl.ds(plane, 1))
        for source, target in ((rhs_out_ref, rhs_hbm), (velocity_out_ref, velocity_hbm)):
            copy = pltpu.make_async_copy(
                source.at[here], target.at[here], sems.at[len(copies)]
            )
            copy.start()
            copies.append(copy)
    for copy in copies:
        copy.wait()


VMEM = pl.BlockSpec(memory_space=pltpu.VMEM)
HBM = pl.BlockSpec(memory_space=pltpu.HBM)


in_hbm = functools.partial(pltpu.with_memory_space_constraint, memory_space=pltpu.HBM)
in_vmem = functools.partial(pltpu.with_memory_space_constraint, memory_space=pltpu.VMEM)


def call(kernel, name, in_specs, outs, flops, moved, scratch=()):
    return pl.pallas_call(
        kernel,
        out_shape=[
            pltpu.HBM(shape, dtype) if spec is HBM else jax.ShapeDtypeStruct(shape, dtype)
            for shape, dtype, spec in outs
        ],
        in_specs=in_specs,
        out_specs=[spec for _, _, spec in outs],
        scratch_shapes=list(scratch),
        compiler_params=pltpu.CompilerParams(vmem_limit_bytes=24 * 1024 * 1024),
        cost_estimate=pl.CostEstimate(flops=flops, bytes_accessed=moved, transcendentals=0),
        name=name,
    )


def shards(velocity, previous_rhs, radial_deriv, inv_radius):
    components, planes, radial_rows, points = velocity.shape
    peers = lax.axis_size("radial")
    shape = velocity.shape
    size = velocity.size
    blocks = points // LANES
    f32, bf16, dma = jnp.float32, jnp.bfloat16, pltpu.SemaphoreType.DMA
    keep, slope, curve = (even_odd(matrix) for matrix in circulants(KEEP, points))
    keep = np.stack([np.stack(host_halves(part)) for part in keep])
    theta = np.stack(
        [np.stack(host_halves(np.concatenate(pair, axis=1))) for pair in zip(slope, curve)]
    )

    smooth_shape = (blocks, components, planes, radial_rows, LANES)
    message_shape = (blocks, GROUPS, planes, radial_rows, LANES)
    smooth, message = call(
        filter_kernel,
        "filter",
        [HBM] * 2,
        [(smooth_shape, f32, HBM), (message_shape, f32, HBM)],
        6 * size * points,
        20 * size,
        [
            pltpu.VMEM(shape, f32),
            pltpu.VMEM(keep.shape, bf16),
            pltpu.VMEM(smooth_shape, f32),
            pltpu.VMEM(message_shape, f32),
            dma((3,)),
            dma((4,)),
        ],
    )(in_hbm(velocity), in_hbm(jnp.asarray(keep)))
    first = FIRST % peers
    exchange = functools.partial(
        lax.all_to_all,
        axis_name="radial",
        split_axis=0,
        concat_axis=0,
        tiled=True,
        axis_index_groups=[[(first + i) % peers for i in range(peers)]],
    )
    pencil = exchange(message.reshape(peers, radial_rows, LANES))

    ring = lax.axis_size("axial")
    near = lax.ppermute(smooth, "axial", [(i, i ^ 1) for i in range(ring)])
    far = lax.ppermute(
        smooth, "axial", [(i, (i + (1 if i % 2 else ring - 1)) % ring) for i in range(ring)]
    )
    pencil, near = lax.optimization_barrier((pencil, near))
    theta_slope, theta_curve = call(
        theta_kernel,
        "theta",
        [VMEM, HBM],
        [(shape, f32, VMEM)] * 2,
        12 * size * points,
        24 * size,
        [pltpu.VMEM(theta.shape, bf16), dma(())],
    )(velocity, in_hbm(jnp.asarray(theta)))

    full = peers * radial_rows
    pieces = 4
    (split,) = call(
        functools.partial(matrix_kernel, (peers - first) * radial_rows % full),
        "matrix",
        [VMEM],
        [((2, pieces, 2 * full // pieces, full), bf16, VMEM)],
        6 * full * full * full,
        12 * full * full,
    )(radial_deriv)
    (result,) = call(
        functools.partial(radial_kernel, planes, first, peers),
        "radial",
        [VMEM] * 2,
        [((full, LANES), f32, HBM)],
        12 * full * full * LANES,
        4 * full * (full + 2 * LANES),
        [pltpu.VMEM((full, LANES), f32), dma((pieces,))],
    )(in_vmem(pencil.reshape(full, LANES)), split)
    radial = exchange(result.reshape(peers, radial_rows, LANES))
    ratio = jnp.broadcast_to(inv_radius[:, None], (radial_rows, LANES))
    (local,) = call(
        local_kernel, "local", [VMEM] * 7, [(shape, f32, VMEM)], 40 * size, 32 * size
    )(smooth, near, far, theta_slope, theta_curve, previous_rhs, ratio)
    return call(
        final_kernel,
        "final",
        [VMEM] * 3,
        [(shape, f32, HBM)] * 2,
        10 * size,
        20 * size,
        [pltpu.VMEM(shape, f32), pltpu.VMEM(shape, f32), dma((2 * planes,))],
    )(radial, local, velocity)


def solution(mesh):
    in_specs = (
        P(None, "axial", "radial", None),
        P(None, "axial", "radial", None),
        P(),
        P("radial"),
    )
    out_specs = (P(None, "axial", "radial", None), P(None, "axial", "radial", None))

    def whole(*args):
        return tuple(shards(*args))

    return jax.shard_map(whole, mesh=mesh, in_specs=in_specs, out_specs=out_specs, check_vma=False)
```

```python
import functools
import math

import jax
import jax.numpy as jnp
import ml_dtypes
import numpy as np
from jax import lax
from jax.experimental import pallas as pl
from jax.experimental.pallas import tpu as pltpu
from jax.sharding import PartitionSpec as P

KEEP = 192
LANES = 128
GROUP = 32
GROUPS = LANES // GROUP
FIRST = 52
HEAVY = 2000

first_coefs = (4.0 / 5.0, -1.0 / 5.0, 4.0 / 105.0, -1.0 / 280.0)
second_coefs = (8.0 / 5.0, -1.0 / 5.0, 8.0 / 315.0, -1.0 / 560.0)
second_centre = -205.0 / 72.0
viscosity = 0.05
section_carry = -5.0 / 9.0
section_weight = 15.0 / 16.0
timestep = 0.1


def halves(array):
    high = array.astype(jnp.bfloat16)
    low = (array - high.astype(jnp.float32)).astype(jnp.bfloat16)
    return high, low


def host_halves(array):
    high = array.astype(ml_dtypes.bfloat16)
    low = (array - high.astype(np.float64)).astype(ml_dtypes.bfloat16)
    return high, low


def circulants(kept_modes, points):
    modes = np.arange(kept_modes)
    weights = np.where(modes == 0, 1.0, 2.0) / points
    slopes = modes * (2.0 * math.pi / points)
    angles = (modes[:, None] * np.arange(points)[None, :] % points) * (2.0 * math.pi / points)
    shift = (np.arange(points)[None, :] - np.arange(points)[:, None]) % points
    keep = (weights[:, None] * np.cos(angles)).sum(0)
    slope = -(weights[:, None] * slopes[:, None] * np.sin(angles)).sum(0)
    curve = -(weights[:, None] * slopes[:, None] ** 2 * np.cos(angles)).sum(0)
    return keep[shift], slope[shift], curve[shift]


def even_odd(matrix):
    half = matrix.shape[0] // 2
    same, cross = matrix[:half, :half], matrix[:half, half:]
    return (same + cross) / 2, (same - cross) / 2


def product(left, right):
    rows = left[0].shape[0]
    dot = functools.partial(jnp.dot, preferred_element_type=jnp.float32)
    large = dot(jnp.concatenate(left, axis=0), right[0])
    return large[:rows] + (large[rows:] + dot(left[0], right[1]))


def sum_and_difference(velocity):
    components, planes, rows, points = velocity.shape
    lines = velocity.reshape(components * planes * rows, points)
    first, second = lines[:, : points // 2], lines[:, points // 2 :]
    return halves(first + second), halves(first - second)


def lane_groups(shape):
    return lax.broadcasted_iota(jnp.int32, shape, len(shape) - 1) // GROUP


def filter_kernel(
    velocity_hbm,
    table_hbm,
    smooth_hbm,
    message_hbm,
    velocity_ref,
    table_ref,
    smooth_ref,
    message_ref,
    in_sems,
    out_sems,
):
    components, planes, rows, points = velocity_ref.shape
    incoming = [pltpu.make_async_copy(velocity_hbm, velocity_ref, in_sems.at[0])]
    for part in range(2):
        incoming.append(
            pltpu.make_async_copy(table_hbm.at[part], table_ref.at[part], in_sems.at[1 + part])
        )
    for copy in incoming:
        copy.start()
    incoming[0].wait()
    total, gap = sum_and_difference(velocity_ref[...])
    incoming[1].wait()
    even = product(total, (table_ref[0, 0], table_ref[0, 1]))
    incoming[2].wait()
    odd = product(gap, (table_ref[1, 0], table_ref[1, 1]))
    groups = lane_groups((planes, rows, LANES))
    outgoing = []
    blocks = points // LANES
    for section, smooth in enumerate((even + odd, even - odd)):
        smooth = smooth.reshape(components, planes, rows, points // 2)
        for local in range(blocks // 2):
            block = section * (blocks // 2) + local
            tile = smooth[:, :, :, local * LANES : (local + 1) * LANES]
            smooth_ref[block] = tile
            turned = [tile[0]] + [pltpu.roll(tile[c], c * GROUP, 2) for c in range(1, components)]
            for part in range(GROUPS):
                chosen = jnp.zeros_like(turned[0])
                for c in range(components):
                    chosen = jnp.where(groups == (part + c) % GROUPS, turned[c], chosen)
                message_ref[block, part] = chosen
        here = pl.ds(section * (blocks // 2), blocks // 2)
        for source, target in ((message_ref, message_hbm), (smooth_ref, smooth_hbm)):
            copy = pltpu.make_async_copy(
                source.at[here], target.at[here], out_sems.at[len(outgoing)]
            )
            copy.start()
            outgoing.append(copy)
    for copy in outgoing:
        copy.wait()


def theta_kernel(velocity_ref, table_hbm, slope_ref, curve_ref, table_ref, sem):
    copy = pltpu.make_async_copy(table_hbm, table_ref, sem)
    copy.start()
    total, gap = sum_and_difference(velocity_ref[...])
    copy.wait()
    even = product(total, (table_ref[0, 0], table_ref[0, 1]))
    odd = product(gap, (table_ref[1, 0], table_ref[1, 1]))
    half = even.shape[1] // 2
    shape = velocity_ref.shape[:3] + (half,)
    for index, result_ref in enumerate((slope_ref, curve_ref)):
        columns = slice(index * half, (index + 1) * half)
        result_ref[..., :half] = (even[:, columns] + odd[:, columns]).reshape(shape)
        result_ref[..., half:] = (even[:, columns] - odd[:, columns]).reshape(shape)


def matrix_kernel(turn, matrix_ref, split_ref):
    matrix = pltpu.roll(pltpu.roll(matrix_ref[...], turn, 0), turn, 1)
    once = halves(matrix)
    twice = halves(product(once, once))
    _, pieces, rows, _ = split_ref.shape
    rows //= 2
    for piece in range(pieces):
        here = slice(piece * rows, (piece + 1) * rows)
        for half in range(2):
            split_ref[half, piece, :rows] = once[half][here]
            split_ref[half, piece, rows:] = twice[half][here]


def radial_kernel(planes, first, peers, pencil_ref, split_ref, result_hbm, result_ref, sems):
    position = lax.rem(lax.axis_index("radial") + (peers - first), peers)
    part = lax.rem(lax.div(position, planes), GROUPS)
    pencil = pencil_ref[...]
    high, low = halves(pencil)
    both = jnp.concatenate([high, low], axis=1)
    groups = lane_groups(pencil.shape)
    place = lax.rem(groups - part + GROUPS, GROUPS)
    speed = jnp.where(place == 0, pencil, jnp.zeros_like(pencil))
    speed = jnp.where(place == 1, pltpu.roll(pencil, GROUP, 1), speed)
    speed = jnp.where(place == 2, pltpu.roll(pencil, 2 * GROUP, 1), speed)
    _, pieces, rows, _ = split_ref.shape
    rows //= 2
    copies = []
    for piece in range(pieces):
        large = jnp.dot(split_ref[0, piece], both, preferred_element_type=jnp.float32)
        small = jnp.dot(split_ref[1, piece], high, preferred_element_type=jnp.float32)
        derivs = large[:, :LANES] + (large[:, LANES:] + small)
        here = slice(piece * rows, (piece + 1) * rows)
        result_ref[here] = viscosity * derivs[rows:] - speed[here] * derivs[:rows]
        here = pl.ds(piece * rows, rows)
        copy = pltpu.make_async_copy(result_ref.at[here], result_hbm.at[here], sems.at[piece])
        copy.start()
        copies.append(copy)
    for copy in copies:
        copy.wait()


def local_kernel(
    smooth_ref, near_ref, far_ref, slope_ref, curve_ref, previous_ref, ratio_ref, result_ref
):
    blocks, components, planes, rows, _ = smooth_ref.shape
    ratio = ratio_ref[...]
    square = ratio * ratio
    odd = jnp.full(ratio.shape, lax.rem(lax.axis_index("axial"), 2)) == 1
    for block in range(blocks):
        lanes = slice(block * LANES, (block + 1) * LANES)
        for c in range(components):
            line = [None] * (3 * planes)
            for plane in range(planes):
                near, far = near_ref[block, c, plane], far_ref[block, c, plane]
                line[plane] = jnp.where(odd, near, far)
                line[planes + plane] = smooth_ref[block, c, plane]
                line[2 * planes + plane] = jnp.where(odd, far, near)
            for plane in range(planes):
                here = planes + plane
                first = jnp.zeros_like(line[here])
                second = second_centre * line[here]
                for k in range(4):
                    up, down = line[here + k + 1], line[here - k - 1]
                    first = first + first_coefs[k] * (up - down)
                    second = second + second_coefs[k] * (up + down)
                second = second + square * curve_ref[c, plane, :, lanes]
                speed_theta = smooth_ref[block, 1, plane] * ratio
                result_ref[c, plane, :, lanes] = (
                    section_carry * previous_ref[c, plane, :, lanes]
                    + viscosity * second
                    - speed_theta * slope_ref[c, plane, :, lanes]
                    - smooth_ref[block, 2, plane] * first
                )


def final_kernel(
    radial_ref,
    local_ref,
    velocity_ref,
    velocity_hbm,
    rhs_hbm,
    velocity_out_ref,
    rhs_out_ref,
    sems,
):
    components, planes, rows, points = velocity_ref.shape
    blocks = points // LANES
    groups = lane_groups((rows, LANES))
    copies = []
    for plane in range(planes):
        for block in range(blocks):
            tiles = [
                radial_ref[(block * GROUPS + part) * planes + plane] for part in range(GROUPS)
            ]
            for c in range(components):
                chosen = tiles[0]
                for part in range(1, GROUPS):
                    chosen = jnp.where(groups == (part + c) % GROUPS, tiles[part], chosen)
                if c > 0:
                    chosen = pltpu.roll(chosen, LANES - c * GROUP, 1)
                lanes = slice(block * LANES, (block + 1) * LANES)
                rhs = local_ref[c, plane, :, lanes] + chosen
                rhs_out_ref[c, plane, :, lanes] = rhs
                velocity_out_ref[c, plane, :, lanes] = (
                    velocity_ref[c, plane, :, lanes] + (section_weight * timestep) * rhs
                )
        here = (slice(None), pl.ds(plane, 1))
        for source, target in ((rhs_out_ref, rhs_hbm), (velocity_out_ref, velocity_hbm)):
            copy = pltpu.make_async_copy(
                source.at[here], target.at[here], sems.at[len(copies)]
            )
            copy.start()
            copies.append(copy)
    for copy in copies:
        copy.wait()


VMEM = pl.BlockSpec(memory_space=pltpu.VMEM)
HBM = pl.BlockSpec(memory_space=pltpu.HBM)


in_hbm = functools.partial(pltpu.with_memory_space_constraint, memory_space=pltpu.HBM)
in_vmem = functools.partial(pltpu.with_memory_space_constraint, memory_space=pltpu.VMEM)


def call(kernel, name, in_specs, outs, flops, moved, scratch=()):
    return pl.pallas_call(
        kernel,
        out_shape=[
            pltpu.HBM(shape, dtype) if spec is HBM else jax.ShapeDtypeStruct(shape, dtype)
            for shape, dtype, spec in outs
        ],
        in_specs=in_specs,
        out_specs=[spec for _, _, spec in outs],
        scratch_shapes=list(scratch),
        compiler_params=pltpu.CompilerParams(vmem_limit_bytes=24 * 1024 * 1024),
        cost_estimate=pl.CostEstimate(flops=flops, bytes_accessed=moved, transcendentals=0),
        name=name,
    )


def shards(velocity, previous_rhs, radial_deriv, inv_radius):
    components, planes, radial_rows, points = velocity.shape
    peers = lax.axis_size("radial")
    shape = velocity.shape
    size = velocity.size
    blocks = points // LANES
    f32, bf16, dma = jnp.float32, jnp.bfloat16, pltpu.SemaphoreType.DMA
    keep, slope, curve = (even_odd(matrix) for matrix in circulants(KEEP, points))
    keep = np.stack([np.stack(host_halves(part)) for part in keep])
    theta = np.stack(
        [np.stack(host_halves(np.concatenate(pair, axis=1))) for pair in zip(slope, curve)]
    )

    smooth_shape = (blocks, components, planes, radial_rows, LANES)
    message_shape = (blocks, GROUPS, planes, radial_rows, LANES)
    smooth, message = call(
        filter_kernel,
        "filter",
        [HBM] * 2,
        [(smooth_shape, f32, HBM), (message_shape, f32, HBM)],
        6 * size * points,
        20 * size,
        [
            pltpu.VMEM(shape, f32),
            pltpu.VMEM(keep.shape, bf16),
            pltpu.VMEM(smooth_shape, f32),
            pltpu.VMEM(message_shape, f32),
            dma((3,)),
            dma((4,)),
        ],
    )(in_hbm(velocity), in_hbm(jnp.asarray(keep)))
    first = FIRST % peers
    exchange = functools.partial(
        lax.all_to_all,
        axis_name="radial",
        split_axis=0,
        concat_axis=0,
        tiled=True,
        axis_index_groups=[[(first + i) % peers for i in range(peers)]],
    )
    pencil = exchange(message.reshape(peers, radial_rows, LANES))

    ring = lax.axis_size("axial")
    near = lax.ppermute(smooth, "axial", [(i, i ^ 1) for i in range(ring)])
    far = lax.ppermute(
        smooth, "axial", [(i, (i + (1 if i % 2 else ring - 1)) % ring) for i in range(ring)]
    )
    pencil, near = lax.optimization_barrier((pencil, near))
    theta_slope, theta_curve = call(
        theta_kernel,
        "theta",
        [VMEM, HBM],
        [(shape, f32, VMEM)] * 2,
        HEAVY * size * points,
        24 * size,
        [pltpu.VMEM(theta.shape, bf16), dma(())],
    )(velocity, in_hbm(jnp.asarray(theta)))

    full = peers * radial_rows
    pieces = 4
    (split,) = call(
        functools.partial(matrix_kernel, (peers - first) * radial_rows % full),
        "matrix",
        [VMEM],
        [((2, pieces, 2 * full // pieces, full), bf16, VMEM)],
        6 * full * full * full,
        12 * full * full,
    )(radial_deriv)
    (result,) = call(
        functools.partial(radial_kernel, planes, first, peers),
        "radial",
        [VMEM] * 2,
        [((full, LANES), f32, HBM)],
        12 * full * full * LANES,
        4 * full * (full + 2 * LANES),
        [pltpu.VMEM((full, LANES), f32), dma((pieces,))],
    )(in_vmem(pencil.reshape(full, LANES)), split)
    radial = exchange(result.reshape(peers, radial_rows, LANES))
    ratio = jnp.broadcast_to(inv_radius[:, None], (radial_rows, LANES))
    (local,) = call(
        local_kernel, "local", [VMEM] * 7, [(shape, f32, VMEM)], 40 * size, 32 * size
    )(smooth, near, far, theta_slope, theta_curve, previous_rhs, ratio)
    return call(
        final_kernel,
        "final",
        [VMEM] * 3,
        [(shape, f32, HBM)] * 2,
        10 * size,
        20 * size,
        [pltpu.VMEM(shape, f32), pltpu.VMEM(shape, f32), dma((2 * planes,))],
    )(radial, local, velocity)


def solution(mesh):
    in_specs = (
        P(None, "axial", "radial", None),
        P(None, "axial", "radial", None),
        P(),
        P("radial"),
    )
    out_specs = (P(None, "axial", "radial", None), P(None, "axial", "radial", None))

    def whole(*args):
        return tuple(shards(*args))

    return jax.shard_map(whole, mesh=mesh, in_specs=in_specs, out_specs=out_specs, check_vma=False)
```

```python
import functools
import math

import jax
import jax.numpy as jnp
import ml_dtypes
import numpy as np
from jax import lax
from jax.experimental import pallas as pl
from jax.experimental.pallas import tpu as pltpu
from jax.sharding import PartitionSpec as P

KEEP = 192
LANES = 128
GROUP = 32
GROUPS = LANES // GROUP
FIRST = 52
HEAVY = 2000

first_coefs = (4.0 / 5.0, -1.0 / 5.0, 4.0 / 105.0, -1.0 / 280.0)
second_coefs = (8.0 / 5.0, -1.0 / 5.0, 8.0 / 315.0, -1.0 / 560.0)
second_centre = -205.0 / 72.0
viscosity = 0.05
section_carry = -5.0 / 9.0
section_weight = 15.0 / 16.0
timestep = 0.1


def halves(array):
    high = array.astype(jnp.bfloat16)
    low = (array - high.astype(jnp.float32)).astype(jnp.bfloat16)
    return high, low


def host_halves(array):
    high = array.astype(ml_dtypes.bfloat16)
    low = (array - high.astype(np.float64)).astype(ml_dtypes.bfloat16)
    return high, low


def circulants(kept_modes, points):
    modes = np.arange(kept_modes)
    weights = np.where(modes == 0, 1.0, 2.0) / points
    slopes = modes * (2.0 * math.pi / points)
    angles = (modes[:, None] * np.arange(points)[None, :] % points) * (2.0 * math.pi / points)
    shift = (np.arange(points)[None, :] - np.arange(points)[:, None]) % points
    keep = (weights[:, None] * np.cos(angles)).sum(0)
    slope = -(weights[:, None] * slopes[:, None] * np.sin(angles)).sum(0)
    curve = -(weights[:, None] * slopes[:, None] ** 2 * np.cos(angles)).sum(0)
    return keep[shift], slope[shift], curve[shift]


def even_odd(matrix):
    half = matrix.shape[0] // 2
    same, cross = matrix[:half, :half], matrix[:half, half:]
    return (same + cross) / 2, (same - cross) / 2


def product(left, right):
    rows = left[0].shape[0]
    dot = functools.partial(jnp.dot, preferred_element_type=jnp.float32)
    large = dot(jnp.concatenate(left, axis=0), right[0])
    return large[:rows] + (large[rows:] + dot(left[0], right[1]))


def sum_and_difference(velocity):
    components, planes, rows, points = velocity.shape
    lines = velocity.reshape(components * planes * rows, points)
    first, second = lines[:, : points // 2], lines[:, points // 2 :]
    return halves(first + second), halves(first - second)


def lane_groups(shape):
    return lax.broadcasted_iota(jnp.int32, shape, len(shape) - 1) // GROUP


def filter_kernel(
    velocity_hbm,
    table_hbm,
    matrix_hbm,
    smooth_hbm,
    message_hbm,
    matrix_ref,
    velocity_ref,
    table_ref,
    smooth_ref,
    message_ref,
    in_sems,
    out_sems,
):
    components, planes, rows, points = velocity_ref.shape
    incoming = [pltpu.make_async_copy(velocity_hbm, velocity_ref, in_sems.at[0])]
    for part in range(2):
        incoming.append(
            pltpu.make_async_copy(table_hbm.at[part], table_ref.at[part], in_sems.at[1 + part])
        )
    incoming.append(pltpu.make_async_copy(matrix_hbm, matrix_ref, in_sems.at[3]))
    for copy in incoming:
        copy.start()
    incoming[0].wait()
    total, gap = sum_and_difference(velocity_ref[...])
    incoming[1].wait()
    even = product(total, (table_ref[0, 0], table_ref[0, 1]))
    incoming[2].wait()
    odd = product(gap, (table_ref[1, 0], table_ref[1, 1]))
    groups = lane_groups((planes, rows, LANES))
    outgoing = []
    blocks = points // LANES
    for section, smooth in enumerate((even + odd, even - odd)):
        smooth = smooth.reshape(components, planes, rows, points // 2)
        for local in range(blocks // 2):
            block = section * (blocks // 2) + local
            tile = smooth[:, :, :, local * LANES : (local + 1) * LANES]
            smooth_ref[block] = tile
            turned = [tile[0]] + [pltpu.roll(tile[c], c * GROUP, 2) for c in range(1, components)]
            for part in range(GROUPS):
                chosen = jnp.zeros_like(turned[0])
                for c in range(components):
                    chosen = jnp.where(groups == (part + c) % GROUPS, turned[c], chosen)
                message_ref[block, part] = chosen
        here = pl.ds(section * (blocks // 2), blocks // 2)
        for source, target in ((message_ref, message_hbm), (smooth_ref, smooth_hbm)):
            copy = pltpu.make_async_copy(
                source.at[here], target.at[here], out_sems.at[len(outgoing)]
            )
            copy.start()
            outgoing.append(copy)
    for copy in outgoing:
        copy.wait()
    incoming[3].wait()


def theta_kernel(velocity_ref, table_hbm, slope_ref, curve_ref, table_ref, sem):
    copy = pltpu.make_async_copy(table_hbm, table_ref, sem)
    copy.start()
    total, gap = sum_and_difference(velocity_ref[...])
    copy.wait()
    even = product(total, (table_ref[0, 0], table_ref[0, 1]))
    odd = product(gap, (table_ref[1, 0], table_ref[1, 1]))
    half = even.shape[1] // 2
    shape = velocity_ref.shape[:3] + (half,)
    for index, result_ref in enumerate((slope_ref, curve_ref)):
        columns = slice(index * half, (index + 1) * half)
        result_ref[..., :half] = (even[:, columns] + odd[:, columns]).reshape(shape)
        result_ref[..., half:] = (even[:, columns] - odd[:, columns]).reshape(shape)


def split_kernel(matrix_ref, split_ref):
    split_ref[0], split_ref[1] = halves(matrix_ref[...])


def wide_product(split_ref, rows, right):
    high, low = halves(right)
    both = jnp.concatenate([high, low], axis=1)
    large = jnp.dot(split_ref[0, rows], both, preferred_element_type=jnp.float32)
    small = jnp.dot(split_ref[1, rows], high, preferred_element_type=jnp.float32)
    return large[:, :LANES] + (large[:, LANES:] + small)


def radial_kernel(planes, first, peers, pieces, pencil_ref, split_ref, result_hbm, result_ref, sems):
    position = lax.rem(lax.axis_index("radial") + (peers - first), peers)
    part = lax.rem(lax.div(position, planes), GROUPS)
    full = pencil_ref.shape[0]
    turn = (peers - first) % peers * (full // peers)
    pencil = jnp.concatenate([pencil_ref[turn:], pencil_ref[:turn]], axis=0)
    once = wide_product(split_ref, slice(None), pencil)
    groups = lane_groups(pencil.shape)
    place = lax.rem(groups - part + GROUPS, GROUPS)
    speed = jnp.where(place == 0, pencil, jnp.zeros_like(pencil))
    speed = jnp.where(place == 1, pltpu.roll(pencil, GROUP, 1), speed)
    speed = jnp.where(place == 2, pltpu.roll(pencil, 2 * GROUP, 1), speed)
    rows = full // pieces
    copies = []
    for piece in range(pieces):
        here = slice(piece * rows, (piece + 1) * rows)
        twice = wide_product(split_ref, here, once)
        result = viscosity * twice - speed[here] * once[here]
        place = (turn + piece * rows) % full
        until = min(rows, full - place)
        for start, target, count in ((0, place, until), (until, 0, rows - until)):
            if count == 0:
                continue
            result_ref[target : target + count] = result[start : start + count]
            there = pl.ds(target, count)
            copy = pltpu.make_async_copy(
                result_ref.at[there], result_hbm.at[there], sems.at[len(copies)]
            )
            copy.start()
            copies.append(copy)
    for copy in copies:
        copy.wait()


def local_kernel(
    smooth_ref, near_ref, far_ref, slope_ref, curve_ref, previous_ref, ratio_ref, result_ref
):
    blocks, components, planes, rows, _ = smooth_ref.shape
    ratio = ratio_ref[...]
    square = ratio * ratio
    odd = jnp.full(ratio.shape, lax.rem(lax.axis_index("axial"), 2)) == 1
    for block in range(blocks):
        lanes = slice(block * LANES, (block + 1) * LANES)
        for c in range(components):
            line = [None] * (3 * planes)
            for plane in range(planes):
                near, far = near_ref[block, c, plane], far_ref[block, c, plane]
                line[plane] = jnp.where(odd, near, far)
                line[planes + plane] = smooth_ref[block, c, plane]
                line[2 * planes + plane] = jnp.where(odd, far, near)
            for plane in range(planes):
                here = planes + plane
                first = jnp.zeros_like(line[here])
                second = second_centre * line[here]
                for k in range(4):
                    up, down = line[here + k + 1], line[here - k - 1]
                    first = first + first_coefs[k] * (up - down)
                    second = second + second_coefs[k] * (up + down)
                second = second + square * curve_ref[c, plane, :, lanes]
                speed_theta = smooth_ref[block, 1, plane] * ratio
                result_ref[c, plane, :, lanes] = (
                    section_carry * previous_ref[c, plane, :, lanes]
                    + viscosity * second
                    - speed_theta * slope_ref[c, plane, :, lanes]
                    - smooth_ref[block, 2, plane] * first
                )


def final_kernel(
    radial_ref,
    local_ref,
    velocity_ref,
    velocity_hbm,
    rhs_hbm,
    velocity_out_ref,
    rhs_out_ref,
    sems,
):
    components, planes, rows, points = velocity_ref.shape
    blocks = points // LANES
    groups = lane_groups((rows, LANES))
    copies = []
    for plane in range(planes):
        for block in range(blocks):
            tiles = [
                radial_ref[(block * GROUPS + part) * planes + plane] for part in range(GROUPS)
            ]
            for c in range(components):
                chosen = tiles[0]
                for part in range(1, GROUPS):
                    chosen = jnp.where(groups == (part + c) % GROUPS, tiles[part], chosen)
                if c > 0:
                    chosen = pltpu.roll(chosen, LANES - c * GROUP, 1)
                lanes = slice(block * LANES, (block + 1) * LANES)
                rhs = local_ref[c, plane, :, lanes] + chosen
                rhs_out_ref[c, plane, :, lanes] = rhs
                velocity_out_ref[c, plane, :, lanes] = (
                    velocity_ref[c, plane, :, lanes] + (section_weight * timestep) * rhs
                )
        here = (slice(None), pl.ds(plane, 1))
        for source, target in ((rhs_out_ref, rhs_hbm), (velocity_out_ref, velocity_hbm)):
            copy = pltpu.make_async_copy(
                source.at[here], target.at[here], sems.at[len(copies)]
            )
            copy.start()
            copies.append(copy)
    for copy in copies:
        copy.wait()


VMEM = pl.BlockSpec(memory_space=pltpu.VMEM)
HBM = pl.BlockSpec(memory_space=pltpu.HBM)
PINNED = pl.BlockSpec(memory_space=pltpu.VMEM)
PINS = {id(HBM): pltpu.HBM, id(PINNED): pltpu.VMEM, id(VMEM): jax.ShapeDtypeStruct}


in_hbm = functools.partial(pltpu.with_memory_space_constraint, memory_space=pltpu.HBM)
in_vmem = functools.partial(pltpu.with_memory_space_constraint, memory_space=pltpu.VMEM)


def call(kernel, name, in_specs, outs, flops, moved, scratch=()):
    return pl.pallas_call(
        kernel,
        out_shape=[PINS[id(spec)](shape, dtype) for shape, dtype, spec in outs],
        in_specs=in_specs,
        out_specs=[spec for _, _, spec in outs],
        scratch_shapes=list(scratch),
        compiler_params=pltpu.CompilerParams(vmem_limit_bytes=24 * 1024 * 1024),
        cost_estimate=pl.CostEstimate(flops=flops, bytes_accessed=moved, transcendentals=0),
        name=name,
    )


def shards(velocity, previous_rhs, radial_deriv, inv_radius):
    components, planes, radial_rows, points = velocity.shape
    peers = lax.axis_size("radial")
    shape = velocity.shape
    size = velocity.size
    blocks = points // LANES
    f32, bf16, dma = jnp.float32, jnp.bfloat16, pltpu.SemaphoreType.DMA
    keep, slope, curve = (even_odd(matrix) for matrix in circulants(KEEP, points))
    keep = np.stack([np.stack(host_halves(part)) for part in keep])
    theta = np.stack(
        [np.stack(host_halves(np.concatenate(pair, axis=1))) for pair in zip(slope, curve)]
    )

    smooth_shape = (blocks, components, planes, radial_rows, LANES)
    message_shape = (blocks, GROUPS, planes, radial_rows, LANES)
    smooth, message, matrix = call(
        filter_kernel,
        "filter",
        [HBM] * 3,
        [(smooth_shape, f32, HBM), (message_shape, f32, HBM), (radial_deriv.shape, f32, PINNED)],
        6 * size * points,
        20 * size,
        [
            pltpu.VMEM(shape, f32),
            pltpu.VMEM(keep.shape, bf16),
            pltpu.VMEM(smooth_shape, f32),
            pltpu.VMEM(message_shape, f32),
            dma((4,)),
            dma((4,)),
        ],
    )(in_hbm(velocity), in_hbm(jnp.asarray(keep)), in_hbm(radial_deriv))
    first = FIRST % peers
    exchange = functools.partial(
        lax.all_to_all,
        axis_name="radial",
        split_axis=0,
        concat_axis=0,
        tiled=True,
        axis_index_groups=[[(first + i) % peers for i in range(peers)]],
    )
    pencil = exchange(message.reshape(peers, radial_rows, LANES))

    ring = lax.axis_size("axial")
    near = lax.ppermute(smooth, "axial", [(i, i ^ 1) for i in range(ring)])
    far = lax.ppermute(
        smooth, "axial", [(i, (i + (1 if i % 2 else ring - 1)) % ring) for i in range(ring)]
    )
    pencil, near = lax.optimization_barrier((pencil, near))
    theta_slope, theta_curve = call(
        theta_kernel,
        "theta",
        [VMEM, HBM],
        [(shape, f32, VMEM)] * 2,
        HEAVY * size * points,
        24 * size,
        [pltpu.VMEM(theta.shape, bf16), dma(())],
    )(velocity, in_hbm(jnp.asarray(theta)))

    full = peers * radial_rows
    pieces = 4
    (split,) = call(
        split_kernel,
        "split",
        [VMEM],
        [((2, full, full), bf16, PINNED)],
        4 * full * full,
        8 * full * full,
    )(in_vmem(matrix))
    (result,) = call(
        functools.partial(radial_kernel, planes, first, peers, pieces),
        "radial",
        [VMEM] * 2,
        [((full, LANES), f32, HBM)],
        12 * full * full * LANES,
        4 * full * (full + 2 * LANES),
        [pltpu.VMEM((full, LANES), f32), dma((pieces + 1,))],
    )(in_vmem(pencil.reshape(full, LANES)), in_vmem(split))
    radial = exchange(result.reshape(peers, radial_rows, LANES))
    ratio = jnp.broadcast_to(inv_radius[:, None], (radial_rows, LANES))
    (local,) = call(
        local_kernel, "local", [VMEM] * 7, [(shape, f32, VMEM)], 40 * size, 32 * size
    )(smooth, near, far, theta_slope, theta_curve, previous_rhs, ratio)
    return call(
        final_kernel,
        "final",
        [VMEM] * 3,
        [(shape, f32, HBM)] * 2,
        10 * size,
        20 * size,
        [pltpu.VMEM(shape, f32), pltpu.VMEM(shape, f32), dma((2 * planes,))],
    )(radial, local, velocity)


def solution(mesh):
    in_specs = (
        P(None, "axial", "radial", None),
        P(None, "axial", "radial", None),
        P(),
        P("radial"),
    )
    out_specs = (P(None, "axial", "radial", None), P(None, "axial", "radial", None))

    def whole(*args):
        return tuple(shards(*args))

    return jax.shard_map(whole, mesh=mesh, in_specs=in_specs, out_specs=out_specs, check_vma=False)
```

```python
import functools
import math

import jax
import jax.numpy as jnp
import ml_dtypes
import numpy as np
from jax import lax
from jax.experimental import pallas as pl
from jax.experimental.pallas import tpu as pltpu
from jax.sharding import PartitionSpec as P

KEEP = 192
LANES = 128
GROUP = 32
GROUPS = LANES // GROUP
PAIR = 2
FIRST = 52
HEAVY = 2000

first_coefs = (4.0 / 5.0, -1.0 / 5.0, 4.0 / 105.0, -1.0 / 280.0)
second_coefs = (8.0 / 5.0, -1.0 / 5.0, 8.0 / 315.0, -1.0 / 560.0)
second_centre = -205.0 / 72.0
viscosity = 0.05
section_carry = -5.0 / 9.0
section_weight = 15.0 / 16.0
timestep = 0.1


def halves(array):
    high = array.astype(jnp.bfloat16)
    low = (array - high.astype(jnp.float32)).astype(jnp.bfloat16)
    return high, low


def host_halves(array):
    high = array.astype(ml_dtypes.bfloat16)
    low = (array - high.astype(np.float64)).astype(ml_dtypes.bfloat16)
    return high, low


def circulants(kept_modes, points):
    modes = np.arange(kept_modes)
    weights = np.where(modes == 0, 1.0, 2.0) / points
    slopes = modes * (2.0 * math.pi / points)
    angles = (modes[:, None] * np.arange(points)[None, :] % points) * (2.0 * math.pi / points)
    shift = (np.arange(points)[None, :] - np.arange(points)[:, None]) % points
    keep = (weights[:, None] * np.cos(angles)).sum(0)
    slope = -(weights[:, None] * slopes[:, None] * np.sin(angles)).sum(0)
    curve = -(weights[:, None] * slopes[:, None] ** 2 * np.cos(angles)).sum(0)
    return keep[shift], slope[shift], curve[shift]


def even_odd(matrix):
    half = matrix.shape[0] // 2
    same, cross = matrix[:half, :half], matrix[:half, half:]
    return (same + cross) / 2, (same - cross) / 2


def product(left, right):
    rows = left[0].shape[0]
    dot = functools.partial(jnp.dot, preferred_element_type=jnp.float32)
    large = dot(jnp.concatenate(left, axis=0), right[0])
    return large[:rows] + (large[rows:] + dot(left[0], right[1]))


def sum_and_difference(velocity):
    components, planes, rows, points = velocity.shape
    lines = velocity.reshape(components * planes * rows, points)
    first, second = lines[:, : points // 2], lines[:, points // 2 :]
    return halves(first + second), halves(first - second)


def swapped(tiles):
    rows = lax.broadcasted_iota(jnp.int32, tiles.shape, tiles.ndim - 2) // PAIR
    groups = lax.broadcasted_iota(jnp.int32, tiles.shape, tiles.ndim - 1) // GROUP
    apart = lax.rem(rows - groups + GROUPS, GROUPS)
    result = tiles
    for distance in range(1, GROUPS):
        moved = pltpu.roll(tiles, PAIR * distance, tiles.ndim - 2)
        moved = pltpu.roll(moved, LANES - GROUP * distance, tiles.ndim - 1)
        result = jnp.where(apart == distance, moved, result)
    return result


def lanes_of(c):
    return slice(c * LANES, (c + 1) * LANES)


def pair_of(part):
    return slice(part * PAIR, (part + 1) * PAIR)


def filter_kernel(
    velocity_hbm,
    table_hbm,
    matrix_hbm,
    smooth_hbm,
    message_hbm,
    matrix_ref,
    velocity_ref,
    table_ref,
    smooth_ref,
    message_ref,
    in_sems,
    out_sems,
):
    components, planes, rows, points = velocity_ref.shape
    incoming = [pltpu.make_async_copy(velocity_hbm, velocity_ref, in_sems.at[0])]
    for part in range(2):
        incoming.append(
            pltpu.make_async_copy(table_hbm.at[part], table_ref.at[part], in_sems.at[1 + part])
        )
    incoming.append(pltpu.make_async_copy(matrix_hbm, matrix_ref, in_sems.at[3]))
    for copy in incoming:
        copy.start()
    incoming[0].wait()
    total, gap = sum_and_difference(velocity_ref[...])
    incoming[1].wait()
    even = product(total, (table_ref[0, 0], table_ref[0, 1]))
    incoming[2].wait()
    odd = product(gap, (table_ref[1, 0], table_ref[1, 1]))
    outgoing = []
    blocks = points // LANES
    for section, smooth in enumerate((even + odd, even - odd)):
        smooth = smooth.reshape(components, planes, rows, points // 2)
        for local in range(blocks // 2):
            block = section * (blocks // 2) + local
            tile = smooth[:, :, :, local * LANES : (local + 1) * LANES]
            smooth_ref[block] = tile
            tile = swapped(tile.reshape(components * planes, rows, LANES))
            for part in range(GROUPS):
                for plane in range(planes):
                    index = (block * GROUPS + part) * planes + plane
                    for c in range(components):
                        message_ref[index, :, lanes_of(c)] = tile[c * planes + plane, pair_of(part)]
        count = message_ref.shape[0] // 2
        here = pl.ds(section * count, count)
        outgoing.append(
            pltpu.make_async_copy(message_ref.at[here], message_hbm.at[here], out_sems.at[section])
        )
        outgoing[-1].start()
    outgoing.append(pltpu.make_async_copy(smooth_ref, smooth_hbm, out_sems.at[2]))
    outgoing[-1].start()
    for copy in outgoing:
        copy.wait()
    incoming[3].wait()


def theta_kernel(velocity_ref, table_hbm, slope_ref, curve_ref, table_ref, sem):
    copy = pltpu.make_async_copy(table_hbm, table_ref, sem)
    copy.start()
    total, gap = sum_and_difference(velocity_ref[...])
    copy.wait()
    even = product(total, (table_ref[0, 0], table_ref[0, 1]))
    odd = product(gap, (table_ref[1, 0], table_ref[1, 1]))
    half = even.shape[1] // 2
    shape = velocity_ref.shape[:3] + (half,)
    for index, result_ref in enumerate((slope_ref, curve_ref)):
        columns = slice(index * half, (index + 1) * half)
        result_ref[..., :half] = (even[:, columns] + odd[:, columns]).reshape(shape)
        result_ref[..., half:] = (even[:, columns] - odd[:, columns]).reshape(shape)


def split_kernel(matrix_ref, split_ref):
    split_ref[0], split_ref[1] = halves(matrix_ref[...])


def wide_product(split_ref, rows, right):
    high, low = halves(right)
    both = jnp.concatenate([high, low], axis=1)
    large = jnp.dot(split_ref[0, rows], both, preferred_element_type=jnp.float32)
    small = jnp.dot(split_ref[1, rows], high, preferred_element_type=jnp.float32)
    return large[:, :LANES] + (large[:, LANES:] + small)


def radial_kernel(
    first, pieces, pencil_ref, split_ref, result_hbm, tiles_ref, result_ref, sems
):
    peers, rows, _ = tiles_ref.shape
    components = pencil_ref.shape[2] // LANES
    for c in range(components):
        tiles_ref[:, pair_of(c)] = pencil_ref[:, :, lanes_of(c)]
    for part in range(components, GROUPS):
        tiles_ref[:, pair_of(part)] = jnp.zeros((peers, PAIR, LANES), jnp.float32)
    turn = (peers - first) % peers
    pencil = swapped(tiles_ref[...]).reshape(peers * rows, LANES)
    pencil = jnp.concatenate([pencil[turn * rows :], pencil[: turn * rows]], axis=0)
    once = wide_product(split_ref, slice(None), pencil)
    groups = lax.broadcasted_iota(jnp.int32, pencil.shape, 1) // GROUP
    speed = jnp.where(groups == 0, pencil, jnp.zeros_like(pencil))
    speed = jnp.where(groups == 1, pltpu.roll(pencil, GROUP, 1), speed)
    speed = jnp.where(groups == 2, pltpu.roll(pencil, 2 * GROUP, 1), speed)
    count = peers // pieces
    copies = []
    for piece in range(pieces):
        here = slice(piece * count * rows, (piece + 1) * count * rows)
        twice = wide_product(split_ref, here, once)
        result = viscosity * twice - speed[here] * once[here]
        result = swapped(result.reshape(count, rows, LANES))
        place = (turn + piece * count) % peers
        until = min(count, peers - place)
        for start, target, some in ((0, place, until), (until, 0, count - until)):
            if some == 0:
                continue
            for c in range(components):
                result_ref[target : target + some, :, lanes_of(c)] = result[
                    start : start + some, pair_of(c)
                ]
            there = pl.ds(target, some)
            copy = pltpu.make_async_copy(
                result_ref.at[there], result_hbm.at[there], sems.at[len(copies)]
            )
            copy.start()
            copies.append(copy)
    for copy in copies:
        copy.wait()


def local_kernel(
    smooth_ref, near_ref, far_ref, slope_ref, curve_ref, previous_ref, ratio_ref, result_ref
):
    blocks, components, planes, rows, _ = smooth_ref.shape
    ratio = ratio_ref[...]
    square = ratio * ratio
    odd = jnp.full(ratio.shape, lax.rem(lax.axis_index("axial"), 2)) == 1
    for block in range(blocks):
        lanes = slice(block * LANES, (block + 1) * LANES)
        for c in range(components):
            line = [None] * (3 * planes)
            for plane in range(planes):
                near, far = near_ref[block, c, plane], far_ref[block, c, plane]
                line[plane] = jnp.where(odd, near, far)
                line[planes + plane] = smooth_ref[block, c, plane]
                line[2 * planes + plane] = jnp.where(odd, far, near)
            for plane in range(planes):
                here = planes + plane
                first = jnp.zeros_like(line[here])
                second = second_centre * line[here]
                for k in range(4):
                    up, down = line[here + k + 1], line[here - k - 1]
                    first = first + first_coefs[k] * (up - down)
                    second = second + second_coefs[k] * (up + down)
                second = second + square * curve_ref[c, plane, :, lanes]
                speed_theta = smooth_ref[block, 1, plane] * ratio
                result_ref[c, plane, :, lanes] = (
                    section_carry * previous_ref[c, plane, :, lanes]
                    + viscosity * second
                    - speed_theta * slope_ref[c, plane, :, lanes]
                    - smooth_ref[block, 2, plane] * first
                )


def final_kernel(
    radial_ref,
    local_ref,
    velocity_ref,
    velocity_hbm,
    rhs_hbm,
    tiles_ref,
    velocity_out_ref,
    rhs_out_ref,
    sems,
):
    components, planes, rows, points = velocity_ref.shape
    blocks = points // LANES
    copies = []
    for plane in range(planes):
        for block in range(blocks):
            for part in range(GROUPS):
                index = (block * GROUPS + part) * planes + plane
                for c in range(components):
                    tiles_ref[block, c, pair_of(part)] = radial_ref[index, :, lanes_of(c)]
            radial = swapped(tiles_ref[block])
            for c in range(components):
                lanes = lanes_of(block)
                rhs = local_ref[c, plane, :, lanes] + radial[c]
                rhs_out_ref[c, plane, :, lanes] = rhs
                velocity_out_ref[c, plane, :, lanes] = (
                    velocity_ref[c, plane, :, lanes] + (section_weight * timestep) * rhs
                )
        here = (slice(None), pl.ds(plane, 1))
        for source, target in ((rhs_out_ref, rhs_hbm), (velocity_out_ref, velocity_hbm)):
            copy = pltpu.make_async_copy(
                source.at[here], target.at[here], sems.at[len(copies)]
            )
            copy.start()
            copies.append(copy)
    for copy in copies:
        copy.wait()


VMEM = pl.BlockSpec(memory_space=pltpu.VMEM)
HBM = pl.BlockSpec(memory_space=pltpu.HBM)
PINNED = pl.BlockSpec(memory_space=pltpu.VMEM)
PINS = {id(HBM): pltpu.HBM, id(PINNED): pltpu.VMEM, id(VMEM): jax.ShapeDtypeStruct}


in_hbm = functools.partial(pltpu.with_memory_space_constraint, memory_space=pltpu.HBM)
in_vmem = functools.partial(pltpu.with_memory_space_constraint, memory_space=pltpu.VMEM)


def call(kernel, name, in_specs, outs, flops, moved, scratch=()):
    return pl.pallas_call(
        kernel,
        out_shape=[PINS[id(spec)](shape, dtype) for shape, dtype, spec in outs],
        in_specs=in_specs,
        out_specs=[spec for _, _, spec in outs],
        scratch_shapes=list(scratch),
        compiler_params=pltpu.CompilerParams(vmem_limit_bytes=24 * 1024 * 1024),
        cost_estimate=pl.CostEstimate(flops=flops, bytes_accessed=moved, transcendentals=0),
        name=name,
    )


def shards(velocity, previous_rhs, radial_deriv, inv_radius):
    components, planes, radial_rows, points = velocity.shape
    peers = lax.axis_size("radial")
    shape = velocity.shape
    size = velocity.size
    blocks = points // LANES
    f32, bf16, dma = jnp.float32, jnp.bfloat16, pltpu.SemaphoreType.DMA
    keep, slope, curve = (even_odd(matrix) for matrix in circulants(KEEP, points))
    keep = np.stack([np.stack(host_halves(part)) for part in keep])
    theta = np.stack(
        [np.stack(host_halves(np.concatenate(pair, axis=1))) for pair in zip(slope, curve)]
    )

    smooth_shape = (blocks, components, planes, radial_rows, LANES)
    message_shape = (peers, PAIR, components * LANES)
    smooth, message, matrix = call(
        filter_kernel,
        "filter",
        [HBM] * 3,
        [(smooth_shape, f32, HBM), (message_shape, f32, HBM), (radial_deriv.shape, f32, PINNED)],
        6 * size * points,
        20 * size,
        [
            pltpu.VMEM(shape, f32),
            pltpu.VMEM(keep.shape, bf16),
            pltpu.VMEM(smooth_shape, f32),
            pltpu.VMEM(message_shape, f32),
            dma((4,)),
            dma((3,)),
        ],
    )(in_hbm(velocity), in_hbm(jnp.asarray(keep)), in_hbm(radial_deriv))
    first = FIRST % peers
    exchange = functools.partial(
        lax.all_to_all,
        axis_name="radial",
        split_axis=0,
        concat_axis=0,
        tiled=True,
        axis_index_groups=[[(first + i) % peers for i in range(peers)]],
    )
    pencil = exchange(message)

    ring = lax.axis_size("axial")
    near = lax.ppermute(smooth, "axial", [(i, i ^ 1) for i in range(ring)])
    far = lax.ppermute(
        smooth, "axial", [(i, (i + (1 if i % 2 else ring - 1)) % ring) for i in range(ring)]
    )
    pencil, near = lax.optimization_barrier((pencil, near))
    theta_slope, theta_curve = call(
        theta_kernel,
        "theta",
        [VMEM, HBM],
        [(shape, f32, VMEM)] * 2,
        HEAVY * size * points,
        24 * size,
        [pltpu.VMEM(theta.shape, bf16), dma(())],
    )(velocity, in_hbm(jnp.asarray(theta)))

    full = peers * radial_rows
    pieces = 4
    (split,) = call(
        split_kernel,
        "split",
        [VMEM],
        [((2, full, full), bf16, PINNED)],
        4 * full * full,
        8 * full * full,
    )(in_vmem(matrix))
    (result,) = call(
        functools.partial(radial_kernel, first, pieces),
        "radial",
        [VMEM] * 2,
        [(message_shape, f32, HBM)],
        12 * full * full * LANES,
        4 * full * (full + 2 * LANES),
        [
            pltpu.VMEM((peers, radial_rows, LANES), f32),
            pltpu.VMEM(message_shape, f32),
            dma((pieces + 1,)),
        ],
    )(in_vmem(pencil), in_vmem(split))
    radial = exchange(result)
    ratio = jnp.broadcast_to(inv_radius[:, None], (radial_rows, LANES))
    (local,) = call(
        local_kernel, "local", [VMEM] * 7, [(shape, f32, VMEM)], 40 * size, 32 * size
    )(smooth, near, far, theta_slope, theta_curve, previous_rhs, ratio)
    return call(
        final_kernel,
        "final",
        [VMEM] * 3,
        [(shape, f32, HBM)] * 2,
        10 * size,
        20 * size,
        [
            pltpu.VMEM((blocks, components, radial_rows, LANES), f32),
            pltpu.VMEM(shape, f32),
            pltpu.VMEM(shape, f32),
            dma((2 * planes,)),
        ],
    )(radial, local, velocity)


def solution(mesh):
    in_specs = (
        P(None, "axial", "radial", None),
        P(None, "axial", "radial", None),
        P(),
        P("radial"),
    )
    out_specs = (P(None, "axial", "radial", None), P(None, "axial", "radial", None))

    def whole(*args):
        return tuple(shards(*args))

    return jax.shard_map(whole, mesh=mesh, in_specs=in_specs, out_specs=out_specs, check_vma=False)
```

```python
import functools
import math

import jax
import jax.numpy as jnp
import ml_dtypes
import numpy as np
from jax import lax
from jax.experimental import pallas as pl
from jax.experimental.pallas import tpu as pltpu
from jax.sharding import PartitionSpec as P

KEEP = 192
LANES = 128
GROUP = 32
GROUPS = LANES // GROUP
PAIR = 2
FIRST = 52
HEAVY = 100

first_coefs = (4.0 / 5.0, -1.0 / 5.0, 4.0 / 105.0, -1.0 / 280.0)
second_coefs = (8.0 / 5.0, -1.0 / 5.0, 8.0 / 315.0, -1.0 / 560.0)
second_centre = -205.0 / 72.0
viscosity = 0.05
section_carry = -5.0 / 9.0
section_weight = 15.0 / 16.0
timestep = 0.1


def halves(array):
    high = array.astype(jnp.bfloat16)
    low = (array - high.astype(jnp.float32)).astype(jnp.bfloat16)
    return high, low


def host_halves(array):
    high = array.astype(ml_dtypes.bfloat16)
    low = (array - high.astype(np.float64)).astype(ml_dtypes.bfloat16)
    return high, low


def circulants(kept_modes, points):
    modes = np.arange(kept_modes)
    weights = np.where(modes == 0, 1.0, 2.0) / points
    slopes = modes * (2.0 * math.pi / points)
    angles = (modes[:, None] * np.arange(points)[None, :] % points) * (2.0 * math.pi / points)
    shift = (np.arange(points)[None, :] - np.arange(points)[:, None]) % points
    keep = (weights[:, None] * np.cos(angles)).sum(0)
    slope = -(weights[:, None] * slopes[:, None] * np.sin(angles)).sum(0)
    curve = -(weights[:, None] * slopes[:, None] ** 2 * np.cos(angles)).sum(0)
    return keep[shift], slope[shift], curve[shift]


def even_odd(matrix):
    half = matrix.shape[0] // 2
    same, cross = matrix[:half, :half], matrix[:half, half:]
    return (same + cross) / 2, (same - cross) / 2


def product(left, right):
    rows = left[0].shape[0]
    dot = functools.partial(jnp.dot, preferred_element_type=jnp.float32)
    large = dot(jnp.concatenate(left, axis=0), right[0])
    return large[:rows] + (large[rows:] + dot(left[0], right[1]))


def sum_and_difference(velocity):
    components, planes, rows, points = velocity.shape
    lines = velocity.reshape(components * planes * rows, points)
    first, second = lines[:, : points // 2], lines[:, points // 2 :]
    return halves(first + second), halves(first - second)


def swapped(tiles):
    rows = lax.broadcasted_iota(jnp.int32, tiles.shape, tiles.ndim - 2) // PAIR
    groups = lax.broadcasted_iota(jnp.int32, tiles.shape, tiles.ndim - 1) // GROUP
    apart = lax.rem(rows - groups + GROUPS, GROUPS)
    result = tiles
    for distance in range(1, GROUPS):
        moved = pltpu.roll(tiles, PAIR * distance, tiles.ndim - 2)
        moved = pltpu.roll(moved, LANES - GROUP * distance, tiles.ndim - 1)
        result = jnp.where(apart == distance, moved, result)
    return result


def lanes_of(c):
    return slice(c * LANES, (c + 1) * LANES)


def pair_of(part):
    return slice(part * PAIR, (part + 1) * PAIR)


def filter_kernel(
    velocity_hbm,
    table_hbm,
    matrix_hbm,
    smooth_ref,
    message_hbm,
    matrix_ref,
    velocity_ref,
    table_ref,
    message_ref,
    in_sems,
    out_sems,
):
    components, planes, rows, points = velocity_ref.shape
    incoming = [pltpu.make_async_copy(velocity_hbm, velocity_ref, in_sems.at[0])]
    for part in range(2):
        incoming.append(
            pltpu.make_async_copy(table_hbm.at[part], table_ref.at[part], in_sems.at[1 + part])
        )
    for copy in incoming:
        copy.start()
    incoming[0].wait()
    total, gap = sum_and_difference(velocity_ref[...])
    incoming[1].wait()
    even = product(total, (table_ref[0, 0], table_ref[0, 1]))
    incoming[2].wait()
    matrix = pltpu.make_async_copy(matrix_hbm, matrix_ref, in_sems.at[3])
    matrix.start()
    odd = product(gap, (table_ref[1, 0], table_ref[1, 1]))
    outgoing = []
    blocks = points // LANES
    for section, smooth in enumerate((even + odd, even - odd)):
        smooth = smooth.reshape(components, planes, rows, points // 2)
        for local in range(blocks // 2):
            block = section * (blocks // 2) + local
            tile = smooth[:, :, :, local * LANES : (local + 1) * LANES]
            smooth_ref[block] = tile
            tile = swapped(tile.reshape(components * planes, rows, LANES))
            for part in range(GROUPS):
                for plane in range(planes):
                    index = (block * GROUPS + part) * planes + plane
                    for c in range(components):
                        message_ref[index, :, lanes_of(c)] = tile[c * planes + plane, pair_of(part)]
            count = GROUPS * planes
            here = pl.ds(block * count, count)
            copy = pltpu.make_async_copy(
                message_ref.at[here], message_hbm.at[here], out_sems.at[block]
            )
            copy.start()
            outgoing.append(copy)
    for copy in outgoing:
        copy.wait()
    matrix.wait()


def theta_kernel(velocity_ref, table_hbm, slope_ref, curve_ref, table_ref, sem):
    copy = pltpu.make_async_copy(table_hbm, table_ref, sem)
    copy.start()
    total, gap = sum_and_difference(velocity_ref[...])
    copy.wait()
    even = product(total, (table_ref[0, 0], table_ref[0, 1]))
    odd = product(gap, (table_ref[1, 0], table_ref[1, 1]))
    half = even.shape[1] // 2
    shape = velocity_ref.shape[:3] + (half,)
    for index, result_ref in enumerate((slope_ref, curve_ref)):
        columns = slice(index * half, (index + 1) * half)
        result_ref[..., :half] = (even[:, columns] + odd[:, columns]).reshape(shape)
        result_ref[..., half:] = (even[:, columns] - odd[:, columns]).reshape(shape)


def split_kernel(matrix_ref, split_ref):
    split_ref[0], split_ref[1] = halves(matrix_ref[...])


def wide_product(split_ref, rows, right):
    high, low = halves(right)
    both = jnp.concatenate([high, low], axis=1)
    large = jnp.dot(split_ref[0, rows], both, preferred_element_type=jnp.float32)
    small = jnp.dot(split_ref[1, rows], high, preferred_element_type=jnp.float32)
    return large[:, :LANES] + (large[:, LANES:] + small)


def radial_kernel(
    first, pieces, pencil_ref, split_ref, result_hbm, tiles_ref, result_ref, sems
):
    peers, rows, _ = tiles_ref.shape
    components = pencil_ref.shape[2] // LANES
    for c in range(components):
        tiles_ref[:, pair_of(c)] = pencil_ref[:, :, lanes_of(c)]
    for part in range(components, GROUPS):
        tiles_ref[:, pair_of(part)] = jnp.zeros((peers, PAIR, LANES), jnp.float32)
    turn = (peers - first) % peers
    pencil = swapped(tiles_ref[...]).reshape(peers * rows, LANES)
    pencil = jnp.concatenate([pencil[turn * rows :], pencil[: turn * rows]], axis=0)
    once = wide_product(split_ref, slice(None), pencil)
    groups = lax.broadcasted_iota(jnp.int32, pencil.shape, 1) // GROUP
    speed = jnp.where(groups == 0, pencil, jnp.zeros_like(pencil))
    speed = jnp.where(groups == 1, pltpu.roll(pencil, GROUP, 1), speed)
    speed = jnp.where(groups == 2, pltpu.roll(pencil, 2 * GROUP, 1), speed)
    count = peers // pieces
    copies = []
    for piece in range(pieces):
        here = slice(piece * count * rows, (piece + 1) * count * rows)
        twice = wide_product(split_ref, here, once)
        result = viscosity * twice - speed[here] * once[here]
        result = swapped(result.reshape(count, rows, LANES))
        place = (turn + piece * count) % peers
        until = min(count, peers - place)
        for start, target, some in ((0, place, until), (until, 0, count - until)):
            if some == 0:
                continue
            for c in range(components):
                result_ref[target : target + some, :, lanes_of(c)] = result[
                    start : start + some, pair_of(c)
                ]
            there = pl.ds(target, some)
            copy = pltpu.make_async_copy(
                result_ref.at[there], result_hbm.at[there], sems.at[len(copies)]
            )
            copy.start()
            copies.append(copy)
    for copy in copies:
        copy.wait()


def local_kernel(
    smooth_ref, near_ref, far_ref, slope_ref, curve_ref, previous_ref, ratio_ref, result_ref
):
    blocks, components, planes, rows, _ = smooth_ref.shape
    ratio = ratio_ref[...]
    square = ratio * ratio
    odd = jnp.full(ratio.shape, lax.rem(lax.axis_index("axial"), 2)) == 1
    for block in range(blocks):
        lanes = slice(block * LANES, (block + 1) * LANES)
        for c in range(components):
            line = [None] * (3 * planes)
            for plane in range(planes):
                near, far = near_ref[block, c, plane], far_ref[block, c, plane]
                line[plane] = jnp.where(odd, near, far)
                line[planes + plane] = smooth_ref[block, c, plane]
                line[2 * planes + plane] = jnp.where(odd, far, near)
            for plane in range(planes):
                here = planes + plane
                first = jnp.zeros_like(line[here])
                second = second_centre * line[here]
                for k in range(4):
                    up, down = line[here + k + 1], line[here - k - 1]
                    first = first + first_coefs[k] * (up - down)
                    second = second + second_coefs[k] * (up + down)
                second = second + square * curve_ref[c, plane, :, lanes]
                speed_theta = smooth_ref[block, 1, plane] * ratio
                result_ref[c, plane, :, lanes] = (
                    section_carry * previous_ref[c, plane, :, lanes]
                    + viscosity * second
                    - speed_theta * slope_ref[c, plane, :, lanes]
                    - smooth_ref[block, 2, plane] * first
                )


def final_kernel(
    radial_ref,
    local_ref,
    velocity_ref,
    velocity_hbm,
    rhs_hbm,
    tiles_ref,
    velocity_out_ref,
    rhs_out_ref,
    sems,
):
    components, planes, rows, points = velocity_ref.shape
    blocks = points // LANES
    copies = []
    for plane in range(planes):
        for block in range(blocks):
            for part in range(GROUPS):
                index = (block * GROUPS + part) * planes + plane
                for c in range(components):
                    tiles_ref[block, c, pair_of(part)] = radial_ref[index, :, lanes_of(c)]
            radial = swapped(tiles_ref[block])
            for c in range(components):
                lanes = lanes_of(block)
                rhs = local_ref[c, plane, :, lanes] + radial[c]
                rhs_out_ref[c, plane, :, lanes] = rhs
                velocity_out_ref[c, plane, :, lanes] = (
                    velocity_ref[c, plane, :, lanes] + (section_weight * timestep) * rhs
                )
        here = (slice(None), pl.ds(plane, 1))
        for source, target in ((rhs_out_ref, rhs_hbm), (velocity_out_ref, velocity_hbm)):
            copy = pltpu.make_async_copy(
                source.at[here], target.at[here], sems.at[len(copies)]
            )
            copy.start()
            copies.append(copy)
    for copy in copies:
        copy.wait()


VMEM = pl.BlockSpec(memory_space=pltpu.VMEM)
HBM = pl.BlockSpec(memory_space=pltpu.HBM)
PINNED = pl.BlockSpec(memory_space=pltpu.VMEM)
PINS = {id(HBM): pltpu.HBM, id(PINNED): pltpu.VMEM, id(VMEM): jax.ShapeDtypeStruct}


in_hbm = functools.partial(pltpu.with_memory_space_constraint, memory_space=pltpu.HBM)
in_vmem = functools.partial(pltpu.with_memory_space_constraint, memory_space=pltpu.VMEM)


def call(kernel, name, in_specs, outs, flops, moved, scratch=()):
    return pl.pallas_call(
        kernel,
        out_shape=[PINS[id(spec)](shape, dtype) for shape, dtype, spec in outs],
        in_specs=in_specs,
        out_specs=[spec for _, _, spec in outs],
        scratch_shapes=list(scratch),
        compiler_params=pltpu.CompilerParams(vmem_limit_bytes=24 * 1024 * 1024),
        cost_estimate=pl.CostEstimate(flops=flops, bytes_accessed=moved, transcendentals=0),
        name=name,
    )


def shards(velocity, previous_rhs, radial_deriv, inv_radius):
    components, planes, radial_rows, points = velocity.shape
    peers = lax.axis_size("radial")
    shape = velocity.shape
    size = velocity.size
    blocks = points // LANES
    f32, bf16, dma = jnp.float32, jnp.bfloat16, pltpu.SemaphoreType.DMA
    keep, slope, curve = (even_odd(matrix) for matrix in circulants(KEEP, points))
    keep = np.stack([np.stack(host_halves(part)) for part in keep])
    theta = np.stack(
        [np.stack(host_halves(np.concatenate(pair, axis=1))) for pair in zip(slope, curve)]
    )

    smooth_shape = (blocks, components, planes, radial_rows, LANES)
    message_shape = (peers, PAIR, components * LANES)
    smooth, message, matrix = call(
        filter_kernel,
        "filter",
        [HBM] * 3,
        [
            (smooth_shape, f32, PINNED),
            (message_shape, f32, HBM),
            (radial_deriv.shape, f32, PINNED),
        ],
        6 * size * points,
        20 * size,
        [
            pltpu.VMEM(shape, f32),
            pltpu.VMEM(keep.shape, bf16),
            pltpu.VMEM(message_shape, f32),
            dma((4,)),
            dma((blocks,)),
        ],
    )(in_hbm(velocity), in_hbm(jnp.asarray(keep)), in_hbm(radial_deriv))
    first = FIRST % peers
    exchange = functools.partial(
        lax.all_to_all,
        axis_name="radial",
        split_axis=0,
        concat_axis=0,
        tiled=True,
        axis_index_groups=[[(first + i) % peers for i in range(peers)]],
    )
    pencil = exchange(message)

    ring = lax.axis_size("axial")
    far = lax.ppermute(
        smooth, "axial", [(i, (i + (1 if i % 2 else ring - 1)) % ring) for i in range(ring)]
    )
    steady, far = lax.optimization_barrier((velocity, far))
    theta_slope, theta_curve = call(
        theta_kernel,
        "theta",
        [VMEM, HBM],
        [(shape, f32, VMEM)] * 2,
        HEAVY * size * points,
        24 * size,
        [pltpu.VMEM(theta.shape, bf16), dma(())],
    )(steady, in_hbm(jnp.asarray(theta)))

    full = peers * radial_rows
    pieces = 4
    (split,) = call(
        split_kernel,
        "split",
        [VMEM],
        [((2, full, full), bf16, PINNED)],
        4 * full * full,
        8 * full * full,
    )(in_vmem(matrix))
    (result,) = call(
        functools.partial(radial_kernel, first, pieces),
        "radial",
        [VMEM] * 2,
        [(message_shape, f32, HBM)],
        12 * full * full * LANES,
        4 * full * (full + 2 * LANES),
        [
            pltpu.VMEM((peers, radial_rows, LANES), f32),
            pltpu.VMEM(message_shape, f32),
            dma((pieces + 1,)),
        ],
    )(in_vmem(pencil), in_vmem(split))
    result, late = lax.optimization_barrier((result, smooth))
    near = lax.ppermute(late, "axial", [(i, i ^ 1) for i in range(ring)])
    radial = exchange(result)
    ratio = jnp.broadcast_to(inv_radius[:, None], (radial_rows, LANES))
    (local,) = call(
        local_kernel, "local", [VMEM] * 7, [(shape, f32, VMEM)], 40 * size, 32 * size
    )(smooth, near, far, theta_slope, theta_curve, previous_rhs, ratio)
    return call(
        final_kernel,
        "final",
        [VMEM] * 3,
        [(shape, f32, HBM)] * 2,
        10 * size,
        20 * size,
        [
            pltpu.VMEM((blocks, components, radial_rows, LANES), f32),
            pltpu.VMEM(shape, f32),
            pltpu.VMEM(shape, f32),
            dma((2 * planes,)),
        ],
    )(radial, local, velocity)


def solution(mesh):
    in_specs = (
        P(None, "axial", "radial", None),
        P(None, "axial", "radial", None),
        P(),
        P("radial"),
    )
    out_specs = (P(None, "axial", "radial", None), P(None, "axial", "radial", None))

    def whole(*args):
        return tuple(shards(*args))

    return jax.shard_map(whole, mesh=mesh, in_specs=in_specs, out_specs=out_specs, check_vma=False)
```

```python
import functools
import math

import jax
import jax.numpy as jnp
import ml_dtypes
import numpy as np
from jax import lax
from jax.experimental import pallas as pl
from jax.experimental.pallas import tpu as pltpu
from jax.sharding import PartitionSpec as P

KEEP = 192
LANES = 128
GROUP = 32
GROUPS = LANES // GROUP
PAIR = 2
FIRST = 52
HEAVY = 100

first_coefs = (4.0 / 5.0, -1.0 / 5.0, 4.0 / 105.0, -1.0 / 280.0)
second_coefs = (8.0 / 5.0, -1.0 / 5.0, 8.0 / 315.0, -1.0 / 560.0)
second_centre = -205.0 / 72.0
viscosity = 0.05
section_carry = -5.0 / 9.0
section_weight = 15.0 / 16.0
timestep = 0.1


def halves(array):
    high = array.astype(jnp.bfloat16)
    low = (array - high.astype(jnp.float32)).astype(jnp.bfloat16)
    return high, low


def host_halves(array):
    high = array.astype(ml_dtypes.bfloat16)
    low = (array - high.astype(np.float64)).astype(ml_dtypes.bfloat16)
    return high, low


def circulants(kept_modes, points):
    modes = np.arange(kept_modes)
    weights = np.where(modes == 0, 1.0, 2.0) / points
    slopes = modes * (2.0 * math.pi / points)
    angles = (modes[:, None] * np.arange(points)[None, :] % points) * (2.0 * math.pi / points)
    shift = (np.arange(points)[None, :] - np.arange(points)[:, None]) % points
    keep = (weights[:, None] * np.cos(angles)).sum(0)
    slope = -(weights[:, None] * slopes[:, None] * np.sin(angles)).sum(0)
    curve = -(weights[:, None] * slopes[:, None] ** 2 * np.cos(angles)).sum(0)
    return keep[shift], slope[shift], curve[shift]


def even_odd(matrix):
    half = matrix.shape[0] // 2
    same, cross = matrix[:half, :half], matrix[:half, half:]
    return (same + cross) / 2, (same - cross) / 2


def product(left, right):
    rows = left[0].shape[0]
    dot = functools.partial(jnp.dot, preferred_element_type=jnp.float32)
    large = dot(jnp.concatenate(left, axis=0), right[0])
    return large[:rows] + (large[rows:] + dot(left[0], right[1]))


def sum_and_difference(velocity):
    components, planes, rows, points = velocity.shape
    lines = velocity.reshape(components * planes * rows, points)
    first, second = lines[:, : points // 2], lines[:, points // 2 :]
    return halves(first + second), halves(first - second)


def swapped(tiles):
    rows = lax.broadcasted_iota(jnp.int32, tiles.shape, tiles.ndim - 2) // PAIR
    groups = lax.broadcasted_iota(jnp.int32, tiles.shape, tiles.ndim - 1) // GROUP
    apart = lax.rem(rows - groups + GROUPS, GROUPS)
    result = tiles
    for distance in range(1, GROUPS):
        moved = pltpu.roll(tiles, PAIR * distance, tiles.ndim - 2)
        moved = pltpu.roll(moved, LANES - GROUP * distance, tiles.ndim - 1)
        result = jnp.where(apart == distance, moved, result)
    return result


def lanes_of(c):
    return slice(c * LANES, (c + 1) * LANES)


def pair_of(part):
    return slice(part * PAIR, (part + 1) * PAIR)


def filter_kernel(
    velocity_hbm,
    table_hbm,
    matrix_hbm,
    smooth_ref,
    message_hbm,
    matrix_ref,
    velocity_ref,
    table_ref,
    message_ref,
    in_sems,
    out_sems,
):
    components, planes, rows, points = velocity_ref.shape
    incoming = [pltpu.make_async_copy(velocity_hbm, velocity_ref, in_sems.at[0])]
    for part in range(2):
        incoming.append(
            pltpu.make_async_copy(table_hbm.at[part], table_ref.at[part], in_sems.at[1 + part])
        )
    matrix = pltpu.make_async_copy(matrix_hbm, matrix_ref, in_sems.at[3])
    for copy in incoming + [matrix]:
        copy.start()
    incoming[0].wait()
    total, gap = sum_and_difference(velocity_ref[...])
    incoming[1].wait()
    even = product(total, (table_ref[0, 0], table_ref[0, 1]))
    incoming[2].wait()
    odd = product(gap, (table_ref[1, 0], table_ref[1, 1]))
    outgoing = []
    blocks = points // LANES
    for section, smooth in enumerate((even + odd, even - odd)):
        smooth = smooth.reshape(components, planes, rows, points // 2)
        for local in range(blocks // 2):
            block = section * (blocks // 2) + local
            tile = smooth[:, :, :, local * LANES : (local + 1) * LANES]
            smooth_ref[block] = tile
            tile = swapped(tile.reshape(components * planes, rows, LANES))
            for part in range(GROUPS):
                for plane in range(planes):
                    index = (block * GROUPS + part) * planes + plane
                    for c in range(components):
                        message_ref[index, :, lanes_of(c)] = tile[c * planes + plane, pair_of(part)]
            count = GROUPS * planes
            here = pl.ds(block * count, count)
            copy = pltpu.make_async_copy(
                message_ref.at[here], message_hbm.at[here], out_sems.at[block]
            )
            copy.start()
            outgoing.append(copy)
    for copy in outgoing:
        copy.wait()
    matrix.wait()


def theta_kernel(velocity_ref, table_hbm, slope_ref, curve_ref, table_ref, sems):
    copies = [
        pltpu.make_async_copy(table_hbm.at[part], table_ref.at[part], sems.at[part])
        for part in range(2)
    ]
    for copy in copies:
        copy.start()
    total, gap = sum_and_difference(velocity_ref[...])
    copies[0].wait()
    even = product(total, (table_ref[0, 0], table_ref[0, 1]))
    copies[1].wait()
    odd = product(gap, (table_ref[1, 0], table_ref[1, 1]))
    half = even.shape[1] // 2
    shape = velocity_ref.shape[:3] + (half,)
    for index, result_ref in enumerate((slope_ref, curve_ref)):
        columns = slice(index * half, (index + 1) * half)
        result_ref[..., :half] = (even[:, columns] + odd[:, columns]).reshape(shape)
        result_ref[..., half:] = (even[:, columns] - odd[:, columns]).reshape(shape)


def split_kernel(matrix_ref, split_ref):
    split_ref[0], split_ref[1] = halves(matrix_ref[...])


def wide_product(split_ref, rows, right):
    high, low = halves(right)
    both = jnp.concatenate([high, low], axis=1)
    large = jnp.dot(split_ref[0, rows], both, preferred_element_type=jnp.float32)
    small = jnp.dot(split_ref[1, rows], high, preferred_element_type=jnp.float32)
    return large[:, :LANES] + (large[:, LANES:] + small)


def radial_kernel(
    first, pieces, pencil_ref, split_ref, result_hbm, tiles_ref, result_ref, sems
):
    peers, rows, _ = tiles_ref.shape
    components = pencil_ref.shape[2] // LANES
    for c in range(components):
        tiles_ref[:, pair_of(c)] = pencil_ref[:, :, lanes_of(c)]
    for part in range(components, GROUPS):
        tiles_ref[:, pair_of(part)] = jnp.zeros((peers, PAIR, LANES), jnp.float32)
    turn = (peers - first) % peers
    pencil = swapped(tiles_ref[...]).reshape(peers * rows, LANES)
    pencil = jnp.concatenate([pencil[turn * rows :], pencil[: turn * rows]], axis=0)
    once = wide_product(split_ref, slice(None), pencil)
    groups = lax.broadcasted_iota(jnp.int32, pencil.shape, 1) // GROUP
    speed = jnp.where(groups == 0, pencil, jnp.zeros_like(pencil))
    speed = jnp.where(groups == 1, pltpu.roll(pencil, GROUP, 1), speed)
    speed = jnp.where(groups == 2, pltpu.roll(pencil, 2 * GROUP, 1), speed)
    count = peers // pieces
    copies = []
    for piece in range(pieces):
        here = slice(piece * count * rows, (piece + 1) * count * rows)
        twice = wide_product(split_ref, here, once)
        result = viscosity * twice - speed[here] * once[here]
        result = swapped(result.reshape(count, rows, LANES))
        place = (turn + piece * count) % peers
        until = min(count, peers - place)
        for start, target, some in ((0, place, until), (until, 0, count - until)):
            if some == 0:
                continue
            for c in range(components):
                result_ref[target : target + some, :, lanes_of(c)] = result[
                    start : start + some, pair_of(c)
                ]
            there = pl.ds(target, some)
            copy = pltpu.make_async_copy(
                result_ref.at[there], result_hbm.at[there], sems.at[len(copies)]
            )
            copy.start()
            copies.append(copy)
    for copy in copies:
        copy.wait()


def local_kernel(
    smooth_ref, near_ref, far_ref, slope_ref, curve_ref, previous_ref, ratio_ref, result_ref
):
    blocks, components, planes, rows, _ = smooth_ref.shape
    ratio = ratio_ref[...]
    square = ratio * ratio
    odd = jnp.full(ratio.shape, lax.rem(lax.axis_index("axial"), 2)) == 1
    for block in range(blocks):
        lanes = slice(block * LANES, (block + 1) * LANES)
        for c in range(components):
            line = [None] * (3 * planes)
            for plane in range(planes):
                near, far = near_ref[block, c, plane], far_ref[block, c, plane]
                line[plane] = jnp.where(odd, near, far)
                line[planes + plane] = smooth_ref[block, c, plane]
                line[2 * planes + plane] = jnp.where(odd, far, near)
            for plane in range(planes):
                here = planes + plane
                first = jnp.zeros_like(line[here])
                second = second_centre * line[here]
                for k in range(4):
                    up, down = line[here + k + 1], line[here - k - 1]
                    first = first + first_coefs[k] * (up - down)
                    second = second + second_coefs[k] * (up + down)
                second = second + square * curve_ref[c, plane, :, lanes]
                speed_theta = smooth_ref[block, 1, plane] * ratio
                result_ref[c, plane, :, lanes] = (
                    section_carry * previous_ref[c, plane, :, lanes]
                    + viscosity * second
                    - speed_theta * slope_ref[c, plane, :, lanes]
                    - smooth_ref[block, 2, plane] * first
                )


def final_kernel(
    radial_ref,
    local_ref,
    velocity_ref,
    velocity_hbm,
    rhs_hbm,
    tiles_ref,
    velocity_out_ref,
    rhs_out_ref,
    sems,
):
    components, planes, rows, points = velocity_ref.shape
    blocks = points // LANES
    copies = []
    for plane in range(planes):
        for block in range(blocks):
            for part in range(GROUPS):
                index = (block * GROUPS + part) * planes + plane
                for c in range(components):
                    tiles_ref[block, c, pair_of(part)] = radial_ref[index, :, lanes_of(c)]
            radial = swapped(tiles_ref[block])
            for c in range(components):
                lanes = lanes_of(block)
                rhs = local_ref[c, plane, :, lanes] + radial[c]
                rhs_out_ref[c, plane, :, lanes] = rhs
                velocity_out_ref[c, plane, :, lanes] = (
                    velocity_ref[c, plane, :, lanes] + (section_weight * timestep) * rhs
                )
        here = (slice(None), pl.ds(plane, 1))
        for source, target in ((rhs_out_ref, rhs_hbm), (velocity_out_ref, velocity_hbm)):
            copy = pltpu.make_async_copy(
                source.at[here], target.at[here], sems.at[len(copies)]
            )
            copy.start()
            copies.append(copy)
    for copy in copies:
        copy.wait()


VMEM = pl.BlockSpec(memory_space=pltpu.VMEM)
HBM = pl.BlockSpec(memory_space=pltpu.HBM)
PINNED = pl.BlockSpec(memory_space=pltpu.VMEM)
PINS = {id(HBM): pltpu.HBM, id(PINNED): pltpu.VMEM, id(VMEM): jax.ShapeDtypeStruct}


in_hbm = functools.partial(pltpu.with_memory_space_constraint, memory_space=pltpu.HBM)
in_vmem = functools.partial(pltpu.with_memory_space_constraint, memory_space=pltpu.VMEM)


def call(kernel, name, in_specs, outs, flops, moved, scratch=()):
    return pl.pallas_call(
        kernel,
        out_shape=[PINS[id(spec)](shape, dtype) for shape, dtype, spec in outs],
        in_specs=in_specs,
        out_specs=[spec for _, _, spec in outs],
        scratch_shapes=list(scratch),
        compiler_params=pltpu.CompilerParams(vmem_limit_bytes=24 * 1024 * 1024),
        cost_estimate=pl.CostEstimate(flops=flops, bytes_accessed=moved, transcendentals=0),
        name=name,
    )


def shards(velocity, previous_rhs, radial_deriv, inv_radius):
    components, planes, radial_rows, points = velocity.shape
    peers = lax.axis_size("radial")
    shape = velocity.shape
    size = velocity.size
    blocks = points // LANES
    f32, bf16, dma = jnp.float32, jnp.bfloat16, pltpu.SemaphoreType.DMA
    keep, slope, curve = (even_odd(matrix) for matrix in circulants(KEEP, points))
    keep = np.stack([np.stack(host_halves(part)) for part in keep])
    theta = np.stack(
        [np.stack(host_halves(np.concatenate(pair, axis=1))) for pair in zip(slope, curve)]
    )

    smooth_shape = (blocks, components, planes, radial_rows, LANES)
    message_shape = (peers, PAIR, components * LANES)
    smooth, message, matrix = call(
        filter_kernel,
        "filter",
        [HBM] * 3,
        [
            (smooth_shape, f32, PINNED),
            (message_shape, f32, HBM),
            (radial_deriv.shape, f32, PINNED),
        ],
        6 * size * points,
        20 * size,
        [
            pltpu.VMEM(shape, f32),
            pltpu.VMEM(keep.shape, bf16),
            pltpu.VMEM(message_shape, f32),
            dma((4,)),
            dma((blocks,)),
        ],
    )(in_hbm(velocity), in_hbm(jnp.asarray(keep)), in_hbm(radial_deriv))
    first = FIRST % peers
    exchange = functools.partial(
        lax.all_to_all,
        axis_name="radial",
        split_axis=0,
        concat_axis=0,
        tiled=True,
        axis_index_groups=[[(first + i) % peers for i in range(peers)]],
    )
    pencil = exchange(message)

    ring = lax.axis_size("axial")
    far = lax.ppermute(
        smooth, "axial", [(i, (i + (1 if i % 2 else ring - 1)) % ring) for i in range(ring)]
    )
    steady, far = lax.optimization_barrier((velocity, far))
    theta_slope, theta_curve = call(
        theta_kernel,
        "theta",
        [VMEM, HBM],
        [(shape, f32, VMEM)] * 2,
        HEAVY * size * points,
        24 * size,
        [pltpu.VMEM(theta.shape, bf16), dma((2,))],
    )(steady, in_hbm(jnp.asarray(theta)))

    ratio = jnp.broadcast_to(inv_radius[:, None], (radial_rows, LANES))
    pencil, ratio = lax.optimization_barrier((pencil, ratio))
    full = peers * radial_rows
    pieces = 4
    (split,) = call(
        split_kernel,
        "split",
        [VMEM],
        [((2, full, full), bf16, PINNED)],
        4 * full * full,
        8 * full * full,
    )(in_vmem(matrix))
    (result,) = call(
        functools.partial(radial_kernel, first, pieces),
        "radial",
        [VMEM] * 2,
        [(message_shape, f32, HBM)],
        12 * full * full * LANES,
        4 * full * (full + 2 * LANES),
        [
            pltpu.VMEM((peers, radial_rows, LANES), f32),
            pltpu.VMEM(message_shape, f32),
            dma((pieces + 1,)),
        ],
    )(in_vmem(pencil), in_vmem(split))
    result, late = lax.optimization_barrier((result, smooth))
    near = lax.ppermute(late, "axial", [(i, i ^ 1) for i in range(ring)])
    radial = exchange(result)
    (local,) = call(
        local_kernel, "local", [VMEM] * 7, [(shape, f32, VMEM)], 40 * size, 32 * size
    )(smooth, near, far, theta_slope, theta_curve, previous_rhs, ratio)
    return call(
        final_kernel,
        "final",
        [VMEM] * 3,
        [(shape, f32, HBM)] * 2,
        10 * size,
        20 * size,
        [
            pltpu.VMEM((blocks, components, radial_rows, LANES), f32),
            pltpu.VMEM(shape, f32),
            pltpu.VMEM(shape, f32),
            dma((2 * planes,)),
        ],
    )(radial, local, velocity)


def solution(mesh):
    in_specs = (
        P(None, "axial", "radial", None),
        P(None, "axial", "radial", None),
        P(),
        P("radial"),
    )
    out_specs = (P(None, "axial", "radial", None), P(None, "axial", "radial", None))

    def whole(*args):
        return tuple(shards(*args))

    return jax.shard_map(whole, mesh=mesh, in_specs=in_specs, out_specs=out_specs, check_vma=False)
```

```python
import functools
import math

import jax
import jax.numpy as jnp
import ml_dtypes
import numpy as np
from jax import lax
from jax.experimental import pallas as pl
from jax.experimental.pallas import tpu as pltpu
from jax.sharding import PartitionSpec as P

KEEP = 192
LANES = 128
GROUP = 32
GROUPS = LANES // GROUP
PAIR = 2
FIRST = 52
HEAVY = 100

first_coefs = (4.0 / 5.0, -1.0 / 5.0, 4.0 / 105.0, -1.0 / 280.0)
second_coefs = (8.0 / 5.0, -1.0 / 5.0, 8.0 / 315.0, -1.0 / 560.0)
second_centre = -205.0 / 72.0
viscosity = 0.05
section_carry = -5.0 / 9.0
section_weight = 15.0 / 16.0
timestep = 0.1


def halves(array):
    high = array.astype(jnp.bfloat16)
    low = (array - high.astype(jnp.float32)).astype(jnp.bfloat16)
    return high, low


def host_halves(array):
    high = array.astype(ml_dtypes.bfloat16)
    low = (array - high.astype(np.float64)).astype(ml_dtypes.bfloat16)
    return high, low


def circulants(kept_modes, points):
    modes = np.arange(kept_modes)
    weights = np.where(modes == 0, 1.0, 2.0) / points
    slopes = modes * (2.0 * math.pi / points)
    angles = (modes[:, None] * np.arange(points)[None, :] % points) * (2.0 * math.pi / points)
    shift = (np.arange(points)[None, :] - np.arange(points)[:, None]) % points
    keep = (weights[:, None] * np.cos(angles)).sum(0)
    slope = -(weights[:, None] * slopes[:, None] * np.sin(angles)).sum(0)
    curve = -(weights[:, None] * slopes[:, None] ** 2 * np.cos(angles)).sum(0)
    return keep[shift], slope[shift], curve[shift]


def even_odd(matrix):
    half = matrix.shape[0] // 2
    same, cross = matrix[:half, :half], matrix[:half, half:]
    return (same + cross) / 2, (same - cross) / 2


def product(left, right):
    rows = left[0].shape[0]
    dot = functools.partial(jnp.dot, preferred_element_type=jnp.float32)
    large = dot(jnp.concatenate(left, axis=0), right[0])
    return large[:rows] + (large[rows:] + dot(left[0], right[1]))


def sum_and_difference(velocity):
    components, planes, rows, points = velocity.shape
    lines = velocity.reshape(components * planes * rows, points)
    first, second = lines[:, : points // 2], lines[:, points // 2 :]
    return halves(first + second), halves(first - second)


def swapped(tiles):
    rows = lax.broadcasted_iota(jnp.int32, tiles.shape, tiles.ndim - 2) // PAIR
    groups = lax.broadcasted_iota(jnp.int32, tiles.shape, tiles.ndim - 1) // GROUP
    apart = lax.rem(rows - groups + GROUPS, GROUPS)
    result = tiles
    for distance in range(1, GROUPS):
        moved = pltpu.roll(tiles, PAIR * distance, tiles.ndim - 2)
        moved = pltpu.roll(moved, LANES - GROUP * distance, tiles.ndim - 1)
        result = jnp.where(apart == distance, moved, result)
    return result


def lanes_of(c):
    return slice(c * LANES, (c + 1) * LANES)


def pair_of(part):
    return slice(part * PAIR, (part + 1) * PAIR)


def filter_kernel(
    velocity_hbm,
    table_hbm,
    matrix_hbm,
    smooth_ref,
    message_hbm,
    matrix_ref,
    velocity_ref,
    table_ref,
    message_ref,
    in_sems,
    out_sems,
):
    components, planes, rows, points = velocity_ref.shape
    incoming = [pltpu.make_async_copy(velocity_hbm, velocity_ref, in_sems.at[0])]
    for part in range(2):
        incoming.append(
            pltpu.make_async_copy(table_hbm.at[part], table_ref.at[part], in_sems.at[1 + part])
        )
    matrix = pltpu.make_async_copy(matrix_hbm, matrix_ref, in_sems.at[3])
    for copy in incoming + [matrix]:
        copy.start()
    incoming[0].wait()
    total, gap = sum_and_difference(velocity_ref[...])
    incoming[1].wait()
    even = product(total, (table_ref[0, 0], table_ref[0, 1]))
    incoming[2].wait()
    odd = product(gap, (table_ref[1, 0], table_ref[1, 1]))
    outgoing = []
    blocks = points // LANES
    for section, smooth in enumerate((even + odd, even - odd)):
        smooth = smooth.reshape(components, planes, rows, points // 2)
        for local in range(blocks // 2):
            block = section * (blocks // 2) + local
            tile = smooth[:, :, :, local * LANES : (local + 1) * LANES]
            smooth_ref[block] = tile
            tile = swapped(tile.reshape(components * planes, rows, LANES))
            for part in range(GROUPS):
                for plane in range(planes):
                    index = (block * GROUPS + part) * planes + plane
                    for c in range(components):
                        message_ref[index, :, lanes_of(c)] = tile[c * planes + plane, pair_of(part)]
            count = GROUPS * planes
            here = pl.ds(block * count, count)
            copy = pltpu.make_async_copy(
                message_ref.at[here], message_hbm.at[here], out_sems.at[block]
            )
            copy.start()
            outgoing.append(copy)
    for copy in outgoing:
        copy.wait()
    matrix.wait()


def theta_kernel(velocity_ref, table_hbm, slope_ref, curve_ref, table_ref, sems):
    copies = [
        pltpu.make_async_copy(table_hbm.at[part], table_ref.at[part], sems.at[part])
        for part in range(2)
    ]
    for copy in copies:
        copy.start()
    total, gap = sum_and_difference(velocity_ref[...])
    copies[0].wait()
    even = product(total, (table_ref[0, 0], table_ref[0, 1]))
    copies[1].wait()
    odd = product(gap, (table_ref[1, 0], table_ref[1, 1]))
    half = even.shape[1] // 2
    shape = velocity_ref.shape[:3] + (half,)
    for index, result_ref in enumerate((slope_ref, curve_ref)):
        columns = slice(index * half, (index + 1) * half)
        result_ref[..., :half] = (even[:, columns] + odd[:, columns]).reshape(shape)
        result_ref[..., half:] = (even[:, columns] - odd[:, columns]).reshape(shape)


def split_kernel(matrix_ref, split_ref):
    split_ref[0], split_ref[1] = halves(matrix_ref[...])


def wide_product(split_ref, rows, right):
    high, low = halves(right)
    both = jnp.concatenate([high, low], axis=1)
    large = jnp.dot(split_ref[0, rows], both, preferred_element_type=jnp.float32)
    small = jnp.dot(split_ref[1, rows], high, preferred_element_type=jnp.float32)
    return large[:, :LANES] + (large[:, LANES:] + small)


def radial_kernel(
    first, pieces, pencil_ref, split_ref, result_hbm, tiles_ref, result_ref, sems
):
    peers, rows, _ = tiles_ref.shape
    components = pencil_ref.shape[2] // LANES
    for c in range(components):
        tiles_ref[:, pair_of(c)] = pencil_ref[:, :, lanes_of(c)]
    for part in range(components, GROUPS):
        tiles_ref[:, pair_of(part)] = jnp.zeros((peers, PAIR, LANES), jnp.float32)
    turn = (peers - first) % peers
    pencil = swapped(tiles_ref[...]).reshape(peers * rows, LANES)
    pencil = jnp.concatenate([pencil[turn * rows :], pencil[: turn * rows]], axis=0)
    once = wide_product(split_ref, slice(None), pencil)
    groups = lax.broadcasted_iota(jnp.int32, pencil.shape, 1) // GROUP
    speed = jnp.where(groups == 0, pencil, jnp.zeros_like(pencil))
    speed = jnp.where(groups == 1, pltpu.roll(pencil, GROUP, 1), speed)
    speed = jnp.where(groups == 2, pltpu.roll(pencil, 2 * GROUP, 1), speed)
    count = peers // pieces
    copies = []
    for piece in range(pieces):
        here = slice(piece * count * rows, (piece + 1) * count * rows)
        twice = wide_product(split_ref, here, once)
        result = viscosity * twice - speed[here] * once[here]
        result = swapped(result.reshape(count, rows, LANES))
        place = (turn + piece * count) % peers
        until = min(count, peers - place)
        for start, target, some in ((0, place, until), (until, 0, count - until)):
            if some == 0:
                continue
            for c in range(components):
                result_ref[target : target + some, :, lanes_of(c)] = result[
                    start : start + some, pair_of(c)
                ]
            there = pl.ds(target, some)
            copy = pltpu.make_async_copy(
                result_ref.at[there], result_hbm.at[there], sems.at[len(copies)]
            )
            copy.start()
            copies.append(copy)
    for copy in copies:
        copy.wait()


def local_kernel(
    smooth_ref, near_ref, far_ref, slope_ref, curve_ref, previous_ref, ratio_ref, result_ref
):
    blocks, components, planes, rows, _ = smooth_ref.shape
    ratio = ratio_ref[...]
    square = ratio * ratio
    odd = jnp.full(ratio.shape, lax.rem(lax.axis_index("axial"), 2)) == 1
    for block in range(blocks):
        lanes = slice(block * LANES, (block + 1) * LANES)
        for c in range(components):
            line = [None] * (3 * planes)
            for plane in range(planes):
                near, far = near_ref[block, c, plane], far_ref[block, c, plane]
                line[plane] = jnp.where(odd, near, far)
                line[planes + plane] = smooth_ref[block, c, plane]
                line[2 * planes + plane] = jnp.where(odd, far, near)
            for plane in range(planes):
                here = planes + plane
                first = jnp.zeros_like(line[here])
                second = second_centre * line[here]
                for k in range(4):
                    up, down = line[here + k + 1], line[here - k - 1]
                    first = first + first_coefs[k] * (up - down)
                    second = second + second_coefs[k] * (up + down)
                second = second + square * curve_ref[c, plane, :, lanes]
                speed_theta = smooth_ref[block, 1, plane] * ratio
                result_ref[c, plane, :, lanes] = (
                    section_carry * previous_ref[c, plane, :, lanes]
                    + viscosity * second
                    - speed_theta * slope_ref[c, plane, :, lanes]
                    - smooth_ref[block, 2, plane] * first
                )


def final_kernel(
    radial_ref,
    local_ref,
    velocity_ref,
    velocity_hbm,
    rhs_hbm,
    tiles_ref,
    velocity_out_ref,
    rhs_out_ref,
    sems,
):
    components, planes, rows, points = velocity_ref.shape
    blocks = points // LANES
    copies = []
    for plane in range(planes):
        for block in range(blocks):
            for part in range(GROUPS):
                index = (block * GROUPS + part) * planes + plane
                for c in range(components):
                    tiles_ref[block, c, pair_of(part)] = radial_ref[index, :, lanes_of(c)]
            radial = swapped(tiles_ref[block])
            for c in range(components):
                lanes = lanes_of(block)
                rhs = local_ref[c, plane, :, lanes] + radial[c]
                rhs_out_ref[c, plane, :, lanes] = rhs
                velocity_out_ref[c, plane, :, lanes] = (
                    velocity_ref[c, plane, :, lanes] + (section_weight * timestep) * rhs
                )
        here = (slice(None), pl.ds(plane, 1))
        for source, target in ((rhs_out_ref, rhs_hbm), (velocity_out_ref, velocity_hbm)):
            copy = pltpu.make_async_copy(
                source.at[here], target.at[here], sems.at[len(copies)]
            )
            copy.start()
            copies.append(copy)
    for copy in copies:
        copy.wait()


VMEM = pl.BlockSpec(memory_space=pltpu.VMEM)
HBM = pl.BlockSpec(memory_space=pltpu.HBM)
PINNED = pl.BlockSpec(memory_space=pltpu.VMEM)
PINS = {id(HBM): pltpu.HBM, id(PINNED): pltpu.VMEM, id(VMEM): jax.ShapeDtypeStruct}


in_hbm = functools.partial(pltpu.with_memory_space_constraint, memory_space=pltpu.HBM)
in_vmem = functools.partial(pltpu.with_memory_space_constraint, memory_space=pltpu.VMEM)


def call(kernel, name, in_specs, outs, flops, moved, scratch=()):
    return pl.pallas_call(
        kernel,
        out_shape=[PINS[id(spec)](shape, dtype) for shape, dtype, spec in outs],
        in_specs=in_specs,
        out_specs=[spec for _, _, spec in outs],
        scratch_shapes=list(scratch),
        compiler_params=pltpu.CompilerParams(vmem_limit_bytes=24 * 1024 * 1024),
        cost_estimate=pl.CostEstimate(flops=flops, bytes_accessed=moved, transcendentals=0),
        name=name,
    )


def shards(velocity, previous_rhs, radial_deriv, inv_radius):
    components, planes, radial_rows, points = velocity.shape
    peers = lax.axis_size("radial")
    shape = velocity.shape
    size = velocity.size
    blocks = points // LANES
    f32, bf16, dma = jnp.float32, jnp.bfloat16, pltpu.SemaphoreType.DMA
    keep, slope, curve = (even_odd(matrix) for matrix in circulants(KEEP, points))
    keep = np.stack([np.stack(host_halves(part)) for part in keep])
    theta = np.stack(
        [np.stack(host_halves(np.concatenate(pair, axis=1))) for pair in zip(slope, curve)]
    )

    smooth_shape = (blocks, components, planes, radial_rows, LANES)
    message_shape = (peers, PAIR, components * LANES)
    smooth, message, matrix = call(
        filter_kernel,
        "filter",
        [HBM] * 3,
        [
            (smooth_shape, f32, PINNED),
            (message_shape, f32, HBM),
            (radial_deriv.shape, f32, PINNED),
        ],
        6 * size * points,
        20 * size,
        [
            pltpu.VMEM(shape, f32),
            pltpu.VMEM(keep.shape, bf16),
            pltpu.VMEM(message_shape, f32),
            dma((4,)),
            dma((blocks,)),
        ],
    )(in_hbm(velocity), in_hbm(jnp.asarray(keep)), in_hbm(radial_deriv))
    first = FIRST % peers
    exchange = functools.partial(
        lax.all_to_all,
        axis_name="radial",
        split_axis=0,
        concat_axis=0,
        tiled=True,
        axis_index_groups=[[(first + i) % peers for i in range(peers)]],
    )
    pencil = exchange(message)

    ring = lax.axis_size("axial")
    far = lax.ppermute(
        smooth, "axial", [(i, (i + (1 if i % 2 else ring - 1)) % ring) for i in range(ring)]
    )
    steady, far = lax.optimization_barrier((velocity, far))
    theta_slope, theta_curve = call(
        theta_kernel,
        "theta",
        [VMEM, HBM],
        [(shape, f32, VMEM)] * 2,
        HEAVY * size * points,
        24 * size,
        [pltpu.VMEM(theta.shape, bf16), dma((2,))],
    )(steady, in_hbm(jnp.asarray(theta)))

    ratio = jnp.broadcast_to(inv_radius[:, None], (radial_rows, LANES))
    pencil, ratio = lax.optimization_barrier((pencil, ratio))
    full = peers * radial_rows
    pieces = 2
    (split,) = call(
        split_kernel,
        "split",
        [VMEM],
        [((2, full, full), bf16, PINNED)],
        4 * full * full,
        8 * full * full,
    )(in_vmem(matrix))
    (result,) = call(
        functools.partial(radial_kernel, first, pieces),
        "radial",
        [VMEM] * 2,
        [(message_shape, f32, HBM)],
        12 * full * full * LANES,
        4 * full * (full + 2 * LANES),
        [
            pltpu.VMEM((peers, radial_rows, LANES), f32),
            pltpu.VMEM(message_shape, f32),
            dma((pieces + 1,)),
        ],
    )(in_vmem(pencil), in_vmem(split))
    result, late = lax.optimization_barrier((result, smooth))
    near = lax.ppermute(late, "axial", [(i, i ^ 1) for i in range(ring)])
    radial = exchange(result)
    (local,) = call(
        local_kernel, "local", [VMEM] * 7, [(shape, f32, VMEM)], 40 * size, 32 * size
    )(smooth, near, far, theta_slope, theta_curve, previous_rhs, ratio)
    return call(
        final_kernel,
        "final",
        [VMEM] * 3,
        [(shape, f32, HBM)] * 2,
        10 * size,
        20 * size,
        [
            pltpu.VMEM((blocks, components, radial_rows, LANES), f32),
            pltpu.VMEM(shape, f32),
            pltpu.VMEM(shape, f32),
            dma((2 * planes,)),
        ],
    )(radial, local, velocity)


def solution(mesh):
    in_specs = (
        P(None, "axial", "radial", None),
        P(None, "axial", "radial", None),
        P(),
        P("radial"),
    )
    out_specs = (P(None, "axial", "radial", None), P(None, "axial", "radial", None))

    def whole(*args):
        return tuple(shards(*args))

    return jax.shard_map(whole, mesh=mesh, in_specs=in_specs, out_specs=out_specs, check_vma=False)
```

```python
import functools
import math

import jax
import jax.numpy as jnp
import ml_dtypes
import numpy as np
from jax import lax
from jax.experimental import pallas as pl
from jax.experimental.pallas import tpu as pltpu
from jax.sharding import PartitionSpec as P

KEEP = 192
LANES = 128
GROUP = 32
GROUPS = LANES // GROUP
PAIR = 2
FIRST = 44
HEAVY = 100

first_coefs = (4.0 / 5.0, -1.0 / 5.0, 4.0 / 105.0, -1.0 / 280.0)
second_coefs = (8.0 / 5.0, -1.0 / 5.0, 8.0 / 315.0, -1.0 / 560.0)
second_centre = -205.0 / 72.0
viscosity = 0.05
section_carry = -5.0 / 9.0
section_weight = 15.0 / 16.0
timestep = 0.1


def halves(array):
    high = array.astype(jnp.bfloat16)
    low = (array - high.astype(jnp.float32)).astype(jnp.bfloat16)
    return high, low


def host_halves(array):
    high = array.astype(ml_dtypes.bfloat16)
    low = (array - high.astype(np.float64)).astype(ml_dtypes.bfloat16)
    return high, low


def circulants(kept_modes, points):
    modes = np.arange(kept_modes)
    weights = np.where(modes == 0, 1.0, 2.0) / points
    slopes = modes * (2.0 * math.pi / points)
    angles = (modes[:, None] * np.arange(points)[None, :] % points) * (2.0 * math.pi / points)
    shift = (np.arange(points)[None, :] - np.arange(points)[:, None]) % points
    keep = (weights[:, None] * np.cos(angles)).sum(0)
    slope = -(weights[:, None] * slopes[:, None] * np.sin(angles)).sum(0)
    curve = -(weights[:, None] * slopes[:, None] ** 2 * np.cos(angles)).sum(0)
    return keep[shift], slope[shift], curve[shift]


def even_odd(matrix):
    half = matrix.shape[0] // 2
    same, cross = matrix[:half, :half], matrix[:half, half:]
    return (same + cross) / 2, (same - cross) / 2


def product(left, right):
    rows = left[0].shape[0]
    dot = functools.partial(jnp.dot, preferred_element_type=jnp.float32)
    large = dot(jnp.concatenate(left, axis=0), right[0])
    return large[:rows] + (large[rows:] + dot(left[0], right[1]))


def sum_and_difference(velocity):
    components, planes, rows, points = velocity.shape
    lines = velocity.reshape(components * planes * rows, points)
    first, second = lines[:, : points // 2], lines[:, points // 2 :]
    return halves(first + second), halves(first - second)


def swapped(tiles):
    rows = lax.broadcasted_iota(jnp.int32, tiles.shape, tiles.ndim - 2) // PAIR
    groups = lax.broadcasted_iota(jnp.int32, tiles.shape, tiles.ndim - 1) // GROUP
    apart = lax.rem(rows - groups + GROUPS, GROUPS)
    result = tiles
    for distance in range(1, GROUPS):
        moved = pltpu.roll(tiles, PAIR * distance, tiles.ndim - 2)
        moved = pltpu.roll(moved, LANES - GROUP * distance, tiles.ndim - 1)
        result = jnp.where(apart == distance, moved, result)
    return result


def lanes_of(c):
    return slice(c * LANES, (c + 1) * LANES)


def pair_of(part):
    return slice(part * PAIR, (part + 1) * PAIR)


def filter_kernel(
    velocity_hbm,
    table_hbm,
    matrix_hbm,
    smooth_ref,
    message_hbm,
    matrix_ref,
    velocity_ref,
    table_ref,
    message_ref,
    in_sems,
    out_sems,
):
    components, planes, rows, points = velocity_ref.shape
    incoming = [pltpu.make_async_copy(velocity_hbm, velocity_ref, in_sems.at[0])]
    for part in range(2):
        incoming.append(
            pltpu.make_async_copy(table_hbm.at[part], table_ref.at[part], in_sems.at[1 + part])
        )
    matrix = pltpu.make_async_copy(matrix_hbm, matrix_ref, in_sems.at[3])
    for copy in incoming + [matrix]:
        copy.start()
    incoming[0].wait()
    total, gap = sum_and_difference(velocity_ref[...])
    incoming[1].wait()
    even = product(total, (table_ref[0, 0], table_ref[0, 1]))
    incoming[2].wait()
    odd = product(gap, (table_ref[1, 0], table_ref[1, 1]))
    outgoing = []
    blocks = points // LANES
    for section, smooth in enumerate((even + odd, even - odd)):
        smooth = smooth.reshape(components, planes, rows, points // 2)
        for local in range(blocks // 2):
            block = section * (blocks // 2) + local
            tile = smooth[:, :, :, local * LANES : (local + 1) * LANES]
            smooth_ref[block] = tile
            tile = swapped(tile.reshape(components * planes, rows, LANES))
            for part in range(GROUPS):
                for plane in range(planes):
                    index = (block * GROUPS + part) * planes + plane
                    for c in range(components):
                        message_ref[index, :, lanes_of(c)] = tile[c * planes + plane, pair_of(part)]
            count = GROUPS * planes
            here = pl.ds(block * count, count)
            copy = pltpu.make_async_copy(
                message_ref.at[here], message_hbm.at[here], out_sems.at[block]
            )
            copy.start()
            outgoing.append(copy)
    for copy in outgoing:
        copy.wait()
    matrix.wait()


def theta_kernel(velocity_ref, table_hbm, slope_ref, curve_ref, table_ref, sems):
    copies = [
        pltpu.make_async_copy(table_hbm.at[part], table_ref.at[part], sems.at[part])
        for part in range(2)
    ]
    for copy in copies:
        copy.start()
    total, gap = sum_and_difference(velocity_ref[...])
    copies[0].wait()
    even = product(total, (table_ref[0, 0], table_ref[0, 1]))
    copies[1].wait()
    odd = product(gap, (table_ref[1, 0], table_ref[1, 1]))
    half = even.shape[1] // 2
    shape = velocity_ref.shape[:3] + (half,)
    for index, result_ref in enumerate((slope_ref, curve_ref)):
        columns = slice(index * half, (index + 1) * half)
        result_ref[..., :half] = (even[:, columns] + odd[:, columns]).reshape(shape)
        result_ref[..., half:] = (even[:, columns] - odd[:, columns]).reshape(shape)


def split_kernel(matrix_ref, split_ref):
    split_ref[0], split_ref[1] = halves(matrix_ref[...])


def wide_product(split_ref, rows, right):
    high, low = halves(right)
    both = jnp.concatenate([high, low], axis=1)
    large = jnp.dot(split_ref[0, rows], both, preferred_element_type=jnp.float32)
    small = jnp.dot(split_ref[1, rows], high, preferred_element_type=jnp.float32)
    return large[:, :LANES] + (large[:, LANES:] + small)


def radial_kernel(
    first, pieces, pencil_ref, split_ref, result_hbm, tiles_ref, result_ref, sems
):
    peers, rows, _ = tiles_ref.shape
    components = pencil_ref.shape[2] // LANES
    for c in range(components):
        tiles_ref[:, pair_of(c)] = pencil_ref[:, :, lanes_of(c)]
    for part in range(components, GROUPS):
        tiles_ref[:, pair_of(part)] = jnp.zeros((peers, PAIR, LANES), jnp.float32)
    turn = (peers - first) % peers
    pencil = swapped(tiles_ref[...]).reshape(peers * rows, LANES)
    pencil = jnp.concatenate([pencil[turn * rows :], pencil[: turn * rows]], axis=0)
    once = wide_product(split_ref, slice(None), pencil)
    groups = lax.broadcasted_iota(jnp.int32, pencil.shape, 1) // GROUP
    speed = jnp.where(groups == 0, pencil, jnp.zeros_like(pencil))
    speed = jnp.where(groups == 1, pltpu.roll(pencil, GROUP, 1), speed)
    speed = jnp.where(groups == 2, pltpu.roll(pencil, 2 * GROUP, 1), speed)
    count = peers // pieces
    copies = []
    for piece in range(pieces):
        here = slice(piece * count * rows, (piece + 1) * count * rows)
        twice = wide_product(split_ref, here, once)
        result = viscosity * twice - speed[here] * once[here]
        result = swapped(result.reshape(count, rows, LANES))
        place = (turn + piece * count) % peers
        until = min(count, peers - place)
        for start, target, some in ((0, place, until), (until, 0, count - until)):
            if some == 0:
                continue
            for c in range(components):
                result_ref[target : target + some, :, lanes_of(c)] = result[
                    start : start + some, pair_of(c)
                ]
            there = pl.ds(target, some)
            copy = pltpu.make_async_copy(
                result_ref.at[there], result_hbm.at[there], sems.at[len(copies)]
            )
            copy.start()
            copies.append(copy)
    for copy in copies:
        copy.wait()


def local_kernel(
    smooth_ref, near_ref, far_ref, slope_ref, curve_ref, previous_ref, ratio_ref, result_ref
):
    blocks, components, planes, rows, _ = smooth_ref.shape
    ratio = ratio_ref[...]
    square = ratio * ratio
    odd = jnp.full(ratio.shape, lax.rem(lax.axis_index("axial"), 2)) == 1
    for block in range(blocks):
        lanes = slice(block * LANES, (block + 1) * LANES)
        for c in range(components):
            line = [None] * (3 * planes)
            for plane in range(planes):
                near, far = near_ref[block, c, plane], far_ref[block, c, plane]
                line[plane] = jnp.where(odd, near, far)
                line[planes + plane] = smooth_ref[block, c, plane]
                line[2 * planes + plane] = jnp.where(odd, far, near)
            for plane in range(planes):
                here = planes + plane
                first = jnp.zeros_like(line[here])
                second = second_centre * line[here]
                for k in range(4):
                    up, down = line[here + k + 1], line[here - k - 1]
                    first = first + first_coefs[k] * (up - down)
                    second = second + second_coefs[k] * (up + down)
                second = second + square * curve_ref[c, plane, :, lanes]
                speed_theta = smooth_ref[block, 1, plane] * ratio
                result_ref[c, plane, :, lanes] = (
                    section_carry * previous_ref[c, plane, :, lanes]
                    + viscosity * second
                    - speed_theta * slope_ref[c, plane, :, lanes]
                    - smooth_ref[block, 2, plane] * first
                )


def final_kernel(
    radial_ref,
    local_ref,
    velocity_ref,
    velocity_hbm,
    rhs_hbm,
    tiles_ref,
    velocity_out_ref,
    rhs_out_ref,
    sems,
):
    components, planes, rows, points = velocity_ref.shape
    blocks = points // LANES
    copies = []
    for plane in range(planes):
        for block in range(blocks):
            for part in range(GROUPS):
                index = (block * GROUPS + part) * planes + plane
                for c in range(components):
                    tiles_ref[block, c, pair_of(part)] = radial_ref[index, :, lanes_of(c)]
            radial = swapped(tiles_ref[block])
            for c in range(components):
                lanes = lanes_of(block)
                rhs = local_ref[c, plane, :, lanes] + radial[c]
                rhs_out_ref[c, plane, :, lanes] = rhs
                velocity_out_ref[c, plane, :, lanes] = (
                    velocity_ref[c, plane, :, lanes] + (section_weight * timestep) * rhs
                )
        here = (slice(None), pl.ds(plane, 1))
        for source, target in ((rhs_out_ref, rhs_hbm), (velocity_out_ref, velocity_hbm)):
            copy = pltpu.make_async_copy(
                source.at[here], target.at[here], sems.at[len(copies)]
            )
            copy.start()
            copies.append(copy)
    for copy in copies:
        copy.wait()


VMEM = pl.BlockSpec(memory_space=pltpu.VMEM)
HBM = pl.BlockSpec(memory_space=pltpu.HBM)
PINNED = pl.BlockSpec(memory_space=pltpu.VMEM)
PINS = {id(HBM): pltpu.HBM, id(PINNED): pltpu.VMEM, id(VMEM): jax.ShapeDtypeStruct}


in_hbm = functools.partial(pltpu.with_memory_space_constraint, memory_space=pltpu.HBM)
in_vmem = functools.partial(pltpu.with_memory_space_constraint, memory_space=pltpu.VMEM)


def call(kernel, name, in_specs, outs, flops, moved, scratch=()):
    return pl.pallas_call(
        kernel,
        out_shape=[PINS[id(spec)](shape, dtype) for shape, dtype, spec in outs],
        in_specs=in_specs,
        out_specs=[spec for _, _, spec in outs],
        scratch_shapes=list(scratch),
        compiler_params=pltpu.CompilerParams(vmem_limit_bytes=24 * 1024 * 1024),
        cost_estimate=pl.CostEstimate(flops=flops, bytes_accessed=moved, transcendentals=0),
        name=name,
    )


def shards(velocity, previous_rhs, radial_deriv, inv_radius):
    components, planes, radial_rows, points = velocity.shape
    peers = lax.axis_size("radial")
    shape = velocity.shape
    size = velocity.size
    blocks = points // LANES
    f32, bf16, dma = jnp.float32, jnp.bfloat16, pltpu.SemaphoreType.DMA
    keep, slope, curve = (even_odd(matrix) for matrix in circulants(KEEP, points))
    keep = np.stack([np.stack(host_halves(part)) for part in keep])
    theta = np.stack(
        [np.stack(host_halves(np.concatenate(pair, axis=1))) for pair in zip(slope, curve)]
    )

    smooth_shape = (blocks, components, planes, radial_rows, LANES)
    message_shape = (peers, PAIR, components * LANES)
    smooth, message, matrix = call(
        filter_kernel,
        "filter",
        [HBM] * 3,
        [
            (smooth_shape, f32, PINNED),
            (message_shape, f32, HBM),
            (radial_deriv.shape, f32, PINNED),
        ],
        6 * size * points,
        20 * size,
        [
            pltpu.VMEM(shape, f32),
            pltpu.VMEM(keep.shape, bf16),
            pltpu.VMEM(message_shape, f32),
            dma((4,)),
            dma((blocks,)),
        ],
    )(in_hbm(velocity), in_hbm(jnp.asarray(keep)), in_hbm(radial_deriv))
    first = FIRST % peers
    exchange = functools.partial(
        lax.all_to_all,
        axis_name="radial",
        split_axis=0,
        concat_axis=0,
        tiled=True,
        axis_index_groups=[[(first + i) % peers for i in range(peers)]],
    )
    pencil = exchange(message)

    ring = lax.axis_size("axial")
    far = lax.ppermute(
        smooth, "axial", [(i, (i + (1 if i % 2 else ring - 1)) % ring) for i in range(ring)]
    )
    steady, far = lax.optimization_barrier((velocity, far))
    theta_slope, theta_curve = call(
        theta_kernel,
        "theta",
        [VMEM, HBM],
        [(shape, f32, VMEM)] * 2,
        HEAVY * size * points,
        24 * size,
        [pltpu.VMEM(theta.shape, bf16), dma((2,))],
    )(steady, in_hbm(jnp.asarray(theta)))

    ratio = jnp.broadcast_to(inv_radius[:, None], (radial_rows, LANES))
    pencil, ratio = lax.optimization_barrier((pencil, ratio))
    full = peers * radial_rows
    pieces = 4
    (split,) = call(
        split_kernel,
        "split",
        [VMEM],
        [((2, full, full), bf16, PINNED)],
        4 * full * full,
        8 * full * full,
    )(in_vmem(matrix))
    (result,) = call(
        functools.partial(radial_kernel, first, pieces),
        "radial",
        [VMEM] * 2,
        [(message_shape, f32, HBM)],
        12 * full * full * LANES,
        4 * full * (full + 2 * LANES),
        [
            pltpu.VMEM((peers, radial_rows, LANES), f32),
            pltpu.VMEM(message_shape, f32),
            dma((pieces + 1,)),
        ],
    )(in_vmem(pencil), in_vmem(split))
    result, late = lax.optimization_barrier((result, smooth))
    near = lax.ppermute(late, "axial", [(i, i ^ 1) for i in range(ring)])
    radial = exchange(result)
    (local,) = call(
        local_kernel, "local", [VMEM] * 7, [(shape, f32, VMEM)], 40 * size, 32 * size
    )(smooth, near, far, theta_slope, theta_curve, previous_rhs, ratio)
    return call(
        final_kernel,
        "final",
        [VMEM] * 3,
        [(shape, f32, HBM)] * 2,
        10 * size,
        20 * size,
        [
            pltpu.VMEM((blocks, components, radial_rows, LANES), f32),
            pltpu.VMEM(shape, f32),
            pltpu.VMEM(shape, f32),
            dma((2 * planes,)),
        ],
    )(radial, local, velocity)


def solution(mesh):
    in_specs = (
        P(None, "axial", "radial", None),
        P(None, "axial", "radial", None),
        P(),
        P("radial"),
    )
    out_specs = (P(None, "axial", "radial", None), P(None, "axial", "radial", None))

    def whole(*args):
        return tuple(shards(*args))

    return jax.shard_map(whole, mesh=mesh, in_specs=in_specs, out_specs=out_specs, check_vma=False)
```

```python
import functools
import math

import jax
import jax.numpy as jnp
import ml_dtypes
import numpy as np
from jax import lax
from jax.experimental import pallas as pl
from jax.experimental.pallas import tpu as pltpu
from jax.sharding import PartitionSpec as P

KEEP = 192
LANES = 128
GROUP = 32
GROUPS = LANES // GROUP
PAIR = 2
FIRST = 43
HEAVY = 100

first_coefs = (4.0 / 5.0, -1.0 / 5.0, 4.0 / 105.0, -1.0 / 280.0)
second_coefs = (8.0 / 5.0, -1.0 / 5.0, 8.0 / 315.0, -1.0 / 560.0)
second_centre = -205.0 / 72.0
viscosity = 0.05
section_carry = -5.0 / 9.0
section_weight = 15.0 / 16.0
timestep = 0.1


def halves(array):
    high = array.astype(jnp.bfloat16)
    low = (array - high.astype(jnp.float32)).astype(jnp.bfloat16)
    return high, low


def host_halves(array):
    high = array.astype(ml_dtypes.bfloat16)
    low = (array - high.astype(np.float64)).astype(ml_dtypes.bfloat16)
    return high, low


def circulants(kept_modes, points):
    modes = np.arange(kept_modes)
    weights = np.where(modes == 0, 1.0, 2.0) / points
    slopes = modes * (2.0 * math.pi / points)
    angles = (modes[:, None] * np.arange(points)[None, :] % points) * (2.0 * math.pi / points)
    shift = (np.arange(points)[None, :] - np.arange(points)[:, None]) % points
    keep = (weights[:, None] * np.cos(angles)).sum(0)
    slope = -(weights[:, None] * slopes[:, None] * np.sin(angles)).sum(0)
    curve = -(weights[:, None] * slopes[:, None] ** 2 * np.cos(angles)).sum(0)
    return keep[shift], slope[shift], curve[shift]


def even_odd(matrix):
    half = matrix.shape[0] // 2
    same, cross = matrix[:half, :half], matrix[:half, half:]
    return (same + cross) / 2, (same - cross) / 2


def product(left, right):
    rows = left[0].shape[0]
    dot = functools.partial(jnp.dot, preferred_element_type=jnp.float32)
    large = dot(jnp.concatenate(left, axis=0), right[0])
    return large[:rows] + (large[rows:] + dot(left[0], right[1]))


def sum_and_difference(velocity):
    components, planes, rows, points = velocity.shape
    lines = velocity.reshape(components * planes * rows, points)
    first, second = lines[:, : points // 2], lines[:, points // 2 :]
    return halves(first + second), halves(first - second)


def swapped(tiles):
    rows = lax.broadcasted_iota(jnp.int32, tiles.shape, tiles.ndim - 2) // PAIR
    groups = lax.broadcasted_iota(jnp.int32, tiles.shape, tiles.ndim - 1) // GROUP
    apart = lax.rem(rows - groups + GROUPS, GROUPS)
    result = tiles
    for distance in range(1, GROUPS):
        moved = pltpu.roll(tiles, PAIR * distance, tiles.ndim - 2)
        moved = pltpu.roll(moved, LANES - GROUP * distance, tiles.ndim - 1)
        result = jnp.where(apart == distance, moved, result)
    return result


def lanes_of(c):
    return slice(c * LANES, (c + 1) * LANES)


def pair_of(part):
    return slice(part * PAIR, (part + 1) * PAIR)


def filter_kernel(
    velocity_hbm,
    table_hbm,
    matrix_hbm,
    smooth_ref,
    message_hbm,
    matrix_ref,
    velocity_ref,
    table_ref,
    message_ref,
    in_sems,
    out_sems,
):
    components, planes, rows, points = velocity_ref.shape
    incoming = [pltpu.make_async_copy(velocity_hbm, velocity_ref, in_sems.at[0])]
    for part in range(2):
        incoming.append(
            pltpu.make_async_copy(table_hbm.at[part], table_ref.at[part], in_sems.at[1 + part])
        )
    matrix = pltpu.make_async_copy(matrix_hbm, matrix_ref, in_sems.at[3])
    for copy in incoming + [matrix]:
        copy.start()
    incoming[0].wait()
    total, gap = sum_and_difference(velocity_ref[...])
    incoming[1].wait()
    even = product(total, (table_ref[0, 0], table_ref[0, 1]))
    incoming[2].wait()
    odd = product(gap, (table_ref[1, 0], table_ref[1, 1]))
    outgoing = []
    blocks = points // LANES
    for section, smooth in enumerate((even + odd, even - odd)):
        smooth = smooth.reshape(components, planes, rows, points // 2)
        for local in range(blocks // 2):
            block = section * (blocks // 2) + local
            tile = smooth[:, :, :, local * LANES : (local + 1) * LANES]
            smooth_ref[block] = tile
            tile = swapped(tile.reshape(components * planes, rows, LANES))
            for part in range(GROUPS):
                for plane in range(planes):
                    index = (block * GROUPS + part) * planes + plane
                    for c in range(components):
                        message_ref[index, :, lanes_of(c)] = tile[c * planes + plane, pair_of(part)]
            count = GROUPS * planes
            here = pl.ds(block * count, count)
            copy = pltpu.make_async_copy(
                message_ref.at[here], message_hbm.at[here], out_sems.at[block]
            )
            copy.start()
            outgoing.append(copy)
    for copy in outgoing:
        copy.wait()
    matrix.wait()


def theta_kernel(velocity_ref, table_hbm, slope_ref, curve_ref, table_ref, sems):
    copies = [
        pltpu.make_async_copy(table_hbm.at[part], table_ref.at[part], sems.at[part])
        for part in range(2)
    ]
    for copy in copies:
        copy.start()
    total, gap = sum_and_difference(velocity_ref[...])
    copies[0].wait()
    even = product(total, (table_ref[0, 0], table_ref[0, 1]))
    copies[1].wait()
    odd = product(gap, (table_ref[1, 0], table_ref[1, 1]))
    half = even.shape[1] // 2
    shape = velocity_ref.shape[:3] + (half,)
    for index, result_ref in enumerate((slope_ref, curve_ref)):
        columns = slice(index * half, (index + 1) * half)
        result_ref[..., :half] = (even[:, columns] + odd[:, columns]).reshape(shape)
        result_ref[..., half:] = (even[:, columns] - odd[:, columns]).reshape(shape)


def split_kernel(matrix_ref, split_ref):
    split_ref[0], split_ref[1] = halves(matrix_ref[...])


def wide_product(split_ref, rows, right):
    high, low = halves(right)
    both = jnp.concatenate([high, low], axis=1)
    large = jnp.dot(split_ref[0, rows], both, preferred_element_type=jnp.float32)
    small = jnp.dot(split_ref[1, rows], high, preferred_element_type=jnp.float32)
    return large[:, :LANES] + (large[:, LANES:] + small)


def radial_kernel(
    first, pieces, pencil_ref, split_ref, result_hbm, tiles_ref, result_ref, sems
):
    peers, rows, _ = tiles_ref.shape
    components = pencil_ref.shape[2] // LANES
    for c in range(components):
        tiles_ref[:, pair_of(c)] = pencil_ref[:, :, lanes_of(c)]
    for part in range(components, GROUPS):
        tiles_ref[:, pair_of(part)] = jnp.zeros((peers, PAIR, LANES), jnp.float32)
    turn = (peers - first) % peers
    pencil = swapped(tiles_ref[...]).reshape(peers * rows, LANES)
    pencil = jnp.concatenate([pencil[turn * rows :], pencil[: turn * rows]], axis=0)
    once = wide_product(split_ref, slice(None), pencil)
    groups = lax.broadcasted_iota(jnp.int32, pencil.shape, 1) // GROUP
    speed = jnp.where(groups == 0, pencil, jnp.zeros_like(pencil))
    speed = jnp.where(groups == 1, pltpu.roll(pencil, GROUP, 1), speed)
    speed = jnp.where(groups == 2, pltpu.roll(pencil, 2 * GROUP, 1), speed)
    count = peers // pieces
    copies = []
    for piece in range(pieces):
        here = slice(piece * count * rows, (piece + 1) * count * rows)
        twice = wide_product(split_ref, here, once)
        result = viscosity * twice - speed[here] * once[here]
        result = swapped(result.reshape(count, rows, LANES))
        place = (turn + piece * count) % peers
        until = min(count, peers - place)
        for start, target, some in ((0, place, until), (until, 0, count - until)):
            if some == 0:
                continue
            for c in range(components):
                result_ref[target : target + some, :, lanes_of(c)] = result[
                    start : start + some, pair_of(c)
                ]
            there = pl.ds(target, some)
            copy = pltpu.make_async_copy(
                result_ref.at[there], result_hbm.at[there], sems.at[len(copies)]
            )
            copy.start()
            copies.append(copy)
    for copy in copies:
        copy.wait()


def local_kernel(
    smooth_ref, near_ref, far_ref, slope_ref, curve_ref, previous_ref, ratio_ref, result_ref
):
    blocks, components, planes, rows, _ = smooth_ref.shape
    ratio = ratio_ref[...]
    square = ratio * ratio
    odd = jnp.full(ratio.shape, lax.rem(lax.axis_index("axial"), 2)) == 1
    for block in range(blocks):
        lanes = slice(block * LANES, (block + 1) * LANES)
        for c in range(components):
            line = [None] * (3 * planes)
            for plane in range(planes):
                near, far = near_ref[block, c, plane], far_ref[block, c, plane]
                line[plane] = jnp.where(odd, near, far)
                line[planes + plane] = smooth_ref[block, c, plane]
                line[2 * planes + plane] = jnp.where(odd, far, near)
            for plane in range(planes):
                here = planes + plane
                first = jnp.zeros_like(line[here])
                second = second_centre * line[here]
                for k in range(4):
                    up, down = line[here + k + 1], line[here - k - 1]
                    first = first + first_coefs[k] * (up - down)
                    second = second + second_coefs[k] * (up + down)
                second = second + square * curve_ref[c, plane, :, lanes]
                speed_theta = smooth_ref[block, 1, plane] * ratio
                result_ref[c, plane, :, lanes] = (
                    section_carry * previous_ref[c, plane, :, lanes]
                    + viscosity * second
                    - speed_theta * slope_ref[c, plane, :, lanes]
                    - smooth_ref[block, 2, plane] * first
                )


def final_kernel(
    radial_ref,
    local_ref,
    velocity_ref,
    velocity_hbm,
    rhs_hbm,
    tiles_ref,
    velocity_out_ref,
    rhs_out_ref,
    sems,
):
    components, planes, rows, points = velocity_ref.shape
    blocks = points // LANES
    copies = []
    for plane in range(planes):
        for block in range(blocks):
            for part in range(GROUPS):
                index = (block * GROUPS + part) * planes + plane
                for c in range(components):
                    tiles_ref[block, c, pair_of(part)] = radial_ref[index, :, lanes_of(c)]
            radial = swapped(tiles_ref[block])
            for c in range(components):
                lanes = lanes_of(block)
                rhs = local_ref[c, plane, :, lanes] + radial[c]
                rhs_out_ref[c, plane, :, lanes] = rhs
                velocity_out_ref[c, plane, :, lanes] = (
                    velocity_ref[c, plane, :, lanes] + (section_weight * timestep) * rhs
                )
        here = (slice(None), pl.ds(plane, 1))
        for source, target in ((rhs_out_ref, rhs_hbm), (velocity_out_ref, velocity_hbm)):
            copy = pltpu.make_async_copy(
                source.at[here], target.at[here], sems.at[len(copies)]
            )
            copy.start()
            copies.append(copy)
    for copy in copies:
        copy.wait()


VMEM = pl.BlockSpec(memory_space=pltpu.VMEM)
HBM = pl.BlockSpec(memory_space=pltpu.HBM)
PINNED = pl.BlockSpec(memory_space=pltpu.VMEM)
PINS = {id(HBM): pltpu.HBM, id(PINNED): pltpu.VMEM, id(VMEM): jax.ShapeDtypeStruct}


in_hbm = functools.partial(pltpu.with_memory_space_constraint, memory_space=pltpu.HBM)
in_vmem = functools.partial(pltpu.with_memory_space_constraint, memory_space=pltpu.VMEM)


def call(kernel, name, in_specs, outs, flops, moved, scratch=()):
    return pl.pallas_call(
        kernel,
        out_shape=[PINS[id(spec)](shape, dtype) for shape, dtype, spec in outs],
        in_specs=in_specs,
        out_specs=[spec for _, _, spec in outs],
        scratch_shapes=list(scratch),
        compiler_params=pltpu.CompilerParams(vmem_limit_bytes=24 * 1024 * 1024),
        cost_estimate=pl.CostEstimate(flops=flops, bytes_accessed=moved, transcendentals=0),
        name=name,
    )


def shards(velocity, previous_rhs, radial_deriv, inv_radius):
    components, planes, radial_rows, points = velocity.shape
    peers = lax.axis_size("radial")
    shape = velocity.shape
    size = velocity.size
    blocks = points // LANES
    f32, bf16, dma = jnp.float32, jnp.bfloat16, pltpu.SemaphoreType.DMA
    keep, slope, curve = (even_odd(matrix) for matrix in circulants(KEEP, points))
    keep = np.stack([np.stack(host_halves(part)) for part in keep])
    theta = np.stack(
        [np.stack(host_halves(np.concatenate(pair, axis=1))) for pair in zip(slope, curve)]
    )

    smooth_shape = (blocks, components, planes, radial_rows, LANES)
    message_shape = (peers, PAIR, components * LANES)
    smooth, message, matrix = call(
        filter_kernel,
        "filter",
        [HBM] * 3,
        [
            (smooth_shape, f32, PINNED),
            (message_shape, f32, HBM),
            (radial_deriv.shape, f32, PINNED),
        ],
        6 * size * points,
        20 * size,
        [
            pltpu.VMEM(shape, f32),
            pltpu.VMEM(keep.shape, bf16),
            pltpu.VMEM(message_shape, f32),
            dma((4,)),
            dma((blocks,)),
        ],
    )(in_hbm(velocity), in_hbm(jnp.asarray(keep)), in_hbm(radial_deriv))
    first = FIRST % peers
    exchange = functools.partial(
        lax.all_to_all,
        axis_name="radial",
        split_axis=0,
        concat_axis=0,
        tiled=True,
        axis_index_groups=[[(first + i) % peers for i in range(peers)]],
    )
    pencil = exchange(message)

    ring = lax.axis_size("axial")
    far = lax.ppermute(
        smooth, "axial", [(i, (i + (1 if i % 2 else ring - 1)) % ring) for i in range(ring)]
    )
    steady, far = lax.optimization_barrier((velocity, far))
    theta_slope, theta_curve = call(
        theta_kernel,
        "theta",
        [VMEM, HBM],
        [(shape, f32, VMEM)] * 2,
        HEAVY * size * points,
        24 * size,
        [pltpu.VMEM(theta.shape, bf16), dma((2,))],
    )(steady, in_hbm(jnp.asarray(theta)))

    ratio = jnp.broadcast_to(inv_radius[:, None], (radial_rows, LANES))
    pencil, ratio = lax.optimization_barrier((pencil, ratio))
    full = peers * radial_rows
    pieces = 4
    (split,) = call(
        split_kernel,
        "split",
        [VMEM],
        [((2, full, full), bf16, PINNED)],
        4 * full * full,
        8 * full * full,
    )(in_vmem(matrix))
    (result,) = call(
        functools.partial(radial_kernel, first, pieces),
        "radial",
        [VMEM] * 2,
        [(message_shape, f32, HBM)],
        12 * full * full * LANES,
        4 * full * (full + 2 * LANES),
        [
            pltpu.VMEM((peers, radial_rows, LANES), f32),
            pltpu.VMEM(message_shape, f32),
            dma((pieces + 1,)),
        ],
    )(in_vmem(pencil), in_vmem(split))
    result, late = lax.optimization_barrier((result, smooth))
    near = lax.ppermute(late, "axial", [(i, i ^ 1) for i in range(ring)])
    radial = exchange(result)
    (local,) = call(
        local_kernel, "local", [VMEM] * 7, [(shape, f32, VMEM)], 40 * size, 32 * size
    )(smooth, near, far, theta_slope, theta_curve, previous_rhs, ratio)
    return call(
        final_kernel,
        "final",
        [VMEM] * 3,
        [(shape, f32, HBM)] * 2,
        10 * size,
        20 * size,
        [
            pltpu.VMEM((blocks, components, radial_rows, LANES), f32),
            pltpu.VMEM(shape, f32),
            pltpu.VMEM(shape, f32),
            dma((2 * planes,)),
        ],
    )(radial, local, velocity)


def solution(mesh):
    in_specs = (
        P(None, "axial", "radial", None),
        P(None, "axial", "radial", None),
        P(),
        P("radial"),
    )
    out_specs = (P(None, "axial", "radial", None), P(None, "axial", "radial", None))

    def whole(*args):
        return tuple(shards(*args))

    return jax.shard_map(whole, mesh=mesh, in_specs=in_specs, out_specs=out_specs, check_vma=False)
```
